32 devices in a mesh: rep: 2 (over x), dp: 8 (over z, core), tensor: 2 (over y).
Axes of the slice: x: 2, y: 2, z: 4, core: 2. Of those that a mesh axis runs over, the one named last changes fastest.
Arguments:
- tokens: bfloat16 [16, 1024, 1536], P(('rep', 'dp'), 'tensor'), may hold values from -6 to 6
- norm_gain: float32 [1536], replicated, may hold values from 0.25 to 1.75
- w_query: bfloat16 [1536, 1536], P(None, 'tensor'), may hold values from -0.15625 to 0.15625
- w_keyval: bfloat16 [1536, 512], replicated, may hold values from -0.15625 to 0.15625
- w_out: bfloat16 [1536, 1536], P('tensor'), may hold values from -0.15625 to 0.15625
- kv_pages: bfloat16 [128, 128, 512], P(('rep', 'dp'), 'tensor')
- page_table: int32 [16, 8], P(('rep', 'dp')), may hold values from 0 to 127, as said below
- lengths: int32 [16], P(('rep', 'dp')), may hold values from 1 to 1024, as said below
- starts: int32 [16], P(('rep', 'dp')), may hold values from 1024 to 3968, as said below
Outputs:
- attended: bfloat16 [16, 1024, 1536], P(('rep', 'dp'), 'tensor')
The draws below stay inside these ranges and needn't reach their ends.
Inputs may be any that keep to these rules, and one draw needn't show every extreme that they name: `page_table`: all 8 pages of a group lie on one replica: its own, or the other one for some groups. Page q is held by the group q // 8 (counted over rep, then dp), whose dp index is within 3 of the group's own, cyclically. `lengths`: some group is full in every draw. `starts`: multiples of 128.
All inputs are finite; a program needn't handle non-finite values.
Results may differ from the reference program's by a relative error of at most 0.034.
Values may be sent and summed in bfloat16 or wider, within the bound.
No kernel may reach another device: no remote copies, remote signals or barrier semaphores. Data moves between devices by JAX's collectives and lax.ppermute only.
A program may use at most 128 MiB of HBM per device.

```python
import math
import jax
import jax.numpy as jnp
from jax import lax

D = 1536
HEADS = 6
HD = 256
PAGE = 128
CTXP = 8
NEAR = 3
TOK = 1024
PPD = 8
WIN = 1024
GROUPS = 16
POOL = 128
N_TENSOR = 2


def draw_kv_pages(key, part):
    first = jax.random.fold_in(key, 0)
    base = jax.random.normal(first, (POOL, PAGE, 2 * HD), jnp.float32)
    return base.astype(jnp.bfloat16)


def draw_page_table(key, part):
    first, second, third = jax.random.split(key, 3)
    half = GROUPS // 2
    moved = (jax.random.randint(first, (GROUPS,), 0, 4) == 0).astype(jnp.int32)
    offset = jax.random.randint(second, (GROUPS, CTXP), -NEAR, NEAR + 1)
    slot = jax.random.randint(third, (GROUPS, CTXP), 0, PPD)
    group = jnp.arange(GROUPS, dtype=jnp.int32)
    home = group // half
    place = group % half
    side = (home + moved) % 2
    holder = side[:, None] * half + jnp.remainder(place[:, None] + offset, half)
    return (holder * PPD + slot).astype(jnp.int32)


def draw_lengths(key, part):
    first, second = jax.random.split(key)
    sizes = jax.random.randint(first, (GROUPS,), 1, TOK + 1)
    fullest = jax.random.randint(second, (), 0, GROUPS)
    return sizes.at[fullest].set(TOK).astype(jnp.int32)


def draw_starts(key, part):
    return (PAGE * jax.random.randint(key, (GROUPS,), CTXP, 4 * CTXP)).astype(jnp.int32)


def level_of(rng, shape, cuts, low, largest):
    def one(axis_at, shards_of):
        steps = jax.random.uniform(jax.random.fold_in(jax.random.fold_in(rng, 6), axis_at), (shards_of,), jnp.float32, low / len(cuts), largest / len(cuts))
        return jnp.repeat(jnp.exp(steps), shape[axis_at] // shards_of).reshape((-1,) + (1,) * (len(shape) - axis_at - 1))

    factor_of = one(*cuts[0])
    for cut in cuts[1:]:
        factor_of = factor_of * one(*cut)
    return factor_of


def centred(stream_key, dims, scale, most, cuts=(), held_as=jnp.bfloat16):
    array = jax.random.normal(stream_key, dims, jnp.float32) * scale
    if len(cuts) > 0:
        array = level_of(stream_key, dims, cuts, -0.22, 0.18) * array
    return jnp.clip(array, min=-most, max=most).astype(held_as)


def setup_inputs(seed: int = 0) -> dict:
    key_of = jax.random.split(jax.random.key(seed), 10)
    tokens = centred(key_of[0], (GROUPS, TOK, D), 1.0, 6.0, ((0, 16), (1, 2)))
    norm_gain = jnp.clip(1.0 + 0.15 * jax.random.normal(key_of[1], (D,), jnp.float32), 0.25, 1.75)
    w_query = centred(key_of[2], (D, D), D ** -0.5, 0.15625, ((1, 2),))
    w_keyval = centred(key_of[3], (D, 2 * HD), D ** -0.5, 0.15625)
    w_out = centred(key_of[4], (D, D), D ** -0.5, 0.15625, ((0, 2),))
    kv_pages = draw_kv_pages(jax.random.fold_in(key_of[9], 71), 0)
    page_table = draw_page_table(jax.random.fold_in(key_of[9], 71), 0)
    lengths = draw_lengths(jax.random.fold_in(key_of[9], 71), 0)
    starts = draw_starts(jax.random.fold_in(key_of[9], 71), 0)
    return dict(tokens=tokens, norm_gain=norm_gain, w_query=w_query, w_keyval=w_keyval, w_out=w_out, kv_pages=kv_pages, page_table=page_table, lengths=lengths, starts=starts)


def rotate_pairs(values, positions, columns_from, head_size):
    rows, cols = values.shape
    column = columns_from + jnp.arange(cols // 2, dtype=jnp.int32) * 2
    within = (column % head_size).astype(jnp.float32)
    inv_freq = jnp.exp(within * (-math.log(10000.0) / head_size))
    angle = positions[:, None] * inv_freq[None, :]
    cosine = jnp.cos(angle)
    sine = jnp.sin(angle)
    pairs = values.reshape(rows, cols // 2, 2)
    first = pairs[:, :, 0]
    second = pairs[:, :, 1]
    turned = jnp.stack([first * cosine - second * sine, first * sine + second * cosine], axis=-1)
    return turned.reshape(rows, cols)

def attend(query, keys, values, first_row):
    rows = query.shape[0]
    count = keys.shape[0]
    q_heads = query.reshape(rows, HEADS, HD).astype(jnp.float32)
    scores = jnp.einsum('rhd,kd->hrk', q_heads, keys.astype(jnp.float32)) * (1.0 / math.sqrt(HD))
    row_ids = first_row + jnp.arange(rows, dtype=jnp.int32)
    key_ids = jnp.arange(count, dtype=jnp.int32)
    seen = (key_ids[None, :] >= row_ids[:, None] + 1) & (key_ids[None, :] <= row_ids[:, None] + WIN)
    scores = jnp.where(seen[None, :, :], scores, -1e+30)
    top = lax.optimization_barrier(jnp.max(scores, axis=-1, keepdims=True))
    expd = jnp.exp(scores - top)
    total = lax.optimization_barrier(jnp.sum(expd, axis=-1, keepdims=True))
    probs = (expd / total).astype(jnp.bfloat16)
    mixed = jnp.einsum('hrk,kd->rhd', probs.astype(jnp.float32), values.astype(jnp.float32))
    return mixed.reshape(rows, HEADS * HD).astype(jnp.bfloat16)

def reference(tokens, norm_gain, w_query, w_keyval, w_out, kv_pages, page_table, lengths, starts):

    def one_group(packed):
        rows_in, table_row, length, start = packed
        xf = rows_in.astype(jnp.float32)
        scale = lax.rsqrt(lax.optimization_barrier(jnp.mean(xf * xf, axis=-1, keepdims=True)) + 1e-06)
        normed = (xf * scale * norm_gain).astype(jnp.bfloat16)
        positions = (start + jnp.arange(TOK, dtype=jnp.int32)).astype(jnp.float32)
        query = rotate_pairs(jnp.dot(normed, w_query, preferred_element_type=jnp.float32), positions, 0, HD).astype(jnp.bfloat16)
        keyval = jnp.dot(normed, w_keyval, preferred_element_type=jnp.float32)
        new_keys = rotate_pairs(keyval[:, :HD], positions, 0, HD).astype(jnp.bfloat16)
        new_values = keyval[:, HD:].astype(jnp.bfloat16)
        cached = kv_pages[table_row].reshape(WIN, 2 * HD)
        keys = jnp.concatenate([cached[:, :HD], new_keys], axis=0)
        values = jnp.concatenate([cached[:, HD:], new_values], axis=0)
        mixed = attend(query, keys, values, 0)
        blocks = mixed.reshape(TOK, N_TENSOR, D // N_TENSOR).astype(jnp.float32)
        weight_blocks = w_out.reshape(N_TENSOR, D // N_TENSOR, D).astype(jnp.float32)
        partial_value = jnp.einsum('tnc,ncd->ntd', blocks, weight_blocks)
        rounded = lax.optimization_barrier(partial_value.astype(jnp.bfloat16))
        summed = lax.optimization_barrier(jnp.sum(rounded.astype(jnp.float32), axis=0))
        live = jnp.arange(TOK, dtype=jnp.int32) < length
        return jnp.where(live[:, None], summed, 0.0).astype(jnp.bfloat16)
    return lax.map(one_group, (tokens, page_table, lengths, starts))
```

```python
import functools
import math

import jax
import jax.numpy as jnp
from jax import lax
from jax.experimental import pallas as pl
from jax.experimental.pallas import tpu as pltpu
from jax.sharding import PartitionSpec as P

BF16 = jnp.bfloat16
F32 = jnp.float32
MASKED = -1e30
ANY = pl.ANY


def spec(space):
    return pl.BlockSpec(memory_space=space)


def rotation_tables(first, rows, step, head_size):
    column = jnp.arange(head_size, dtype=jnp.int32)
    within = (column // 2 * 2).astype(F32)
    inv_freq = jnp.exp(within * (-math.log(10000.0) / head_size))
    sign = jnp.where(column % 2 == 0, -1.0, 1.0).astype(F32)
    coarse = (first + step * jnp.arange(rows // step, dtype=jnp.int32)).astype(F32)
    fine = jnp.arange(step, dtype=jnp.int32).astype(F32)
    at = jnp.concatenate([coarse, fine])
    angle = at[:, None] * inv_freq[None, :]
    return jnp.cos(angle), jnp.sin(angle) * sign[None, :]


def fill_rotation(cos_t, sin_t, cos_s, sin_s, step):
    blocks = cos_s.shape[0] // step
    cf = cos_t[blocks:, :]
    sf = sin_t[blocks:, :]
    for u in range(blocks):
        cu = cos_t[u : u + 1, :]
        su = sin_t[u : u + 1, :]
        cos_s[u * step : (u + 1) * step, :] = cu * cf - su * sf
        sin_s[u * step : (u + 1) * step, :] = su * cf + cu * sf


def rotate(v, cos, sin, even):
    width = v.shape[1]
    swapped = jnp.where(even, pltpu.roll(v, width - 1, 1), pltpu.roll(v, 1, 1))
    return v * cos + swapped * sin


def project_kernel(head_size, step, tok, gain, wq, wkv, cos_t, sin_t, normed, q, kv, cos, sin):
    rows = tok.shape[0]
    tile = min(256, rows)
    fill_rotation(cos_t, sin_t, cos, sin, step)
    even = lax.broadcasted_iota(jnp.int32, (tile, head_size), 1) % 2 == 0
    for i in range(rows // tile):
        at = pl.ds(i * tile, tile)
        xf = tok[at, :].astype(F32)
        scale = lax.rsqrt(jnp.mean(xf * xf, axis=-1, keepdims=True) + 1e-06)
        nb = (xf * scale * gain[...]).astype(BF16)
        normed[at, :] = nb
        c = cos[at, :]
        s = sin[at, :]
        both = jnp.dot(nb, wkv[...], preferred_element_type=F32)
        kv[at, :head_size] = rotate(both[:, :head_size], c, s, even).astype(BF16)
        kv[at, head_size:] = both[:, head_size:].astype(BF16)
        for h in range(wq.shape[1] // head_size):
            cols = slice(h * head_size, (h + 1) * head_size)
            part = jnp.dot(nb, wq[:, cols], preferred_element_type=F32)
            q[at, cols] = rotate(part, c, s, even).astype(BF16)


def project(tok, gain, wq, wkv, cos_t, sin_t, head_size, step):
    rows, width = tok.shape
    qc, kc = wq.shape[1], wkv.shape[1]
    return pl.pallas_call(
        functools.partial(project_kernel, head_size, step),
        out_shape=(
            jax.ShapeDtypeStruct((rows, width), BF16),
            jax.ShapeDtypeStruct((rows, qc), BF16),
            jax.ShapeDtypeStruct((rows, kc), BF16),
            jax.ShapeDtypeStruct((rows, head_size), F32),
            jax.ShapeDtypeStruct((rows, head_size), F32),
        ),
        in_specs=[spec(pltpu.VMEM)] * 6,
        out_specs=[spec(pltpu.VMEM)] * 5,
        compiler_params=pltpu.CompilerParams(vmem_limit_bytes=48 * 2**20),
        cost_estimate=pl.CostEstimate(
            flops=2 * rows * width * (qc + kc), bytes_accessed=10 * 2**20, transcendentals=0
        ),
        name="project_own",
    )(tok, gain.reshape(1, width), wq, wkv, cos_t, sin_t)


def other_kernel(head_size, order, normed, w0, w1, w2, w3, cos, sin, q):
    rows = normed.shape[0]
    tile = min(256, rows)
    deep = w0.shape[0]
    even = lax.broadcasted_iota(jnp.int32, (tile, head_size), 1) % 2 == 0
    for i in range(rows // tile):
        at = pl.ds(i * tile, tile)
        c = cos[at, :]
        s = sin[at, :]
        total = None
        for n, w in enumerate((w0, w1, w2, w3)):
            x = normed[at, pl.ds(pl.multiple_of(order[n] * deep, 128), deep)]
            part = jnp.dot(x, w[...], preferred_element_type=F32)
            total = part if total is None else total + part
        for h in range(q.shape[1] // head_size):
            cols = slice(h * head_size, (h + 1) * head_size)
            q[at, cols] = rotate(total[:, cols], c, s, even).astype(BF16)


def project_other(normed, pieces, order, cos, sin, head_size):
    rows, width = normed.shape
    qc = pieces[0].shape[1]
    return pl.pallas_call(
        functools.partial(other_kernel, head_size),
        out_shape=jax.ShapeDtypeStruct((rows, qc), BF16),
        in_specs=[spec(pltpu.SMEM)] + [spec(pltpu.VMEM)] * 7,
        out_specs=spec(pltpu.VMEM),
        compiler_params=pltpu.CompilerParams(vmem_limit_bytes=48 * 2**20),
        cost_estimate=pl.CostEstimate(
            flops=2 * rows * width * qc, bytes_accessed=6 * 2**20, transcendentals=0
        ),
        name="project_other",
    )(order, normed, *pieces, cos, sin)


def pick_kernel(idx, pool, out, sem):
    copies = [
        pltpu.make_async_copy(pool.at[idx[j]], out.at[j], sem.at[j]) for j in range(out.shape[0])
    ]
    for c in copies:
        c.start()
    for c in copies:
        c.wait()


def pick(pool, idx):
    count = idx.shape[0]
    return pl.pallas_call(
        pick_kernel,
        out_shape=jax.ShapeDtypeStruct((count,) + pool.shape[1:], pool.dtype),
        in_specs=[spec(pltpu.SMEM), spec(ANY)],
        out_specs=spec(ANY),
        scratch_shapes=[pltpu.SemaphoreType.DMA((count,))],
        cost_estimate=pl.CostEstimate(flops=0, bytes_accessed=2 * 2**20, transcendentals=0),
        name="pick_pages",
    )(idx, pool)


def choose_kernel(home, idx, pool, came, out, sem):
    count = out.shape[0]

    @pl.when(home[0] == 1)
    def _():
        for j in range(count):
            pltpu.make_async_copy(pool.at[idx[j]], out.at[j], sem.at[j]).start()

    @pl.when(home[0] == 0)
    def _():
        for j in range(count):
            pltpu.make_async_copy(came.at[j], out.at[j], sem.at[j]).start()

    for j in range(count):
        pltpu.make_async_copy(came.at[j], out.at[j], sem.at[j]).wait()


def choose(pool, idx, home, came):
    count = idx.shape[0]
    return pl.pallas_call(
        choose_kernel,
        out_shape=jax.ShapeDtypeStruct(came.shape, came.dtype),
        in_specs=[spec(pltpu.SMEM), spec(pltpu.SMEM), spec(ANY), spec(ANY)],
        out_specs=spec(ANY),
        scratch_shapes=[pltpu.SemaphoreType.DMA((count,))],
        cost_estimate=pl.CostEstimate(flops=0, bytes_accessed=2 * 2**20, transcendentals=0),
        name="choose_pages",
    )(home, idx, pool, came)


def attend_kernel(
    head_size,
    info,
    qa,
    qb,
    mine,
    peer,
    kv_own,
    kv_peer,
    woa,
    w0,
    w1,
    w2,
    w3,
    out,
    keys,
    vals,
    wa,
    wb,
    mix,
    ksem,
    vsem,
    wsem,
):
    part = info[0]
    length = info[1]
    rows, half = qa.shape
    pages, prow, _ = mine.shape
    page = 2 * prow
    width = out.shape[1]
    nheads = half // head_size
    window = pages * page
    wcols = w0.shape[1]

    def move(which, dst, sem, lo):
        cols = pl.ds(lo, head_size)
        got = []
        here = part == 0
        for u in range(pages):
            at0 = u * page
            at1 = (u - rows // page) * page
            for src, side in ((mine, part), (peer, 1 - part)):
                row = pl.multiple_of(side * prow, prow)
                got.append((True, src.at[u, :, cols], at0, row, prow))
                if at1 >= 0:
                    got.append((False, src.at[u, :, cols], at1, row, prow))
        got.append((True, kv_own.at[:, cols], window, 0, rows))
        got.append((False, kv_own.at[:, cols], window, 0, rows))
        got.append((False, kv_peer.at[:, cols], window - rows, 0, rows))
        return got

    def start(dst, sem, lo):
        moves = move(None, dst, sem, lo)
        for case in (True, False):

            @pl.when((part == 0) == case)
            def _():
                for which, src, at, row, count in moves:
                    if which == case:
                        pltpu.make_async_copy(src, dst.at[pl.ds(at + row, count), :], sem).start()

    def finish(dst, sem, lo):
        pltpu.make_async_copy(dst, dst, sem).wait()

    start(keys, ksem, 0)
    start(vals, vsem, head_size)
    weights = [pltpu.make_async_copy(woa, wa, wsem.at[0])]
    for n, w in enumerate((w0, w1, w2, w3)):
        cols = pl.ds(pl.multiple_of(info[2 + n] * wcols, 128), wcols)
        weights.append(pltpu.make_async_copy(w, wb.at[:, cols], wsem.at[1 + n]))
    for c in weights:
        c.start()

    tile = min(256, rows)
    span = window + tile
    row_id = lax.broadcasted_iota(jnp.int32, (tile, tile), 0)
    col_id = lax.broadcasted_iota(jnp.int32, (tile, tile), 1)
    first_seen = col_id >= row_id + 1
    last_seen = col_id <= row_id
    factor = math.log2(math.e) / math.sqrt(head_size)
    finish(keys, ksem, 0)
    for i in range(rows // tile):
        at = pl.ds(i * tile, tile)
        for n, q in enumerate((qa, qb)):
            for h in range(nheads):
                cols = slice(h * head_size, (h + 1) * head_size)
                kk = keys[pl.ds(i * tile, span), :]
                s = lax.dot_general(
                    q[at, cols], kk, (((1,), (1,)), ((), ())), preferred_element_type=F32
                )
                s = jnp.concatenate(
                    [
                        jnp.where(first_seen, s[:, :tile], MASKED),
                        s[:, tile : span - tile],
                        jnp.where(last_seen, s[:, span - tile :], MASKED),
                    ],
                    axis=1,
                )
                top = jnp.max(s, axis=-1, keepdims=True)
                e = jnp.exp2((s - top) * factor)
                total = jnp.sum(e, axis=-1, keepdims=True)
                if i == 0 and n == 0 and h == 0:
                    finish(vals, vsem, head_size)
                vv = vals[pl.ds(i * tile, span), :]
                m = jnp.dot(e.astype(BF16), vv, preferred_element_type=F32)
                mix[n, at, cols] = (m / total).astype(BF16)
    for c in weights:
        c.wait()
    for i in range(rows // tile):
        at = pl.ds(i * tile, tile)
        row = part * rows + i * tile + lax.broadcasted_iota(jnp.int32, (tile, 1), 0)
        live = row < length
        for j in range(width // wcols):
            cols = slice(j * wcols, (j + 1) * wcols)
            a = jnp.dot(mix[0, at, :], wa[:, cols], preferred_element_type=F32)
            b = jnp.dot(mix[1, at, :], wb[:, cols], preferred_element_type=F32)
            both = a.astype(BF16).astype(F32) + b.astype(BF16).astype(F32)
            out[at, cols] = jnp.where(live, both, 0.0).astype(BF16)


def attend_pages(info, qa, qb, mine, peer, kv_own, kv_peer, woa, pieces, head_size):
    rows, half = qa.shape
    width = woa.shape[1]
    window = mine.shape[0] * mine.shape[1] * 2
    return pl.pallas_call(
        functools.partial(attend_kernel, head_size),
        out_shape=jax.ShapeDtypeStruct((rows, width), BF16),
        in_specs=[spec(pltpu.SMEM)] + [spec(pltpu.VMEM)] * 2 + [spec(ANY)] * 9,
        out_specs=spec(pltpu.VMEM),
        scratch_shapes=[
            pltpu.VMEM((window + rows, head_size), BF16),
            pltpu.VMEM((window + rows, head_size), BF16),
            pltpu.VMEM(woa.shape, BF16),
            pltpu.VMEM(woa.shape, BF16),
            pltpu.VMEM((2, rows, half), BF16),
            pltpu.SemaphoreType.DMA,
            pltpu.SemaphoreType.DMA,
            pltpu.SemaphoreType.DMA((5,)),
        ],
        compiler_params=pltpu.CompilerParams(vmem_limit_bytes=56 * 2**20),
        cost_estimate=pl.CostEstimate(
            flops=4 * rows * 2 * half * (window + 256) + 4 * rows * half * width,
            bytes_accessed=12 * 2**20,
            transcendentals=rows * 6 * (window + 256),
        ),
        name="attend_and_out",
    )(info, qa, qb, mine, peer, kv_own, kv_peer, woa, *pieces)


def pair_shards(tokens, norm_gain, w_query, w_keyval, w_out, kv_pages, page_table, lengths, starts):
    head_size = w_keyval.shape[1] // 2
    part = lax.axis_index("tensor")
    rep = lax.axis_index("rep")
    dp = lax.axis_index("dp")
    ndp = lax.axis_size("dp")
    core = dp % 2
    rows = tokens.shape[1]
    swap = [(0, 1), (1, 0)]
    cores = [(i, i ^ 1) for i in range(ndp)]

    quarter = rep * 2 + core
    order = jnp.stack(
        [quarter, (1 - rep) * 2 + core, rep * 2 + 1 - core, (1 - rep) * 2 + 1 - core]
    ).astype(jnp.int32)

    def spread(piece):
        a = lax.ppermute(piece, "tensor", swap)
        b = lax.ppermute(a, "rep", swap)
        return a, b, lax.ppermute(a, "dp", cores), lax.ppermute(b, "dp", cores)

    deep = w_query.shape[0] // 4
    wide = w_out.shape[1] // 4
    wq_pieces = spread(lax.dynamic_slice_in_dim(w_query, quarter * deep, deep, 0))
    wo_pieces = spread(lax.dynamic_slice_in_dim(w_out, quarter * wide, wide, 1))

    table = page_table[0]
    peer_table = lax.ppermute(table, "rep", swap)
    per_rep = kv_pages.shape[0] * ndp
    pool = lax.all_gather(kv_pages, "dp", axis=0, tiled=True)
    came = lax.ppermute(pick(pool, peer_table % per_rep), "rep", swap)
    home = (table[:1] // per_rep == rep).astype(jnp.int32)
    mine = choose(pool, table % per_rep, home, came)
    peer = lax.ppermute(mine, "tensor", swap)

    step = 32
    cos_t, sin_t = rotation_tables(starts[0] + part * rows, rows, step, head_size)
    normed, qa, kv_own, cos, sin = project(
        tokens[0], norm_gain, w_query, w_keyval, cos_t, sin_t, head_size, step
    )
    kv_peer = lax.ppermute(kv_own, "tensor", swap)
    qb = project_other(normed, wq_pieces, order, cos, sin, head_size)
    info = jnp.concatenate([jnp.stack([part, lengths[0]]).astype(jnp.int32), order])
    return attend_pages(info, qa, qb, mine, peer, kv_own, kv_peer, w_out, wo_pieces, head_size)[None]


def rotate_pairs(values, positions, columns_from, head_size):
    rows, cols = values.shape
    column = columns_from + jnp.arange(cols // 2, dtype=jnp.int32) * 2
    within = (column % head_size).astype(jnp.float32)
    inv_freq = jnp.exp(within * (-math.log(10000.0) / head_size))
    angle = positions[:, None] * inv_freq[None, :]
    cosine = jnp.cos(angle)
    sine = jnp.sin(angle)
    pairs = values.reshape(rows, cols // 2, 2)
    first = pairs[:, :, 0]
    second = pairs[:, :, 1]
    turned = jnp.stack([first * cosine - second * sine, first * sine + second * cosine], axis=-1)
    return turned.reshape(rows, cols)


def attend(query, keys, values, first_row, heads, head_size, window):
    rows = query.shape[0]
    count = keys.shape[0]
    q_heads = query.reshape(rows, heads, head_size)
    scores = jnp.einsum("rhd,kd->hrk", q_heads, keys, preferred_element_type=jnp.float32) * (
        1.0 / math.sqrt(head_size)
    )
    row_ids = first_row + jnp.arange(rows, dtype=jnp.int32)
    key_ids = jnp.arange(count, dtype=jnp.int32)
    seen = (key_ids[None, :] >= row_ids[:, None] + 1) & (
        key_ids[None, :] <= row_ids[:, None] + window
    )
    scores = jnp.where(seen[None, :, :], scores, -1e30)
    top = jnp.max(scores, axis=-1, keepdims=True)
    expd = jnp.exp(scores - top)
    total = jnp.sum(expd, axis=-1, keepdims=True)
    probs = (expd / total).astype(jnp.bfloat16)
    mixed = jnp.einsum("hrk,kd->rhd", probs, values, preferred_element_type=jnp.float32)
    return mixed.reshape(rows, heads * head_size).astype(jnp.bfloat16)


def shards(tokens, norm_gain, w_query, w_keyval, w_out, kv_pages, page_table, lengths, starts):
    width = tokens.shape[2]
    head_size = w_keyval.shape[1] // 2
    heads = width // head_size
    part = lax.axis_index("tensor")
    local_rows = tokens.shape[1]
    q_cols = w_query.shape[1]
    start = starts[0]
    length = lengths[0]
    xf = tokens[0].astype(jnp.float32)
    scale = lax.rsqrt(jnp.mean(xf * xf, axis=-1, keepdims=True) + 1e-06)
    normed = (xf * scale * norm_gain).astype(jnp.bfloat16)
    piece = lax.all_gather(normed, "tensor", axis=0, tiled=True)
    positions = (start + jnp.arange(piece.shape[0], dtype=jnp.int32)).astype(jnp.float32)
    query = rotate_pairs(
        jnp.dot(piece, w_query, preferred_element_type=jnp.float32),
        positions,
        part * q_cols,
        head_size,
    )
    keyval = jnp.dot(piece, w_keyval, preferred_element_type=jnp.float32)
    new_keys = rotate_pairs(keyval[:, :head_size], positions, 0, head_size)
    projected = jnp.concatenate([query, new_keys, keyval[:, head_size:]], axis=1).astype(
        jnp.bfloat16
    )
    query_cols = projected[:, :q_cols]
    keys_new = projected[:, q_cols : q_cols + head_size]
    values_new = projected[:, q_cols + head_size :]
    query = lax.all_to_all(query_cols, "tensor", split_axis=0, concat_axis=1, tiled=True)
    table = page_table[0]
    piece = lax.all_gather(kv_pages, ("rep", "dp"), axis=0, tiled=True)
    ident = jnp.arange(piece.shape[0], dtype=jnp.int32)
    onehot = (table[:, None] == ident[None, :]).astype(jnp.bfloat16)
    picked = jnp.einsum("cn,nrk->crk", onehot, piece, preferred_element_type=jnp.float32)
    window_pages = lax.all_gather(picked.astype(jnp.bfloat16), "tensor", axis=1, tiled=True)
    cached = window_pages.reshape(-1, 2 * head_size)
    window = cached.shape[0]
    keys = jnp.concatenate([cached[:, :head_size], keys_new], axis=0)
    values = jnp.concatenate([cached[:, head_size:], values_new], axis=0)
    mixed = attend(query, keys, values, part * local_rows, heads, head_size, window)
    mixed_cols = lax.all_to_all(mixed, "tensor", split_axis=1, concat_axis=0, tiled=True)
    summed = lax.psum_scatter(
        jnp.dot(mixed_cols, w_out, preferred_element_type=jnp.float32).astype(jnp.bfloat16),
        "tensor",
        scatter_dimension=0,
        tiled=True,
    ).astype(jnp.float32)
    live = part * local_rows + jnp.arange(local_rows, dtype=jnp.int32) < length
    return jnp.where(live[:, None], summed, 0.0).astype(jnp.bfloat16)[None]


def solution(mesh):
    placed = (
        P(("rep", "dp"), "tensor", None),
        P(),
        P(None, "tensor"),
        P(),
        P("tensor", None),
        P(("rep", "dp"), "tensor", None),
        P(("rep", "dp"), None),
        P(("rep", "dp")),
        P(("rep", "dp")),
    )
    body = pair_shards if mesh.shape["tensor"] == 2 and mesh.shape["rep"] == 2 else shards
    return jax.shard_map(
        body,
        mesh=mesh,
        in_specs=placed,
        out_specs=P(("rep", "dp"), "tensor", None),
        check_vma=False,
    )
```

```python
import functools
import math

import jax
import jax.numpy as jnp
from jax import lax
from jax.experimental import pallas as pl
from jax.experimental.pallas import tpu as pltpu
from jax.sharding import PartitionSpec as P

BF16 = jnp.bfloat16
F32 = jnp.float32
MASKED = -1e30
ANY = pl.ANY


def spec(space):
    return pl.BlockSpec(memory_space=space)


def rotation_tables(first, rows, step, head_size):
    column = jnp.arange(head_size, dtype=jnp.int32)
    within = (column // 2 * 2).astype(F32)
    inv_freq = jnp.exp(within * (-math.log(10000.0) / head_size))
    sign = jnp.where(column % 2 == 0, -1.0, 1.0).astype(F32)
    coarse = (first + step * jnp.arange(rows // step, dtype=jnp.int32)).astype(F32)
    fine = jnp.arange(step, dtype=jnp.int32).astype(F32)
    at = jnp.concatenate([coarse, fine])
    angle = at[:, None] * inv_freq[None, :]
    return jnp.cos(angle), jnp.sin(angle) * sign[None, :]


def fill_rotation(cos_t, sin_t, cos_s, sin_s, step):
    blocks = cos_s.shape[0] // step
    cf = cos_t[blocks:, :]
    sf = sin_t[blocks:, :]
    for u in range(blocks):
        cu = cos_t[u : u + 1, :]
        su = sin_t[u : u + 1, :]
        cos_s[u * step : (u + 1) * step, :] = cu * cf - su * sf
        sin_s[u * step : (u + 1) * step, :] = su * cf + cu * sf


def rotate(v, cos, sin, even):
    width = v.shape[1]
    swapped = jnp.where(even, pltpu.roll(v, width - 1, 1), pltpu.roll(v, 1, 1))
    return v * cos + swapped * sin


def project_kernel(head_size, step, tok, gain, wq, wkv, cos_t, sin_t, normed, q, kv, cos, sin):
    rows = tok.shape[0]
    tile = min(256, rows)
    fill_rotation(cos_t, sin_t, cos, sin, step)
    even = lax.broadcasted_iota(jnp.int32, (tile, head_size), 1) % 2 == 0
    for i in range(rows // tile):
        at = pl.ds(i * tile, tile)
        xf = tok[at, :].astype(F32)
        scale = lax.rsqrt(jnp.mean(xf * xf, axis=-1, keepdims=True) + 1e-06)
        nb = (xf * scale * gain[...]).astype(BF16)
        normed[at, :] = nb
        c = cos[at, :]
        s = sin[at, :]
        both = jnp.dot(nb, wkv[...], preferred_element_type=F32)
        kv[at, :head_size] = rotate(both[:, :head_size], c, s, even).astype(BF16)
        kv[at, head_size:] = both[:, head_size:].astype(BF16)
        for h in range(wq.shape[1] // head_size):
            cols = slice(h * head_size, (h + 1) * head_size)
            part = jnp.dot(nb, wq[:, cols], preferred_element_type=F32)
            q[at, cols] = rotate(part, c, s, even).astype(BF16)


def project(tok, gain, wq, wkv, cos_t, sin_t, head_size, step):
    rows, width = tok.shape
    qc, kc = wq.shape[1], wkv.shape[1]
    return pl.pallas_call(
        functools.partial(project_kernel, head_size, step),
        out_shape=(
            jax.ShapeDtypeStruct((rows, width), BF16),
            jax.ShapeDtypeStruct((rows, qc), BF16),
            jax.ShapeDtypeStruct((rows, kc), BF16),
            jax.ShapeDtypeStruct((rows, head_size), F32),
            jax.ShapeDtypeStruct((rows, head_size), F32),
        ),
        in_specs=[spec(pltpu.VMEM)] * 6,
        out_specs=[spec(pltpu.VMEM)] * 5,
        compiler_params=pltpu.CompilerParams(vmem_limit_bytes=20 * 2**20),
        cost_estimate=pl.CostEstimate(
            flops=2 * rows * width * (qc + kc), bytes_accessed=10 * 2**20, transcendentals=0
        ),
        name="project_own",
    )(tok, gain.reshape(1, width), wq, wkv, cos_t, sin_t)


def other_kernel(head_size, normed, wq, cos, sin, q):
    rows = normed.shape[0]
    tile = min(256, rows)
    even = lax.broadcasted_iota(jnp.int32, (tile, head_size), 1) % 2 == 0
    for i in range(rows // tile):
        at = pl.ds(i * tile, tile)
        c = cos[at, :]
        s = sin[at, :]
        for h in range(q.shape[1] // head_size):
            cols = slice(h * head_size, (h + 1) * head_size)
            part = jnp.dot(normed[at, :], wq[:, cols], preferred_element_type=F32)
            q[at, cols] = rotate(part, c, s, even).astype(BF16)


def project_other(normed, wq, cos, sin, head_size):
    rows, width = normed.shape
    qc = wq.shape[1]
    return pl.pallas_call(
        functools.partial(other_kernel, head_size),
        out_shape=jax.ShapeDtypeStruct((rows, qc), BF16),
        in_specs=[spec(pltpu.VMEM)] * 4,
        out_specs=spec(pltpu.VMEM),
        compiler_params=pltpu.CompilerParams(vmem_limit_bytes=20 * 2**20),
        cost_estimate=pl.CostEstimate(
            flops=2 * rows * width * qc, bytes_accessed=6 * 2**20, transcendentals=0
        ),
        name="project_other",
    )(normed, wq, cos, sin)


def collect_kernel(where, *refs):
    arrays, out = refs[:-1], refs[-1]

    def one(j, _):
        for n, array in enumerate(arrays):

            @pl.when(where[0, j] == n)
            def _():
                out[j] = array[where[1, j]]

        return 0

    lax.fori_loop(0, out.shape[0], one, 0)


def collect(where, arrays, name):
    count = where.shape[1]
    shape = (count,) + arrays[0].shape[1:]
    return pl.pallas_call(
        collect_kernel,
        out_shape=jax.ShapeDtypeStruct(shape, arrays[0].dtype),
        in_specs=[spec(pltpu.SMEM)] + [spec(pltpu.VMEM)] * len(arrays),
        out_specs=spec(pltpu.VMEM),
        compiler_params=pltpu.CompilerParams(vmem_limit_bytes=12 * 2**20),
        cost_estimate=pl.CostEstimate(flops=0, bytes_accessed=2 * 2**20, transcendentals=0),
        name=name,
    )(where, *arrays)


def attend_kernel(
    head_size,
    info,
    qa,
    qb,
    k_mine,
    k_peer,
    v_mine,
    v_peer,
    kv_own,
    kv_peer,
    woa,
    wob,
    out,
    keys,
    vals,
    wa,
    wb,
    mix,
    ksem,
    vsem,
    wsem,
):
    part = info[0]
    length = info[1]
    rows, half = qa.shape
    pages, prow, _ = k_mine.shape
    page = 2 * prow
    width = out.shape[1]
    nheads = half // head_size
    window = pages * page

    def start(mine, peer, lo, dst, sem):
        cols = pl.ds(lo, head_size)
        for case in (0, 1):

            @pl.when(part == case)
            def _():
                skip = case * rows // page
                for u in range(skip, pages):
                    for src, side in ((mine, case), (peer, 1 - case)):
                        to = pl.ds((u - skip) * page + side * prow, prow)
                        pltpu.make_async_copy(src.at[u], dst.at[to, :], sem).start()
                if case == 1:
                    to = pl.ds(window - rows, rows)
                    pltpu.make_async_copy(kv_peer.at[:, cols], dst.at[to, :], sem).start()
                to = pl.ds(window, rows)
                pltpu.make_async_copy(kv_own.at[:, cols], dst.at[to, :], sem).start()

    def finish(dst, sem):
        pltpu.make_async_copy(dst, dst, sem).wait()

    start(k_mine, k_peer, 0, keys, ksem)
    start(v_mine, v_peer, head_size, vals, vsem)
    weights = [
        pltpu.make_async_copy(woa, wa, wsem.at[0]),
        pltpu.make_async_copy(wob, wb, wsem.at[1]),
    ]
    for c in weights:
        c.start()

    tile = min(256, rows)
    span = window + tile
    row_id = lax.broadcasted_iota(jnp.int32, (tile, tile), 0)
    col_id = lax.broadcasted_iota(jnp.int32, (tile, tile), 1)
    first_seen = col_id >= row_id + 1
    last_seen = col_id <= row_id
    factor = math.log2(math.e) / math.sqrt(head_size)
    finish(keys, ksem)
    for i in range(rows // tile):
        at = pl.ds(i * tile, tile)
        for n, q in enumerate((qa, qb)):
            for h in range(nheads):
                cols = slice(h * head_size, (h + 1) * head_size)
                kk = keys[pl.ds(i * tile, span), :]
                s = lax.dot_general(
                    q[at, cols], kk, (((1,), (1,)), ((), ())), preferred_element_type=F32
                )
                s = jnp.concatenate(
                    [
                        jnp.where(first_seen, s[:, :tile], MASKED),
                        s[:, tile : span - tile],
                        jnp.where(last_seen, s[:, span - tile :], MASKED),
                    ],
                    axis=1,
                )
                top = jnp.max(s, axis=-1, keepdims=True)
                e = jnp.exp2((s - top) * factor)
                total = jnp.sum(e, axis=-1, keepdims=True)
                if i == 0 and n == 0 and h == 0:
                    finish(vals, vsem)
                vv = vals[pl.ds(i * tile, span), :]
                m = jnp.dot(e.astype(BF16), vv, preferred_element_type=F32)
                mix[n, at, cols] = (m / total).astype(BF16)
    for c in weights:
        c.wait()
    for i in range(rows // tile):
        at = pl.ds(i * tile, tile)
        row = part * rows + i * tile + lax.broadcasted_iota(jnp.int32, (tile, 1), 0)
        live = row < length
        for j in range(width // 512):
            cols = slice(j * 512, (j + 1) * 512)
            a = jnp.dot(mix[0, at, :], wa[:, cols], preferred_element_type=F32)
            b = jnp.dot(mix[1, at, :], wb[:, cols], preferred_element_type=F32)
            both = a.astype(BF16).astype(F32) + b.astype(BF16).astype(F32)
            out[at, cols] = jnp.where(live, both, 0.0).astype(BF16)


def attend_pages(info, qa, qb, k_mine, k_peer, v_mine, v_peer, kv_own, kv_peer, woa, wob):
    rows, half = qa.shape
    width = woa.shape[1]
    head_size = k_mine.shape[2]
    window = k_mine.shape[0] * k_mine.shape[1] * 2
    return pl.pallas_call(
        functools.partial(attend_kernel, head_size),
        out_shape=jax.ShapeDtypeStruct((rows, width), BF16),
        in_specs=[spec(pltpu.SMEM)] + [spec(pltpu.VMEM)] * 2 + [spec(ANY)] * 8,
        out_specs=spec(pltpu.VMEM),
        scratch_shapes=[
            pltpu.VMEM((window + rows, head_size), BF16),
            pltpu.VMEM((window + rows, head_size), BF16),
            pltpu.VMEM(woa.shape, BF16),
            pltpu.VMEM(wob.shape, BF16),
            pltpu.VMEM((2, rows, half), BF16),
            pltpu.SemaphoreType.DMA,
            pltpu.SemaphoreType.DMA,
            pltpu.SemaphoreType.DMA((2,)),
        ],
        compiler_params=pltpu.CompilerParams(vmem_limit_bytes=28 * 2**20),
        cost_estimate=pl.CostEstimate(
            flops=4 * rows * 2 * half * (window + 256) + 4 * rows * half * width,
            bytes_accessed=12 * 2**20,
            transcendentals=rows * 6 * (window + 256),
        ),
        name="attend_and_out",
    )(info, qa, qb, k_mine, k_peer, v_mine, v_peer, kv_own, kv_peer, woa, wob)


def line_gather(x, swap_at, after):
    pairs = swap_at([(0, 1), (1, 0), (2, 3), (3, 2)])
    middle = swap_at([(1, 2), (2, 1)])
    outward = swap_at([(1, 0), (2, 3)])
    first = lax.ppermute(x, "dp", pairs)
    near = lax.ppermute(x, "dp", middle)
    first, near, _ = lax.optimization_barrier((first, near, after))
    far = lax.ppermute(first, "dp", middle)
    return [x, first, near, lax.ppermute(near, "dp", outward), far, lax.ppermute(far, "dp", outward)]


def pair_shards(tokens, norm_gain, w_query, w_keyval, w_out, kv_pages, page_table, lengths, starts):
    head_size = w_keyval.shape[1] // 2
    part = lax.axis_index("tensor")
    rep = lax.axis_index("rep")
    dp = lax.axis_index("dp")
    ndp = lax.axis_size("dp")
    chip, core = dp // 2, dp % 2
    rows = tokens.shape[1]
    held = kv_pages.shape[0]
    count = page_table.shape[1]
    swap = [(0, 1), (1, 0)]
    cores = [(i, i ^ 1) for i in range(ndp)]

    def both_cores(perm):
        return [(2 * a + c, 2 * b + c) for a, b in perm for c in (0, 1)]

    quarter = rep * 2 + core
    groups = [[r * ndp + 2 * z + c for r in (0, 1) for c in (0, 1)] for z in range(ndp // 2)]

    def other_half(w):
        deep = w.shape[0] // 4
        piece = lax.dynamic_slice_in_dim(w, quarter * deep, deep, 0)
        piece = lax.ppermute(piece, "tensor", swap)
        return lax.all_gather(
            piece, ("rep", "dp"), axis=0, tiled=True, axis_index_groups=groups
        )

    wq_other = other_half(w_query)
    wo_other = other_half(w_out)

    table = page_table
    chip_tables = jnp.concatenate([table, lax.ppermute(table, "dp", cores)], axis=0)
    peer_tables = lax.ppermute(chip_tables, "rep", swap)
    per_rep = held * ndp
    upper = chip >= 2
    is_end = (chip == 0) | (chip == 3)
    near_chip = jnp.where(upper, 1, 2)

    def locate(pages):
        page = pages % per_rep
        holder = page // held
        at = holder // 2
        ends = is_end.astype(jnp.int32)
        array = jnp.where(
            at == chip, 0, jnp.where(at == chip ^ 1, 1, jnp.where(at == near_chip, 2, 4) + ends)
        )
        return array, page % held, holder % 2 == core

    array_c, slot_c, line_c = locate(chip_tables)
    array_p, slot_p, line_p = locate(peer_tables)
    j = jnp.arange(count, dtype=jnp.int32)
    where_core = jnp.stack(
        [jnp.concatenate([array_c[1], array_p[1]]), jnp.concatenate([slot_c[1], slot_p[1]])]
    )
    lines = 6
    where_peer = jnp.stack(
        [jnp.where(line_p[0], array_p[0], lines), jnp.where(line_p[0], slot_p[0], count + j)]
    )
    home = chip_tables[0] // per_rep == rep
    where_own = jnp.stack(
        [
            jnp.where(home, jnp.where(line_c[0], array_c[0], lines), lines + 1),
            jnp.where(home & line_c[0], slot_c[0], j),
        ]
    )

    step = 32
    cos_t, sin_t = rotation_tables(starts[0] + part * rows, rows, step, head_size)
    normed, qa, kv_own, cos, sin = project(
        tokens[0], norm_gain, w_query, w_keyval, cos_t, sin_t, head_size, step
    )
    kv_peer = lax.ppermute(kv_own, "tensor", swap)

    def window_half(x):
        line = line_gather(x, both_cores, kv_own)
        given = lax.ppermute(collect(where_core, line, "pick_core"), "dp", cores)
        came = lax.ppermute(collect(where_peer, line + [given], "pick_rep"), "rep", swap)
        mine = collect(where_own, line + [given, came], "pick_own")
        return mine, lax.ppermute(mine, "tensor", swap)

    k_mine, k_peer = window_half(kv_pages[:, :, :head_size])
    v_mine, v_peer = window_half(kv_pages[:, :, head_size:])

    qb = project_other(normed, wq_other, cos, sin, head_size)
    info = jnp.stack([part, lengths[0]]).astype(jnp.int32)
    return attend_pages(
        info, qa, qb, k_mine, k_peer, v_mine, v_peer, kv_own, kv_peer, w_out, wo_other
    )[None]


def rotate_pairs(values, positions, columns_from, head_size):
    rows, cols = values.shape
    column = columns_from + jnp.arange(cols // 2, dtype=jnp.int32) * 2
    within = (column % head_size).astype(jnp.float32)
    inv_freq = jnp.exp(within * (-math.log(10000.0) / head_size))
    angle = positions[:, None] * inv_freq[None, :]
    cosine = jnp.cos(angle)
    sine = jnp.sin(angle)
    pairs = values.reshape(rows, cols // 2, 2)
    first = pairs[:, :, 0]
    second = pairs[:, :, 1]
    turned = jnp.stack([first * cosine - second * sine, first * sine + second * cosine], axis=-1)
    return turned.reshape(rows, cols)


def attend(query, keys, values, first_row, heads, head_size, window):
    rows = query.shape[0]
    count = keys.shape[0]
    q_heads = query.reshape(rows, heads, head_size)
    scores = jnp.einsum("rhd,kd->hrk", q_heads, keys, preferred_element_type=jnp.float32) * (
        1.0 / math.sqrt(head_size)
    )
    row_ids = first_row + jnp.arange(rows, dtype=jnp.int32)
    key_ids = jnp.arange(count, dtype=jnp.int32)
    seen = (key_ids[None, :] >= row_ids[:, None] + 1) & (
        key_ids[None, :] <= row_ids[:, None] + window
    )
    scores = jnp.where(seen[None, :, :], scores, -1e30)
    top = jnp.max(scores, axis=-1, keepdims=True)
    expd = jnp.exp(scores - top)
    total = jnp.sum(expd, axis=-1, keepdims=True)
    probs = (expd / total).astype(jnp.bfloat16)
    mixed = jnp.einsum("hrk,kd->rhd", probs, values, preferred_element_type=jnp.float32)
    return mixed.reshape(rows, heads * head_size).astype(jnp.bfloat16)


def shards(tokens, norm_gain, w_query, w_keyval, w_out, kv_pages, page_table, lengths, starts):
    width = tokens.shape[2]
    head_size = w_keyval.shape[1] // 2
    heads = width // head_size
    part = lax.axis_index("tensor")
    local_rows = tokens.shape[1]
    q_cols = w_query.shape[1]
    start = starts[0]
    length = lengths[0]
    xf = tokens[0].astype(jnp.float32)
    scale = lax.rsqrt(jnp.mean(xf * xf, axis=-1, keepdims=True) + 1e-06)
    normed = (xf * scale * norm_gain).astype(jnp.bfloat16)
    piece = lax.all_gather(normed, "tensor", axis=0, tiled=True)
    positions = (start + jnp.arange(piece.shape[0], dtype=jnp.int32)).astype(jnp.float32)
    query = rotate_pairs(
        jnp.dot(piece, w_query, preferred_element_type=jnp.float32),
        positions,
        part * q_cols,
        head_size,
    )
    keyval = jnp.dot(piece, w_keyval, preferred_element_type=jnp.float32)
    new_keys = rotate_pairs(keyval[:, :head_size], positions, 0, head_size)
    projected = jnp.concatenate([query, new_keys, keyval[:, head_size:]], axis=1).astype(
        jnp.bfloat16
    )
    query_cols = projected[:, :q_cols]
    keys_new = projected[:, q_cols : q_cols + head_size]
    values_new = projected[:, q_cols + head_size :]
    query = lax.all_to_all(query_cols, "tensor", split_axis=0, concat_axis=1, tiled=True)
    table = page_table[0]
    piece = lax.all_gather(kv_pages, ("rep", "dp"), axis=0, tiled=True)
    ident = jnp.arange(piece.shape[0], dtype=jnp.int32)
    onehot = (table[:, None] == ident[None, :]).astype(jnp.bfloat16)
    picked = jnp.einsum("cn,nrk->crk", onehot, piece, preferred_element_type=jnp.float32)
    window_pages = lax.all_gather(picked.astype(jnp.bfloat16), "tensor", axis=1, tiled=True)
    cached = window_pages.reshape(-1, 2 * head_size)
    window = cached.shape[0]
    keys = jnp.concatenate([cached[:, :head_size], keys_new], axis=0)
    values = jnp.concatenate([cached[:, head_size:], values_new], axis=0)
    mixed = attend(query, keys, values, part * local_rows, heads, head_size, window)
    mixed_cols = lax.all_to_all(mixed, "tensor", split_axis=1, concat_axis=0, tiled=True)
    summed = lax.psum_scatter(
        jnp.dot(mixed_cols, w_out, preferred_element_type=jnp.float32).astype(jnp.bfloat16),
        "tensor",
        scatter_dimension=0,
        tiled=True,
    ).astype(jnp.float32)
    live = part * local_rows + jnp.arange(local_rows, dtype=jnp.int32) < length
    return jnp.where(live[:, None], summed, 0.0).astype(jnp.bfloat16)[None]


def solution(mesh):
    placed = (
        P(("rep", "dp"), "tensor", None),
        P(),
        P(None, "tensor"),
        P(),
        P("tensor", None),
        P(("rep", "dp"), "tensor", None),
        P(("rep", "dp"), None),
        P(("rep", "dp")),
        P(("rep", "dp")),
    )
    line = mesh.shape["tensor"] == 2 and mesh.shape["rep"] == 2 and mesh.shape["dp"] == 8
    body = pair_shards if line else shards
    return jax.shard_map(
        body,
        mesh=mesh,
        in_specs=placed,
        out_specs=P(("rep", "dp"), "tensor", None),
        check_vma=False,
    )
```

```python
import functools
import math

import jax
import jax.numpy as jnp
from jax import lax
from jax.experimental import pallas as pl
from jax.experimental.pallas import tpu as pltpu
from jax.sharding import PartitionSpec as P

BF16 = jnp.bfloat16
F32 = jnp.float32
MASKED = -1e30
ANY = pl.ANY


def spec(space):
    return pl.BlockSpec(memory_space=space)


def rotation_tables(first, rows, step, head_size):
    column = jnp.arange(head_size, dtype=jnp.int32)
    within = (column // 2 * 2).astype(F32)
    inv_freq = jnp.exp(within * (-math.log(10000.0) / head_size))
    sign = jnp.where(column % 2 == 0, -1.0, 1.0).astype(F32)
    coarse = (first + step * jnp.arange(rows // step, dtype=jnp.int32)).astype(F32)
    fine = jnp.arange(step, dtype=jnp.int32).astype(F32)
    at = jnp.concatenate([coarse, fine])
    angle = at[:, None] * inv_freq[None, :]
    return jnp.cos(angle), jnp.sin(angle) * sign[None, :]


def fill_rotation(cos_t, sin_t, cos_s, sin_s, step):
    blocks = cos_s.shape[0] // step
    cf = cos_t[blocks:, :]
    sf = sin_t[blocks:, :]
    for u in range(blocks):
        cu = cos_t[u : u + 1, :]
        su = sin_t[u : u + 1, :]
        cos_s[u * step : (u + 1) * step, :] = cu * cf - su * sf
        sin_s[u * step : (u + 1) * step, :] = su * cf + cu * sf


def rotate(v, cos, sin, even):
    width = v.shape[1]
    swapped = jnp.where(even, pltpu.roll(v, width - 1, 1), pltpu.roll(v, 1, 1))
    return v * cos + swapped * sin


def project_kernel(head_size, step, tok, gain, wq, wkv, cos_t, sin_t, normed, q, kv, cos, sin):
    rows = tok.shape[0]
    tile = min(256, rows)
    fill_rotation(cos_t, sin_t, cos, sin, step)
    even = lax.broadcasted_iota(jnp.int32, (tile, head_size), 1) % 2 == 0
    for i in range(rows // tile):
        at = pl.ds(i * tile, tile)
        xf = tok[at, :].astype(F32)
        scale = lax.rsqrt(jnp.mean(xf * xf, axis=-1, keepdims=True) + 1e-06)
        nb = (xf * scale * gain[...]).astype(BF16)
        normed[at, :] = nb
        c = cos[at, :]
        s = sin[at, :]
        both = jnp.dot(nb, wkv[...], preferred_element_type=F32)
        kv[at, :head_size] = rotate(both[:, :head_size], c, s, even).astype(BF16)
        kv[at, head_size:] = both[:, head_size:].astype(BF16)
        for h in range(wq.shape[1] // head_size):
            cols = slice(h * head_size, (h + 1) * head_size)
            part = jnp.dot(nb, wq[:, cols], preferred_element_type=F32)
            q[at, cols] = rotate(part, c, s, even).astype(BF16)


def project(tok, gain, wq, wkv, cos_t, sin_t, head_size, step):
    rows, width = tok.shape
    qc, kc = wq.shape[1], wkv.shape[1]
    return pl.pallas_call(
        functools.partial(project_kernel, head_size, step),
        out_shape=(
            jax.ShapeDtypeStruct((rows, width), BF16),
            jax.ShapeDtypeStruct((rows, qc), BF16),
            jax.ShapeDtypeStruct((rows, kc), BF16),
            jax.ShapeDtypeStruct((rows, head_size), F32),
            jax.ShapeDtypeStruct((rows, head_size), F32),
        ),
        in_specs=[spec(pltpu.VMEM)] * 6,
        out_specs=[spec(pltpu.VMEM)] * 5,
        compiler_params=pltpu.CompilerParams(vmem_limit_bytes=20 * 2**20),
        cost_estimate=pl.CostEstimate(
            flops=2 * rows * width * (qc + kc), bytes_accessed=10 * 2**20, transcendentals=0
        ),
        name="project_own",
    )(tok, gain.reshape(1, width), wq, wkv, cos_t, sin_t)


def other_kernel(head_size, normed, wq, cos, sin, q):
    rows = normed.shape[0]
    tile = min(256, rows)
    even = lax.broadcasted_iota(jnp.int32, (tile, head_size), 1) % 2 == 0
    for i in range(rows // tile):
        at = pl.ds(i * tile, tile)
        c = cos[at, :]
        s = sin[at, :]
        for h in range(q.shape[1] // head_size):
            cols = slice(h * head_size, (h + 1) * head_size)
            part = jnp.dot(normed[at, :], wq[:, cols], preferred_element_type=F32)
            q[at, cols] = rotate(part, c, s, even).astype(BF16)


def project_other(normed, wq, cos, sin, head_size):
    rows, width = normed.shape
    qc = wq.shape[1]
    return pl.pallas_call(
        functools.partial(other_kernel, head_size),
        out_shape=jax.ShapeDtypeStruct((rows, qc), BF16),
        in_specs=[spec(pltpu.VMEM)] * 4,
        out_specs=spec(pltpu.VMEM),
        compiler_params=pltpu.CompilerParams(vmem_limit_bytes=20 * 2**20),
        cost_estimate=pl.CostEstimate(
            flops=2 * rows * width * qc, bytes_accessed=6 * 2**20, transcendentals=0
        ),
        name="project_other",
    )(normed, wq, cos, sin)


def collect_kernel(where, *refs):
    arrays, out = refs[:-1], refs[-1]

    def one(j, _):
        for n, array in enumerate(arrays):

            @pl.when(where[0, j] == n)
            def _():
                out[j] = array[where[1, j]]

        return 0

    lax.fori_loop(0, out.shape[0], one, 0)


def collect(where, arrays, name):
    count = where.shape[1]
    shape = (count,) + arrays[0].shape[1:]
    return pl.pallas_call(
        collect_kernel,
        out_shape=jax.ShapeDtypeStruct(shape, arrays[0].dtype),
        in_specs=[spec(pltpu.SMEM)] + [spec(pltpu.VMEM)] * len(arrays),
        out_specs=spec(pltpu.VMEM),
        compiler_params=pltpu.CompilerParams(vmem_limit_bytes=12 * 2**20),
        cost_estimate=pl.CostEstimate(flops=0, bytes_accessed=1024, transcendentals=0),
        name=name,
    )(where, *arrays)


def start_rows(part, mine, peer, kv_own, kv_peer, lo, dst, sem):
    pages, prow, head_size = mine.shape
    rows = kv_own.shape[0]
    page = 2 * prow
    window = pages * page
    cols = pl.ds(lo, head_size)
    for case in (0, 1):

        @pl.when(part == case)
        def _():
            skip = case * rows // page
            for u in range(skip, pages):
                for src, side in ((mine, case), (peer, 1 - case)):
                    to = pl.ds((u - skip) * page + side * prow, prow)
                    pltpu.make_async_copy(src.at[u], dst.at[to, :], sem).start()
            if case == 1:
                to = pl.ds(window - rows, rows)
                pltpu.make_async_copy(kv_peer.at[:, cols], dst.at[to, :], sem).start()
            to = pl.ds(window, rows)
            pltpu.make_async_copy(kv_own.at[:, cols], dst.at[to, :], sem).start()


def finish_rows(dst, sem):
    pltpu.make_async_copy(dst, dst, sem).wait()


def weigh_kernel(
    head_size, info, qa_hbm, qb_hbm, k_mine, k_peer, kv_own, kv_peer, probs, qa, qb, keys, done, ksem, qsem, psem
):
    rows, half = qa.shape
    start_rows(info[0], k_mine, k_peer, kv_own, kv_peer, 0, keys, ksem)
    loads = [
        pltpu.make_async_copy(qa_hbm, qa, qsem.at[0]),
        pltpu.make_async_copy(qb_hbm, qb, qsem.at[1]),
    ]
    for c in loads:
        c.start()
    nheads = half // head_size
    span = probs.shape[2]
    tile = span + rows - keys.shape[0]
    row_id = lax.broadcasted_iota(jnp.int32, (tile, tile), 0)
    col_id = lax.broadcasted_iota(jnp.int32, (tile, tile), 1)
    first_seen = col_id >= row_id + 1
    last_seen = col_id <= row_id
    factor = math.log2(math.e) / math.sqrt(head_size)
    for c in loads:
        c.wait()
    finish_rows(keys, ksem)
    stores = []
    for i in range(rows // tile):
        at = pl.ds(i * tile, tile)
        for n, q in enumerate((qa, qb)):
            for h in range(nheads):
                kk = keys[pl.ds(i * tile, span), :]
                s = lax.dot_general(
                    q[at, h * head_size : (h + 1) * head_size],
                    kk,
                    (((1,), (1,)), ((), ())),
                    preferred_element_type=F32,
                )
                s = jnp.concatenate(
                    [
                        jnp.where(first_seen, s[:, :tile], MASKED),
                        s[:, tile : span - tile],
                        jnp.where(last_seen, s[:, span - tile :], MASKED),
                    ],
                    axis=1,
                )
                top = jnp.max(s, axis=-1, keepdims=True)
                e = jnp.exp2((s - top) * factor)
                total = jnp.sum(e, axis=-1, keepdims=True)
                m = len(stores)
                done[m] = (e * (1.0 / total)).astype(BF16)
                stores.append(
                    pltpu.make_async_copy(done.at[m], probs.at[n * nheads + h, at, :], psem.at[m])
                )
                stores[m].start()
    for c in stores:
        c.wait()


def weigh(info, qa, qb, k_mine, k_peer, kv_own, kv_peer):
    rows, half = qa.shape
    head_size = k_mine.shape[2]
    heads = 2 * half // head_size
    window = k_mine.shape[0] * k_mine.shape[1] * 2
    span = window + min(256, rows)
    chunks = heads * rows // (span - window)
    return pl.pallas_call(
        functools.partial(weigh_kernel, head_size),
        out_shape=jax.ShapeDtypeStruct((heads, rows, span), BF16),
        in_specs=[spec(pltpu.SMEM)] + [spec(ANY)] * 6,
        out_specs=spec(ANY),
        scratch_shapes=[
            pltpu.VMEM((rows, half), BF16),
            pltpu.VMEM((rows, half), BF16),
            pltpu.VMEM((window + rows, head_size), BF16),
            pltpu.VMEM((chunks, span - window, span), BF16),
            pltpu.SemaphoreType.DMA,
            pltpu.SemaphoreType.DMA((2,)),
            pltpu.SemaphoreType.DMA((chunks,)),
        ],
        compiler_params=pltpu.CompilerParams(vmem_limit_bytes=56 * 2**20),
        cost_estimate=pl.CostEstimate(
            flops=4 * rows * half * span,
            bytes_accessed=12 * 2**20,
            transcendentals=rows * heads * span,
        ),
        name="scores_softmax",
    )(info, qa, qb, k_mine, k_peer, kv_own, kv_peer)


def out_kernel(
    info, probs, v_mine, v_peer, kv_own, kv_peer, woa, wob, out, vals, pv, wa, wb, mix, vsem, psem, wsem
):
    part = info[0]
    length = info[1]
    heads, rows, span = probs.shape
    head_size = vals.shape[1]
    width = out.shape[1]
    nheads = heads // 2
    tile = span + rows - vals.shape[0]
    start_rows(part, v_mine, v_peer, kv_own, kv_peer, head_size, vals, vsem)
    order = [(i, h) for i in range(rows // tile) for h in range(heads)]
    loads = [
        pltpu.make_async_copy(probs.at[h, pl.ds(i * tile, tile), :], pv.at[m], psem.at[m])
        for m, (i, h) in enumerate(order)
    ]
    for c in loads:
        c.start()
    weights = [
        pltpu.make_async_copy(woa, wa, wsem.at[0]),
        pltpu.make_async_copy(wob, wb, wsem.at[1]),
    ]
    for c in weights:
        c.start()
    finish_rows(vals, vsem)
    for m, (i, h) in enumerate(order):
        vv = vals[pl.ds(i * tile, span), :]
        loads[m].wait()
        mixed = jnp.dot(pv[m], vv, preferred_element_type=F32).astype(BF16)
        lo = h % nheads * head_size
        mix[h // nheads, pl.ds(i * tile, tile), lo : lo + head_size] = mixed
    for c in weights:
        c.wait()
    for i in range(rows // tile):
        at = pl.ds(i * tile, tile)
        row = part * rows + i * tile + lax.broadcasted_iota(jnp.int32, (tile, 1), 0)
        live = row < length
        for lo in range(0, width, 512):
            cols = slice(lo, lo + 512)
            a = jnp.dot(mix[0, at, :], wa[:, cols], preferred_element_type=F32)
            b = jnp.dot(mix[1, at, :], wb[:, cols], preferred_element_type=F32)
            both = a.astype(BF16).astype(F32) + b.astype(BF16).astype(F32)
            out[at, cols] = jnp.where(live, both, 0.0).astype(BF16)


def mix_and_out(info, probs, v_mine, v_peer, kv_own, kv_peer, woa, wob):
    heads, rows, span = probs.shape
    half, width = woa.shape
    head_size = v_mine.shape[2]
    window = v_mine.shape[0] * v_mine.shape[1] * 2
    chunks = heads * rows // (span - window)
    return pl.pallas_call(
        out_kernel,
        out_shape=jax.ShapeDtypeStruct((rows, width), BF16),
        in_specs=[spec(pltpu.SMEM)] + [spec(ANY)] * 7,
        out_specs=spec(pltpu.VMEM),
        scratch_shapes=[
            pltpu.VMEM((window + rows, head_size), BF16),
            pltpu.VMEM((chunks, span - window, span), BF16),
            pltpu.VMEM(woa.shape, BF16),
            pltpu.VMEM(wob.shape, BF16),
            pltpu.VMEM((2, rows, half), BF16),
            pltpu.SemaphoreType.DMA,
            pltpu.SemaphoreType.DMA((chunks,)),
            pltpu.SemaphoreType.DMA((2,)),
        ],
        compiler_params=pltpu.CompilerParams(vmem_limit_bytes=56 * 2**20),
        cost_estimate=pl.CostEstimate(
            flops=4 * rows * half * span + 4 * rows * half * width,
            bytes_accessed=16 * 2**20,
            transcendentals=0,
        ),
        name="mix_and_out",
    )(info, probs, v_mine, v_peer, kv_own, kv_peer, woa, wob)


def first_hop(x, swap_at):
    pairs = swap_at([(0, 1), (1, 0), (2, 3), (3, 2)])
    middle = swap_at([(1, 2), (2, 1)])
    return lax.ppermute(x, "dp", pairs), lax.ppermute(x, "dp", middle)


def pair_shards(tokens, norm_gain, w_query, w_keyval, w_out, kv_pages, page_table, lengths, starts):
    head_size = w_keyval.shape[1] // 2
    part = lax.axis_index("tensor")
    rep = lax.axis_index("rep")
    dp = lax.axis_index("dp")
    ndp = lax.axis_size("dp")
    chip, core = dp // 2, dp % 2
    rows = tokens.shape[1]
    held = kv_pages.shape[0]
    count = page_table.shape[1]
    swap = [(0, 1), (1, 0)]
    cores = [(i, i ^ 1) for i in range(ndp)]

    def both_cores(perm):
        return [(2 * a + c, 2 * b + c) for a, b in perm for c in (0, 1)]

    k_pages = kv_pages[:, :, :head_size]
    v_pages = kv_pages[:, :, head_size:]
    k_first = first_hop(k_pages, both_cores)
    v_first = first_hop(v_pages, both_cores)

    quarter = rep * 2 + core
    groups = [[r * ndp + 2 * z + c for r in (0, 1) for c in (0, 1)] for z in range(ndp // 2)]

    def peer_quarter(w):
        deep = w.shape[0] // 4
        return lax.ppermute(lax.dynamic_slice_in_dim(w, quarter * deep, deep, 0), "tensor", swap)

    def share(piece):
        return lax.all_gather(piece, ("rep", "dp"), axis=0, tiled=True, axis_index_groups=groups)

    wq_piece = peer_quarter(w_query)

    step = 32
    cos_t, sin_t = rotation_tables(starts[0] + part * rows, rows, step, head_size)
    normed, qa, kv_own, cos, sin = project(
        tokens[0], norm_gain, w_query, w_keyval, cos_t, sin_t, head_size, step
    )
    kv_peer = lax.ppermute(kv_own, "tensor", swap)

    table, kv_own = lax.optimization_barrier((page_table, kv_own))
    chip_tables = jnp.concatenate([table, lax.ppermute(table, "dp", cores)], axis=0)
    peer_tables = lax.ppermute(chip_tables, "rep", swap)
    per_rep = held * ndp
    upper = chip >= 2
    is_end = (chip == 0) | (chip == 3)
    near_chip = jnp.where(upper, 1, 2)

    def locate(pages):
        page = pages % per_rep
        holder = page // held
        at = holder // 2
        ends = is_end.astype(jnp.int32)
        array = jnp.where(
            at == chip, 0, jnp.where(at == chip ^ 1, 1, jnp.where(at == near_chip, 2, 4) + ends)
        )
        return array, page % held, holder % 2 == core

    array_c, slot_c, line_c = locate(chip_tables)
    array_p, slot_p, line_p = locate(peer_tables)
    j = jnp.arange(count, dtype=jnp.int32)
    where_core = jnp.stack(
        [jnp.concatenate([array_c[1], array_p[1]]), jnp.concatenate([slot_c[1], slot_p[1]])]
    )
    lines = 6
    where_peer = jnp.stack(
        [jnp.where(line_p[0], array_p[0], lines), jnp.where(line_p[0], slot_p[0], count + j)]
    )
    home = chip_tables[0] // per_rep == rep
    where_own = jnp.stack(
        [
            jnp.where(home, jnp.where(line_c[0], array_c[0], lines), lines + 1),
            jnp.where(home & line_c[0], slot_c[0], j),
        ]
    )

    middle = both_cores([(1, 2), (2, 1)])
    outward = both_cores([(1, 0), (2, 3)])
    kf, kn, _ = lax.optimization_barrier((*k_first, kv_own))
    k_near = lax.ppermute(kn, "dp", outward)
    k_far = lax.ppermute(kf, "dp", middle)
    wq_piece, w_out_late, _ = lax.optimization_barrier((wq_piece, w_out, kf))
    vf, vn = v_first
    v_far = lax.ppermute(vf, "dp", middle)
    v_near = lax.ppermute(vn, "dp", outward)
    wq_other = share(wq_piece)
    wo_piece = peer_quarter(w_out_late)
    k_far, k_near, v_far, v_near = lax.optimization_barrier((k_far, k_near, v_far, v_near))
    k_end = lax.ppermute(k_far, "dp", outward)
    v_end = lax.ppermute(v_far, "dp", outward)
    k_end, wo_piece = lax.optimization_barrier((k_end, wo_piece))
    wo_other = share(wo_piece)
    k_line = [k_pages, kf, kn, k_near, k_far, k_end]
    k_given = lax.ppermute(collect(where_core, k_line, "pick_core"), "dp", cores)
    k_given, v_end, kv_peer = lax.optimization_barrier((k_given, v_end, kv_peer))
    v_line = [v_pages, vf, vn, v_near, v_far, v_end]
    v_given = lax.ppermute(collect(where_core, v_line, "pick_core"), "dp", cores)
    k_came = lax.ppermute(collect(where_peer, k_line + [k_given], "pick_rep"), "rep", swap)
    k_came, v_given = lax.optimization_barrier((k_came, v_given))
    v_came = lax.ppermute(collect(where_peer, v_line + [v_given], "pick_rep"), "rep", swap)
    k_mine = collect(where_own, k_line + [k_given, k_came], "pick_own")
    k_peer = lax.ppermute(k_mine, "tensor", swap)
    v_mine = collect(where_own, v_line + [v_given, v_came], "pick_own")
    v_peer = lax.ppermute(v_mine, "tensor", swap)

    qb = project_other(normed, wq_other, cos, sin, head_size)
    info = jnp.stack([part, lengths[0]]).astype(jnp.int32)
    probs = weigh(info, qa, qb, k_mine, k_peer, kv_own, kv_peer)
    return mix_and_out(info, probs, v_mine, v_peer, kv_own, kv_peer, w_out, wo_other)[None]


def rotate_pairs(values, positions, columns_from, head_size):
    rows, cols = values.shape
    column = columns_from + jnp.arange(cols // 2, dtype=jnp.int32) * 2
    within = (column % head_size).astype(jnp.float32)
    inv_freq = jnp.exp(within * (-math.log(10000.0) / head_size))
    angle = positions[:, None] * inv_freq[None, :]
    cosine = jnp.cos(angle)
    sine = jnp.sin(angle)
    pairs = values.reshape(rows, cols // 2, 2)
    first = pairs[:, :, 0]
    second = pairs[:, :, 1]
    turned = jnp.stack([first * cosine - second * sine, first * sine + second * cosine], axis=-1)
    return turned.reshape(rows, cols)


def attend(query, keys, values, first_row, heads, head_size, window):
    rows = query.shape[0]
    count = keys.shape[0]
    q_heads = query.reshape(rows, heads, head_size)
    scores = jnp.einsum("rhd,kd->hrk", q_heads, keys, preferred_element_type=jnp.float32) * (
        1.0 / math.sqrt(head_size)
    )
    row_ids = first_row + jnp.arange(rows, dtype=jnp.int32)
    key_ids = jnp.arange(count, dtype=jnp.int32)
    seen = (key_ids[None, :] >= row_ids[:, None] + 1) & (
        key_ids[None, :] <= row_ids[:, None] + window
    )
    scores = jnp.where(seen[None, :, :], scores, -1e30)
    top = jnp.max(scores, axis=-1, keepdims=True)
    expd = jnp.exp(scores - top)
    total = jnp.sum(expd, axis=-1, keepdims=True)
    probs = (expd / total).astype(jnp.bfloat16)
    mixed = jnp.einsum("hrk,kd->rhd", probs, values, preferred_element_type=jnp.float32)
    return mixed.reshape(rows, heads * head_size).astype(jnp.bfloat16)


def shards(tokens, norm_gain, w_query, w_keyval, w_out, kv_pages, page_table, lengths, starts):
    width = tokens.shape[2]
    head_size = w_keyval.shape[1] // 2
    heads = width // head_size
    part = lax.axis_index("tensor")
    local_rows = tokens.shape[1]
    q_cols = w_query.shape[1]
    start = starts[0]
    length = lengths[0]
    xf = tokens[0].astype(jnp.float32)
    scale = lax.rsqrt(jnp.mean(xf * xf, axis=-1, keepdims=True) + 1e-06)
    normed = (xf * scale * norm_gain).astype(jnp.bfloat16)
    piece = lax.all_gather(normed, "tensor", axis=0, tiled=True)
    positions = (start + jnp.arange(piece.shape[0], dtype=jnp.int32)).astype(jnp.float32)
    query = rotate_pairs(
        jnp.dot(piece, w_query, preferred_element_type=jnp.float32),
        positions,
        part * q_cols,
        head_size,
    )
    keyval = jnp.dot(piece, w_keyval, preferred_element_type=jnp.float32)
    new_keys = rotate_pairs(keyval[:, :head_size], positions, 0, head_size)
    projected = jnp.concatenate([query, new_keys, keyval[:, head_size:]], axis=1).astype(
        jnp.bfloat16
    )
    query_cols = projected[:, :q_cols]
    keys_new = projected[:, q_cols : q_cols + head_size]
    values_new = projected[:, q_cols + head_size :]
    query = lax.all_to_all(query_cols, "tensor", split_axis=0, concat_axis=1, tiled=True)
    table = page_table[0]
    piece = lax.all_gather(kv_pages, ("rep", "dp"), axis=0, tiled=True)
    ident = jnp.arange(piece.shape[0], dtype=jnp.int32)
    onehot = (table[:, None] == ident[None, :]).astype(jnp.bfloat16)
    picked = jnp.einsum("cn,nrk->crk", onehot, piece, preferred_element_type=jnp.float32)
    window_pages = lax.all_gather(picked.astype(jnp.bfloat16), "tensor", axis=1, tiled=True)
    cached = window_pages.reshape(-1, 2 * head_size)
    window = cached.shape[0]
    keys = jnp.concatenate([cached[:, :head_size], keys_new], axis=0)
    values = jnp.concatenate([cached[:, head_size:], values_new], axis=0)
    mixed = attend(query, keys, values, part * local_rows, heads, head_size, window)
    mixed_cols = lax.all_to_all(mixed, "tensor", split_axis=1, concat_axis=0, tiled=True)
    summed = lax.psum_scatter(
        jnp.dot(mixed_cols, w_out, preferred_element_type=jnp.float32).astype(jnp.bfloat16),
        "tensor",
        scatter_dimension=0,
        tiled=True,
    ).astype(jnp.float32)
    live = part * local_rows + jnp.arange(local_rows, dtype=jnp.int32) < length
    return jnp.where(live[:, None], summed, 0.0).astype(jnp.bfloat16)[None]


def solution(mesh):
    placed = (
        P(("rep", "dp"), "tensor", None),
        P(),
        P(None, "tensor"),
        P(),
        P("tensor", None),
        P(("rep", "dp"), "tensor", None),
        P(("rep", "dp"), None),
        P(("rep", "dp")),
        P(("rep", "dp")),
    )
    line = mesh.shape["tensor"] == 2 and mesh.shape["rep"] == 2 and mesh.shape["dp"] == 8
    body = pair_shards if line else shards
    return jax.shard_map(
        body,
        mesh=mesh,
        in_specs=placed,
        out_specs=P(("rep", "dp"), "tensor", None),
        check_vma=False,
    )
```

```python
import functools
import math

import jax
import jax.numpy as jnp
from jax import lax
from jax.experimental import pallas as pl
from jax.experimental.pallas import tpu as pltpu
from jax.sharding import PartitionSpec as P

BF16 = jnp.bfloat16
F32 = jnp.float32
MASKED = -1e30
ANY = pl.ANY


def spec(space):
    return pl.BlockSpec(memory_space=space)


def rotation_tables(first, rows, step, head_size):
    column = jnp.arange(head_size, dtype=jnp.int32)
    within = (column // 2 * 2).astype(F32)
    inv_freq = jnp.exp(within * (-math.log(10000.0) / head_size))
    sign = jnp.where(column % 2 == 0, -1.0, 1.0).astype(F32)
    coarse = (first + step * jnp.arange(rows // step, dtype=jnp.int32)).astype(F32)
    fine = jnp.arange(step, dtype=jnp.int32).astype(F32)
    at = jnp.concatenate([coarse, fine])
    angle = at[:, None] * inv_freq[None, :]
    return jnp.cos(angle), jnp.sin(angle) * sign[None, :]


def fill_rotation(cos_t, sin_t, cos_s, sin_s, step):
    blocks = cos_s.shape[0] // step
    cf = cos_t[blocks:, :]
    sf = sin_t[blocks:, :]
    for u in range(blocks):
        cu = cos_t[u : u + 1, :]
        su = sin_t[u : u + 1, :]
        cos_s[u * step : (u + 1) * step, :] = cu * cf - su * sf
        sin_s[u * step : (u + 1) * step, :] = su * cf + cu * sf


def rotate(v, cos, sin, even):
    width = v.shape[1]
    swapped = jnp.where(even, pltpu.roll(v, width - 1, 1), pltpu.roll(v, 1, 1))
    return v * cos + swapped * sin


def project_kernel(head_size, step, tok, gain, wq, wkv, cos_t, sin_t, normed, q, kv, cos, sin):
    rows = tok.shape[0]
    tile = min(256, rows)
    fill_rotation(cos_t, sin_t, cos, sin, step)
    even = lax.broadcasted_iota(jnp.int32, (tile, head_size), 1) % 2 == 0
    for i in range(rows // tile):
        at = pl.ds(i * tile, tile)
        xf = tok[at, :].astype(F32)
        scale = lax.rsqrt(jnp.mean(xf * xf, axis=-1, keepdims=True) + 1e-06)
        nb = (xf * scale * gain[...]).astype(BF16)
        normed[at, :] = nb
        c = cos[at, :]
        s = sin[at, :]
        both = jnp.dot(nb, wkv[...], preferred_element_type=F32)
        kv[at, :head_size] = rotate(both[:, :head_size], c, s, even).astype(BF16)
        kv[at, head_size:] = both[:, head_size:].astype(BF16)
        for h in range(wq.shape[1] // head_size):
            cols = slice(h * head_size, (h + 1) * head_size)
            part = jnp.dot(nb, wq[:, cols], preferred_element_type=F32)
            q[at, cols] = rotate(part, c, s, even).astype(BF16)


def project(tok, gain, wq, wkv, cos_t, sin_t, head_size, step):
    rows, width = tok.shape
    qc, kc = wq.shape[1], wkv.shape[1]
    return pl.pallas_call(
        functools.partial(project_kernel, head_size, step),
        out_shape=(
            jax.ShapeDtypeStruct((rows, width), BF16),
            jax.ShapeDtypeStruct((rows, qc), BF16),
            jax.ShapeDtypeStruct((rows, kc), BF16),
            jax.ShapeDtypeStruct((rows, head_size), F32),
            jax.ShapeDtypeStruct((rows, head_size), F32),
        ),
        in_specs=[spec(pltpu.VMEM)] * 6,
        out_specs=[spec(pltpu.VMEM)] * 5,
        compiler_params=pltpu.CompilerParams(vmem_limit_bytes=20 * 2**20),
        cost_estimate=pl.CostEstimate(
            flops=2 * rows * width * (qc + kc), bytes_accessed=10 * 2**20, transcendentals=0
        ),
        name="project_own",
    )(tok, gain.reshape(1, width), wq, wkv, cos_t, sin_t)


def other_kernel(head_size, normed, wq_hbm, cos, sin, wo, q, wo_held, wq, sem):
    rows = normed.shape[0]
    heads = q.shape[1] // head_size
    loads = [
        pltpu.make_async_copy(wq_hbm.at[:, pl.ds(h * head_size, head_size)], wq.at[h], sem.at[h])
        for h in range(heads)
    ]
    loads.append(pltpu.make_async_copy(wo, wo_held, sem.at[heads]))
    for c in loads:
        c.start()
    tile = min(256, rows)
    even = lax.broadcasted_iota(jnp.int32, (tile, head_size), 1) % 2 == 0
    for h in range(heads):
        loads[h].wait()
        for i in range(rows // tile):
            at = pl.ds(i * tile, tile)
            part = jnp.dot(normed[at, :], wq[h], preferred_element_type=F32)
            turned = rotate(part, cos[at, :], sin[at, :], even)
            q[at, h * head_size : (h + 1) * head_size] = turned.astype(BF16)
    loads[heads].wait()


def project_other(normed, wq, cos, sin, wo, head_size):
    rows, width = normed.shape
    qc = wq.shape[1]
    heads = qc // head_size
    return pl.pallas_call(
        functools.partial(other_kernel, head_size),
        out_shape=(
            jax.ShapeDtypeStruct((rows, qc), BF16),
            jax.ShapeDtypeStruct(wo.shape, BF16),
        ),
        in_specs=[
            spec(pltpu.VMEM),
            spec(pltpu.HBM),
            spec(pltpu.VMEM),
            spec(pltpu.VMEM),
            spec(pltpu.HBM),
        ],
        out_specs=[spec(pltpu.VMEM)] * 2,
        scratch_shapes=[
            pltpu.VMEM((heads, width, head_size), BF16),
            pltpu.SemaphoreType.DMA((heads + 1,)),
        ],
        compiler_params=pltpu.CompilerParams(vmem_limit_bytes=20 * 2**20),
        cost_estimate=pl.CostEstimate(
            flops=2 * rows * width * qc, bytes_accessed=4 * 2**20, transcendentals=0
        ),
        name="project_other",
    )(normed, wq, cos, sin, wo)


def collect_kernel(where, *refs):
    arrays, out = refs[:-1], refs[-1]

    def one(j, _):
        for n, array in enumerate(arrays):

            @pl.when(where[0, j] == n)
            def _():
                out[j] = array[where[1, j]]

        return 0

    lax.fori_loop(0, out.shape[0], one, 0)


def collect(where, arrays, name):
    count = where.shape[1]
    shape = (count,) + arrays[0].shape[1:]
    return pl.pallas_call(
        collect_kernel,
        out_shape=jax.ShapeDtypeStruct(shape, arrays[0].dtype),
        in_specs=[spec(pltpu.SMEM)] + [spec(pltpu.VMEM)] * len(arrays),
        out_specs=spec(pltpu.VMEM),
        compiler_params=pltpu.CompilerParams(vmem_limit_bytes=12 * 2**20),
        cost_estimate=pl.CostEstimate(flops=0, bytes_accessed=1024, transcendentals=0),
        name=name,
    )(where, *arrays)


def gather_rows(part, mine, peer, kv_own, kv_peer, lo, dst):
    pages, prow, head_size = mine.shape
    rows = kv_own.shape[0]
    page = 2 * prow
    window = pages * page
    cols = slice(lo, lo + head_size)
    for case in (0, 1):

        @pl.when(part == case)
        def _():
            skip = case * rows // page
            for u in range(skip, pages):
                for src, side in ((mine, case), (peer, 1 - case)):
                    at = (u - skip) * page + side * prow
                    dst[at : at + prow, :] = src[u]
            if case == 1:
                dst[window - rows : window, :] = kv_peer[:, cols]
            dst[window : window + rows, :] = kv_own[:, cols]


def weigh_kernel(
    head_size, info, qa, qb, k_mine, k_peer, kv_own, kv_peer, probs, keys
):
    rows, half = qa.shape
    gather_rows(info[0], k_mine, k_peer, kv_own, kv_peer, 0, keys)
    nheads = half // head_size
    span = probs.shape[2]
    tile = span + rows - keys.shape[0]
    row_id = lax.broadcasted_iota(jnp.int32, (tile, tile), 0)
    col_id = lax.broadcasted_iota(jnp.int32, (tile, tile), 1)
    first_seen = col_id >= row_id + 1
    last_seen = col_id <= row_id
    factor = math.log2(math.e) / math.sqrt(head_size)
    for i in range(rows // tile):
        at = pl.ds(i * tile, tile)
        for n, q in enumerate((qa, qb)):
            for h in range(nheads):
                s = lax.dot_general(
                    q[at, h * head_size : (h + 1) * head_size],
                    keys[pl.ds(i * tile, span), :],
                    (((1,), (1,)), ((), ())),
                    preferred_element_type=F32,
                )
                s = jnp.concatenate(
                    [
                        jnp.where(first_seen, s[:, :tile], MASKED),
                        s[:, tile : span - tile],
                        jnp.where(last_seen, s[:, span - tile :], MASKED),
                    ],
                    axis=1,
                )
                top = jnp.max(s, axis=-1, keepdims=True)
                e = jnp.exp2((s - top) * factor)
                total = jnp.sum(e, axis=-1, keepdims=True)
                probs[n * nheads + h, at, :] = (e * (1.0 / total)).astype(BF16)


def weigh(info, qa, qb, k_mine, k_peer, kv_own, kv_peer):
    rows, half = qa.shape
    head_size = k_mine.shape[2]
    heads = 2 * half // head_size
    window = k_mine.shape[0] * k_mine.shape[1] * 2
    span = window + min(256, rows)
    return pl.pallas_call(
        functools.partial(weigh_kernel, head_size),
        out_shape=jax.ShapeDtypeStruct((heads, rows, span), BF16),
        in_specs=[spec(pltpu.SMEM)] + [spec(pltpu.VMEM)] * 6,
        out_specs=spec(pltpu.VMEM),
        scratch_shapes=[pltpu.VMEM((window + rows, head_size), BF16)],
        compiler_params=pltpu.CompilerParams(vmem_limit_bytes=28 * 2**20),
        cost_estimate=pl.CostEstimate(
            flops=4 * rows * half * span,
            bytes_accessed=6 * 2**20,
            transcendentals=rows * heads * span,
        ),
        name="scores_softmax",
    )(info, qa, qb, k_mine, k_peer, kv_own, kv_peer)


def out_kernel(info, probs, v_mine, v_peer, kv_own, kv_peer, wa, wb, out, vals, mix):
    part = info[0]
    length = info[1]
    heads, rows, span = probs.shape
    head_size = vals.shape[1]
    width = out.shape[1]
    nheads = heads // 2
    tile = span + rows - vals.shape[0]
    gather_rows(part, v_mine, v_peer, kv_own, kv_peer, head_size, vals)
    for i in range(rows // tile):
        at = pl.ds(i * tile, tile)
        for h in range(heads):
            vv = vals[pl.ds(i * tile, span), :]
            mixed = jnp.dot(probs[h, at, :], vv, preferred_element_type=F32).astype(BF16)
            lo = h % nheads * head_size
            mix[h // nheads, at, lo : lo + head_size] = mixed
        row = part * rows + i * tile + lax.broadcasted_iota(jnp.int32, (tile, 1), 0)
        live = row < length
        for lo in range(0, width, 512):
            cols = slice(lo, lo + 512)
            a = jnp.dot(mix[0, at, :], wa[:, cols], preferred_element_type=F32)
            b = jnp.dot(mix[1, at, :], wb[:, cols], preferred_element_type=F32)
            both = a.astype(BF16).astype(F32) + b.astype(BF16).astype(F32)
            out[at, cols] = jnp.where(live, both, 0.0).astype(BF16)


def mix_and_out(info, probs, v_mine, v_peer, kv_own, kv_peer, wa, wb):
    heads, rows, span = probs.shape
    half, width = wa.shape
    head_size = v_mine.shape[2]
    window = v_mine.shape[0] * v_mine.shape[1] * 2
    return pl.pallas_call(
        out_kernel,
        out_shape=jax.ShapeDtypeStruct((rows, width), BF16),
        in_specs=[spec(pltpu.SMEM)] + [spec(pltpu.VMEM)] * 7,
        out_specs=spec(pltpu.VMEM),
        scratch_shapes=[
            pltpu.VMEM((window + rows, head_size), BF16),
            pltpu.VMEM((2, rows, half), BF16),
        ],
        compiler_params=pltpu.CompilerParams(vmem_limit_bytes=28 * 2**20),
        cost_estimate=pl.CostEstimate(
            flops=4 * rows * half * span + 4 * rows * half * width,
            bytes_accessed=4 * 2**20,
            transcendentals=0,
        ),
        name="mix_and_out",
    )(info, probs, v_mine, v_peer, kv_own, kv_peer, wa, wb)


def first_hop(x, swap_at):
    pairs = swap_at([(0, 1), (1, 0), (2, 3), (3, 2)])
    middle = swap_at([(1, 2), (2, 1)])
    return lax.ppermute(x, "dp", pairs), lax.ppermute(x, "dp", middle)


def pair_shards(tokens, norm_gain, w_query, w_keyval, w_out, kv_pages, page_table, lengths, starts):
    head_size = w_keyval.shape[1] // 2
    part = lax.axis_index("tensor")
    rep = lax.axis_index("rep")
    dp = lax.axis_index("dp")
    ndp = lax.axis_size("dp")
    chip, core = dp // 2, dp % 2
    rows = tokens.shape[1]
    held = kv_pages.shape[0]
    count = page_table.shape[1]
    swap = [(0, 1), (1, 0)]
    cores = [(i, i ^ 1) for i in range(ndp)]

    def both_cores(perm):
        return [(2 * a + c, 2 * b + c) for a, b in perm for c in (0, 1)]

    k_pages = kv_pages[:, :, :head_size]
    v_pages = kv_pages[:, :, head_size:]
    k_first = first_hop(k_pages, both_cores)
    v_first = first_hop(v_pages, both_cores)

    quads = [[r * ndp + 2 * z + c for r in (0, 1) for c in (0, 1)] for z in range(ndp // 2)]
    chips = [[2 * z, 2 * z + 1] for z in range(ndp // 2)]

    def peer_rows(w, at, parts):
        deep = w.shape[0] // parts
        return lax.ppermute(lax.dynamic_slice_in_dim(w, at * deep, deep, 0), "tensor", swap)

    wq_piece = peer_rows(w_query, rep * 2 + core, 4)

    kf, kn, vf, vn, wq_piece, tokens, w_out_late, table = lax.optimization_barrier(
        (*k_first, *v_first, wq_piece, tokens, w_out, page_table)
    )
    wq_other = lax.all_gather(wq_piece, ("rep", "dp"), axis=0, tiled=True, axis_index_groups=quads)
    wo_piece = peer_rows(w_out_late, core, 2)

    step = 32
    cos_t, sin_t = rotation_tables(starts[0] + part * rows, rows, step, head_size)
    normed, qa, kv_own, cos, sin = project(
        tokens[0], norm_gain, w_query, w_keyval, cos_t, sin_t, head_size, step
    )
    kv_peer = lax.ppermute(kv_own, "tensor", swap)

    chip_tables = jnp.concatenate([table, lax.ppermute(table, "dp", cores)], axis=0)
    peer_tables = lax.ppermute(chip_tables, "rep", swap)
    per_rep = held * ndp
    upper = chip >= 2
    is_end = (chip == 0) | (chip == 3)
    near_chip = jnp.where(upper, 1, 2)

    def locate(pages):
        page = pages % per_rep
        holder = page // held
        at = holder // 2
        ends = is_end.astype(jnp.int32)
        array = jnp.where(
            at == chip, 0, jnp.where(at == chip ^ 1, 1, jnp.where(at == near_chip, 2, 4) + ends)
        )
        return array, page % held, holder % 2 == core

    array_c, slot_c, line_c = locate(chip_tables)
    array_p, slot_p, line_p = locate(peer_tables)
    j = jnp.arange(count, dtype=jnp.int32)
    where_core = jnp.stack(
        [jnp.concatenate([array_c[1], array_p[1]]), jnp.concatenate([slot_c[1], slot_p[1]])]
    )
    lines = 6
    where_peer = jnp.stack(
        [jnp.where(line_p[0], array_p[0], lines), jnp.where(line_p[0], slot_p[0], count + j)]
    )
    home = chip_tables[0] // per_rep == rep
    where_own = jnp.stack(
        [
            jnp.where(home, jnp.where(line_c[0], array_c[0], lines), lines + 1),
            jnp.where(home & line_c[0], slot_c[0], j),
        ]
    )

    middle = both_cores([(1, 2), (2, 1)])
    outward = both_cores([(1, 0), (2, 3)])
    k_near = lax.ppermute(kn, "dp", outward)
    v_near = lax.ppermute(vn, "dp", outward)
    k_far = lax.ppermute(kf, "dp", middle)
    v_far = lax.ppermute(vf, "dp", middle)
    k_end = lax.ppermute(k_far, "dp", outward)
    v_end = lax.ppermute(v_far, "dp", outward)
    k_near, v_near, k_end, v_end, kv_own, where_core = lax.optimization_barrier(
        (k_near, v_near, k_end, v_end, kv_own, where_core)
    )
    k_line = [k_pages, kf, kn, k_near, k_far, k_end]
    v_line = [v_pages, vf, vn, v_near, v_far, v_end]
    k_given = lax.ppermute(collect(where_core, k_line, "pick_core"), "dp", cores)
    v_given = lax.ppermute(collect(where_core, v_line, "pick_core"), "dp", cores)
    k_given, v_given = lax.optimization_barrier((k_given, v_given))
    k_came = lax.ppermute(collect(where_peer, k_line + [k_given], "pick_rep"), "rep", swap)
    v_sent = collect(where_peer, v_line + [v_given], "pick_rep")
    v_sent, normed = lax.optimization_barrier((v_sent, normed))
    v_came = lax.ppermute(v_sent, "rep", swap)
    qb, wa = project_other(normed, wq_other, cos, sin, w_out, head_size)
    k_came, qb, kv_peer, wo_piece = lax.optimization_barrier((k_came, qb, kv_peer, wo_piece))
    wo_other = lax.all_gather(wo_piece, "dp", axis=0, tiled=True, axis_index_groups=chips)
    k_mine = collect(where_own, k_line + [k_given, k_came], "pick_own")
    k_peer = lax.ppermute(k_mine, "tensor", swap)
    v_mine = collect(where_own, v_line + [v_given, v_came], "pick_own")
    v_peer = lax.ppermute(v_mine, "tensor", swap)

    info = jnp.stack([part, lengths[0]]).astype(jnp.int32)
    probs = weigh(info, qa, qb, k_mine, k_peer, kv_own, kv_peer)
    return mix_and_out(info, probs, v_mine, v_peer, kv_own, kv_peer, wa, wo_other)[None]


def rotate_pairs(values, positions, columns_from, head_size):
    rows, cols = values.shape
    column = columns_from + jnp.arange(cols // 2, dtype=jnp.int32) * 2
    within = (column % head_size).astype(jnp.float32)
    inv_freq = jnp.exp(within * (-math.log(10000.0) / head_size))
    angle = positions[:, None] * inv_freq[None, :]
    cosine = jnp.cos(angle)
    sine = jnp.sin(angle)
    pairs = values.reshape(rows, cols // 2, 2)
    first = pairs[:, :, 0]
    second = pairs[:, :, 1]
    turned = jnp.stack([first * cosine - second * sine, first * sine + second * cosine], axis=-1)
    return turned.reshape(rows, cols)


def attend(query, keys, values, first_row, heads, head_size, window):
    rows = query.shape[0]
    count = keys.shape[0]
    q_heads = query.reshape(rows, heads, head_size)
    scores = jnp.einsum("rhd,kd->hrk", q_heads, keys, preferred_element_type=jnp.float32) * (
        1.0 / math.sqrt(head_size)
    )
    row_ids = first_row + jnp.arange(rows, dtype=jnp.int32)
    key_ids = jnp.arange(count, dtype=jnp.int32)
    seen = (key_ids[None, :] >= row_ids[:, None] + 1) & (
        key_ids[None, :] <= row_ids[:, None] + window
    )
    scores = jnp.where(seen[None, :, :], scores, -1e30)
    top = jnp.max(scores, axis=-1, keepdims=True)
    expd = jnp.exp(scores - top)
    total = jnp.sum(expd, axis=-1, keepdims=True)
    probs = (expd / total).astype(jnp.bfloat16)
    mixed = jnp.einsum("hrk,kd->rhd", probs, values, preferred_element_type=jnp.float32)
    return mixed.reshape(rows, heads * head_size).astype(jnp.bfloat16)


def shards(tokens, norm_gain, w_query, w_keyval, w_out, kv_pages, page_table, lengths, starts):
    width = tokens.shape[2]
    head_size = w_keyval.shape[1] // 2
    heads = width // head_size
    part = lax.axis_index("tensor")
    local_rows = tokens.shape[1]
    q_cols = w_query.shape[1]
    start = starts[0]
    length = lengths[0]
    xf = tokens[0].astype(jnp.float32)
    scale = lax.rsqrt(jnp.mean(xf * xf, axis=-1, keepdims=True) + 1e-06)
    normed = (xf * scale * norm_gain).astype(jnp.bfloat16)
    piece = lax.all_gather(normed, "tensor", axis=0, tiled=True)
    positions = (start + jnp.arange(piece.shape[0], dtype=jnp.int32)).astype(jnp.float32)
    query = rotate_pairs(
        jnp.dot(piece, w_query, preferred_element_type=jnp.float32),
        positions,
        part * q_cols,
        head_size,
    )
    keyval = jnp.dot(piece, w_keyval, preferred_element_type=jnp.float32)
    new_keys = rotate_pairs(keyval[:, :head_size], positions, 0, head_size)
    projected = jnp.concatenate([query, new_keys, keyval[:, head_size:]], axis=1).astype(
        jnp.bfloat16
    )
    query_cols = projected[:, :q_cols]
    keys_new = projected[:, q_cols : q_cols + head_size]
    values_new = projected[:, q_cols + head_size :]
    query = lax.all_to_all(query_cols, "tensor", split_axis=0, concat_axis=1, tiled=True)
    table = page_table[0]
    piece = lax.all_gather(kv_pages, ("rep", "dp"), axis=0, tiled=True)
    ident = jnp.arange(piece.shape[0], dtype=jnp.int32)
    onehot = (table[:, None] == ident[None, :]).astype(jnp.bfloat16)
    picked = jnp.einsum("cn,nrk->crk", onehot, piece, preferred_element_type=jnp.float32)
    window_pages = lax.all_gather(picked.astype(jnp.bfloat16), "tensor", axis=1, tiled=True)
    cached = window_pages.reshape(-1, 2 * head_size)
    window = cached.shape[0]
    keys = jnp.concatenate([cached[:, :head_size], keys_new], axis=0)
    values = jnp.concatenate([cached[:, head_size:], values_new], axis=0)
    mixed = attend(query, keys, values, part * local_rows, heads, head_size, window)
    mixed_cols = lax.all_to_all(mixed, "tensor", split_axis=1, concat_axis=0, tiled=True)
    summed = lax.psum_scatter(
        jnp.dot(mixed_cols, w_out, preferred_element_type=jnp.float32).astype(jnp.bfloat16),
        "tensor",
        scatter_dimension=0,
        tiled=True,
    ).astype(jnp.float32)
    live = part * local_rows + jnp.arange(local_rows, dtype=jnp.int32) < length
    return jnp.where(live[:, None], summed, 0.0).astype(jnp.bfloat16)[None]


def solution(mesh):
    placed = (
        P(("rep", "dp"), "tensor", None),
        P(),
        P(None, "tensor"),
        P(),
        P("tensor", None),
        P(("rep", "dp"), "tensor", None),
        P(("rep", "dp"), None),
        P(("rep", "dp")),
        P(("rep", "dp")),
    )
    line = mesh.shape["tensor"] == 2 and mesh.shape["rep"] == 2 and mesh.shape["dp"] == 8
    body = pair_shards if line else shards
    return jax.shard_map(
        body,
        mesh=mesh,
        in_specs=placed,
        out_specs=P(("rep", "dp"), "tensor", None),
        check_vma=False,
    )
```

```python
import functools
import math

import jax
import jax.numpy as jnp
from jax import lax
from jax.experimental import pallas as pl
from jax.experimental.pallas import tpu as pltpu
from jax.sharding import PartitionSpec as P

BF16 = jnp.bfloat16
F32 = jnp.float32
MASKED = -1e30
ANY = pl.ANY


def spec(space):
    return pl.BlockSpec(memory_space=space)


def rotation_tables(first, rows, step, head_size):
    column = jnp.arange(head_size, dtype=jnp.int32)
    within = (column // 2 * 2).astype(F32)
    inv_freq = jnp.exp(within * (-math.log(10000.0) / head_size))
    sign = jnp.where(column % 2 == 0, -1.0, 1.0).astype(F32)
    coarse = (first + step * jnp.arange(rows // step, dtype=jnp.int32)).astype(F32)
    fine = jnp.arange(step, dtype=jnp.int32).astype(F32)
    at = jnp.concatenate([coarse, fine])
    angle = at[:, None] * inv_freq[None, :]
    return jnp.cos(angle), jnp.sin(angle) * sign[None, :]


def fill_rotation(cos_t, sin_t, cos_s, sin_s, step):
    blocks = cos_s.shape[0] // step
    cf = cos_t[blocks:, :]
    sf = sin_t[blocks:, :]
    for u in range(blocks):
        cu = cos_t[u : u + 1, :]
        su = sin_t[u : u + 1, :]
        cos_s[u * step : (u + 1) * step, :] = cu * cf - su * sf
        sin_s[u * step : (u + 1) * step, :] = su * cf + cu * sf


def rotate(v, cos, sin, even):
    width = v.shape[1]
    swapped = jnp.where(even, pltpu.roll(v, width - 1, 1), pltpu.roll(v, 1, 1))
    return v * cos + swapped * sin


def score_factor(head_size):
    return math.log2(math.e) / math.sqrt(head_size)


def project_kernel(head_size, step, factor, tok, gain, wq, wkv, cos_t, sin_t, normed, q, kv, cos, sin):
    rows = tok.shape[0]
    tile = min(256, rows)
    fill_rotation(cos_t, sin_t, cos, sin, step)
    even = lax.broadcasted_iota(jnp.int32, (tile, head_size), 1) % 2 == 0
    for i in range(rows // tile):
        at = pl.ds(i * tile, tile)
        xf = tok[at, :].astype(F32)
        scale = lax.rsqrt(jnp.mean(xf * xf, axis=-1, keepdims=True) + 1e-06)
        nb = (xf * scale * gain[...]).astype(BF16)
        normed[at, :] = nb
        c = cos[at, :]
        s = sin[at, :]
        both = jnp.dot(nb, wkv[...], preferred_element_type=F32)
        kv[at, :head_size] = rotate(both[:, :head_size], c, s, even).astype(BF16)
        kv[at, head_size:] = both[:, head_size:].astype(BF16)
        for h in range(wq.shape[1] // head_size):
            cols = slice(h * head_size, (h + 1) * head_size)
            part = jnp.dot(nb, wq[:, cols], preferred_element_type=F32)
            q[at, cols] = (rotate(part, c, s, even) * factor).astype(BF16)


def project(tok, gain, wq, wkv, cos_t, sin_t, head_size, step):
    rows, width = tok.shape
    qc, kc = wq.shape[1], wkv.shape[1]
    return pl.pallas_call(
        functools.partial(project_kernel, head_size, step, score_factor(head_size)),
        out_shape=(
            jax.ShapeDtypeStruct((rows, width), BF16),
            jax.ShapeDtypeStruct((rows, qc), BF16),
            jax.ShapeDtypeStruct((rows, kc), BF16),
            jax.ShapeDtypeStruct((rows, head_size), F32),
            jax.ShapeDtypeStruct((rows, head_size), F32),
        ),
        in_specs=[spec(pltpu.VMEM)] * 6,
        out_specs=[spec(pltpu.VMEM)] * 5,
        compiler_params=pltpu.CompilerParams(vmem_limit_bytes=20 * 2**20),
        cost_estimate=pl.CostEstimate(
            flops=2 * rows * width * (qc + kc), bytes_accessed=10 * 2**20, transcendentals=0
        ),
        name="project_own",
    )(tok, gain.reshape(1, width), wq, wkv, cos_t, sin_t)


def other_kernel(head_size, factor, order, normed, w0, w1, w2, w3, cos, sin, q):
    rows = normed.shape[0]
    tile = min(256, rows)
    deep = w0.shape[0]
    even = lax.broadcasted_iota(jnp.int32, (tile, head_size), 1) % 2 == 0
    for i in range(rows // tile):
        at = pl.ds(i * tile, tile)
        c = cos[at, :]
        s = sin[at, :]
        for h in range(q.shape[1] // head_size):
            cols = slice(h * head_size, (h + 1) * head_size)
            total = None
            for n, w in enumerate((w0, w1, w2, w3)):
                x = normed[at, pl.ds(pl.multiple_of(order[n] * deep, 128), deep)]
                part = jnp.dot(x, w[:, cols], preferred_element_type=F32)
                total = part if total is None else total + part
            q[at, cols] = (rotate(total, c, s, even) * factor).astype(BF16)


def project_other(normed, pieces, order, cos, sin, head_size):
    rows, width = normed.shape
    qc = pieces[0].shape[1]
    return pl.pallas_call(
        functools.partial(other_kernel, head_size, score_factor(head_size)),
        out_shape=jax.ShapeDtypeStruct((rows, qc), BF16),
        in_specs=[spec(pltpu.SMEM)] + [spec(pltpu.VMEM)] * 7,
        out_specs=spec(pltpu.VMEM),
        compiler_params=pltpu.CompilerParams(vmem_limit_bytes=20 * 2**20),
        cost_estimate=pl.CostEstimate(
            flops=2 * rows * width * qc, bytes_accessed=6 * 2**20, transcendentals=0
        ),
        name="project_other",
    )(order, normed, *pieces, cos, sin)


def pick_kernel(idx, pool, out, sem):
    copies = [
        pltpu.make_async_copy(pool.at[idx[j]], out.at[j], sem.at[j]) for j in range(out.shape[0])
    ]
    for c in copies:
        c.start()
    for c in copies:
        c.wait()


def pick(pool, idx):
    count = idx.shape[0]
    return pl.pallas_call(
        pick_kernel,
        out_shape=jax.ShapeDtypeStruct((count,) + pool.shape[1:], pool.dtype),
        in_specs=[spec(pltpu.SMEM), spec(ANY)],
        out_specs=spec(pltpu.VMEM),
        scratch_shapes=[pltpu.SemaphoreType.DMA((count,))],
        compiler_params=pltpu.CompilerParams(vmem_limit_bytes=60 * 2**20),
        cost_estimate=pl.CostEstimate(flops=0, bytes_accessed=2**20, transcendentals=0),
        name="pick_pages",
    )(idx, pool)


def choose_kernel(home, idx, pool, came, out, sem):
    count = out.shape[0]

    @pl.when(home[0] == 1)
    def _():
        for j in range(count):
            pltpu.make_async_copy(pool.at[idx[j]], out.at[j], sem.at[j]).start()

    @pl.when(home[0] == 0)
    def _():
        for j in range(count):
            pltpu.make_async_copy(came.at[j], out.at[j], sem.at[j]).start()

    for j in range(count):
        pltpu.make_async_copy(came.at[j], out.at[j], sem.at[j]).wait()


def choose(pool, idx, home, came):
    count = idx.shape[0]
    return pl.pallas_call(
        choose_kernel,
        out_shape=jax.ShapeDtypeStruct(came.shape, came.dtype),
        in_specs=[spec(pltpu.SMEM), spec(pltpu.SMEM), spec(ANY), spec(pltpu.VMEM)],
        out_specs=spec(pltpu.VMEM),
        scratch_shapes=[pltpu.SemaphoreType.DMA((count,))],
        compiler_params=pltpu.CompilerParams(vmem_limit_bytes=60 * 2**20),
        cost_estimate=pl.CostEstimate(flops=0, bytes_accessed=2**20, transcendentals=0),
        name="choose_pages",
    )(home, idx, pool, came)


def attend_kernel(
    head_size,
    info,
    qa_hbm,
    qb_hbm,
    k_mine,
    k_peer,
    v_mine,
    v_peer,
    kv_own,
    kv_peer,
    woa,
    wob0,
    wob1,
    out_hbm,
    qa,
    qb,
    keys,
    vals,
    wa,
    wb,
    mix,
    out,
    ksem,
    vsem,
    wsem,
    osem,
):
    part = info[0]
    length = info[1]
    rows, half = qa.shape
    pages, prow, _ = k_mine.shape
    page = 2 * prow
    width = out.shape[1]
    core = info[2]
    deep = wob0.shape[0]
    nheads = half // head_size
    window = pages * page

    def start(mine, peer, lo, dst, sem):
        cols = pl.ds(lo, head_size)
        for case in (0, 1):

            @pl.when(part == case)
            def _():
                skip = case * rows // page
                for u in range(skip, pages):
                    for src, side in ((mine, case), (peer, 1 - case)):
                        to = pl.ds((u - skip) * page + side * prow, prow)
                        pltpu.make_async_copy(src.at[u], dst.at[to, :], sem).start()
                if case == 1:
                    to = pl.ds(window - rows, rows)
                    pltpu.make_async_copy(kv_peer.at[:, cols], dst.at[to, :], sem).start()
                to = pl.ds(window, rows)
                pltpu.make_async_copy(kv_own.at[:, cols], dst.at[to, :], sem).start()

    def finish(dst, sem):
        pltpu.make_async_copy(dst, dst, sem).wait()

    queries = [
        pltpu.make_async_copy(qa_hbm, qa, wsem.at[3]),
        pltpu.make_async_copy(qb_hbm, qb, wsem.at[4]),
    ]
    queries[0].start()
    start(k_mine, k_peer, 0, keys, ksem)
    queries[1].start()
    start(v_mine, v_peer, head_size, vals, vsem)
    weights = [
        pltpu.make_async_copy(woa, wa, wsem.at[0]),
        pltpu.make_async_copy(wob0, wb.at[pl.ds(core * deep, deep), :], wsem.at[1]),
        pltpu.make_async_copy(wob1, wb.at[pl.ds((1 - core) * deep, deep), :], wsem.at[2]),
    ]
    for c in weights:
        c.start()

    tile = min(256, rows)
    span = window + tile
    row_id = lax.broadcasted_iota(jnp.int32, (tile, tile), 0)
    col_id = lax.broadcasted_iota(jnp.int32, (tile, tile), 1)
    first_seen = col_id >= row_id + 1
    last_seen = col_id <= row_id
    queries[0].wait()
    finish(keys, ksem)
    stores = []
    for i in range(rows // tile):
        at = pl.ds(i * tile, tile)
        for n, q in enumerate((qa, qb)):
            for h in range(nheads):
                cols = slice(h * head_size, (h + 1) * head_size)
                kk = keys[pl.ds(i * tile, span), :]
                s = lax.dot_general(
                    q[at, cols], kk, (((1,), (1,)), ((), ())), preferred_element_type=F32
                )
                s = jnp.concatenate(
                    [
                        jnp.where(first_seen, s[:, :tile], MASKED),
                        s[:, tile : span - tile],
                        jnp.where(last_seen, s[:, span - tile :], MASKED),
                    ],
                    axis=1,
                )
                top = jnp.max(s, axis=-1, keepdims=True)
                e = jnp.exp2(s - top)
                total = jnp.sum(e, axis=-1, keepdims=True)
                if i == 0 and n == 0 and h == 0:
                    finish(vals, vsem)
                    queries[1].wait()
                vv = vals[pl.ds(i * tile, span), :]
                m = jnp.dot(e.astype(BF16), vv, preferred_element_type=F32)
                mix[n, at, cols] = (m / total).astype(BF16)
        if i == 0:
            for c in weights:
                c.wait()
        row = part * rows + i * tile + lax.broadcasted_iota(jnp.int32, (tile, 1), 0)
        live = row < length
        for j in range(width // 512):
            cols = slice(j * 512, (j + 1) * 512)
            a = jnp.dot(mix[0, at, :], wa[:, cols], preferred_element_type=F32)
            b = jnp.dot(mix[1, at, :], wb[:, cols], preferred_element_type=F32)
            both = a.astype(BF16).astype(F32) + b.astype(BF16).astype(F32)
            out[at, cols] = jnp.where(live, both, 0.0).astype(BF16)
        stores.append(pltpu.make_async_copy(out.at[at, :], out_hbm.at[at, :], osem.at[i]))
        stores[i].start()
    for c in stores:
        c.wait()


def attend_pages(info, qa, qb, k_mine, k_peer, v_mine, v_peer, kv_own, kv_peer, woa, wobs):
    rows, half = qa.shape
    width = woa.shape[1]
    head_size = k_mine.shape[2]
    window = k_mine.shape[0] * k_mine.shape[1] * 2
    return pl.pallas_call(
        functools.partial(attend_kernel, head_size),
        out_shape=jax.ShapeDtypeStruct((rows, width), BF16),
        in_specs=[spec(pltpu.SMEM)]
        + [spec(ANY)] * 2
        + [spec(pltpu.VMEM)] * 4
        + [spec(ANY)] * 5,
        out_specs=spec(ANY),
        scratch_shapes=[
            pltpu.VMEM((rows, half), BF16),
            pltpu.VMEM((rows, half), BF16),
            pltpu.VMEM((window + rows, head_size), BF16),
            pltpu.VMEM((window + rows, head_size), BF16),
            pltpu.VMEM(woa.shape, BF16),
            pltpu.VMEM(woa.shape, BF16),
            pltpu.VMEM((2, rows, half), BF16),
            pltpu.VMEM((rows, width), BF16),
            pltpu.SemaphoreType.DMA,
            pltpu.SemaphoreType.DMA,
            pltpu.SemaphoreType.DMA((5,)),
            pltpu.SemaphoreType.DMA((rows // min(256, rows),)),
        ],
        compiler_params=pltpu.CompilerParams(vmem_limit_bytes=56 * 2**20),
        cost_estimate=pl.CostEstimate(
            flops=4 * rows * 2 * half * (window + 256) + 4 * rows * half * width,
            bytes_accessed=12 * 2**20,
            transcendentals=rows * 6 * (window + 256),
        ),
        name="attend_and_out",
    )(info, qa, qb, k_mine, k_peer, v_mine, v_peer, kv_own, kv_peer, woa, *wobs)


def pair_shards(tokens, norm_gain, w_query, w_keyval, w_out, kv_pages, page_table, lengths, starts):
    head_size = w_keyval.shape[1] // 2
    part = lax.axis_index("tensor")
    rep = lax.axis_index("rep")
    dp = lax.axis_index("dp")
    ndp = lax.axis_size("dp")
    core = dp % 2
    rows = tokens.shape[1]
    swap = [(0, 1), (1, 0)]
    cores = [(i, i ^ 1) for i in range(ndp)]

    k_pool = lax.all_gather(kv_pages[:, :, :head_size], "dp", axis=0, tiled=True)
    v_pool = lax.all_gather(kv_pages[:, :, head_size:], "dp", axis=0, tiled=True)

    def peer_rows(w, at, parts):
        deep = w.shape[0] // parts
        return lax.ppermute(lax.dynamic_slice_in_dim(w, at * deep, deep, 0), "tensor", swap)

    a = peer_rows(w_query, rep * 2 + core, 4)
    a, w_out_late = lax.optimization_barrier((a, w_out))
    b = lax.ppermute(a, "rep", swap)
    wq_pieces = (a, b, lax.ppermute(a, "dp", cores), lax.ppermute(b, "dp", cores))
    order = jnp.stack(
        [rep * 2 + core, (1 - rep) * 2 + core, rep * 2 + 1 - core, (1 - rep) * 2 + 1 - core]
    ).astype(jnp.int32)
    c = peer_rows(w_out_late, core, 2)
    wo_pieces = (c, lax.ppermute(c, "dp", cores))

    step = 32
    cos_t, sin_t = rotation_tables(starts[0] + part * rows, rows, step, head_size)
    normed, qa, kv_own, cos, sin = project(
        tokens[0], norm_gain, w_query, w_keyval, cos_t, sin_t, head_size, step
    )
    kv_peer = lax.ppermute(kv_own, "tensor", swap)
    qb = project_other(normed, wq_pieces, order, cos, sin, head_size)

    table = page_table[0]
    peer_table = lax.ppermute(table, "rep", swap)
    per_rep = kv_pages.shape[0] * ndp
    home = (table[:1] // per_rep == rep).astype(jnp.int32)
    own_at, peer_at = table % per_rep, peer_table % per_rep

    wo_pieces, qb, kv_peer, k_pool, own_at, peer_at = lax.optimization_barrier(
        (wo_pieces, qb, kv_peer, k_pool, own_at, peer_at)
    )
    k_came = lax.ppermute(pick(k_pool, peer_at), "rep", swap)
    v_came = lax.ppermute(pick(v_pool, peer_at), "rep", swap)
    k_mine = choose(k_pool, own_at, home, k_came)
    k_peer = lax.ppermute(k_mine, "tensor", swap)
    v_mine = choose(v_pool, own_at, home, v_came)
    v_peer = lax.ppermute(v_mine, "tensor", swap)

    info = jnp.stack([part, lengths[0], core]).astype(jnp.int32)
    return attend_pages(
        info, qa, qb, k_mine, k_peer, v_mine, v_peer, kv_own, kv_peer, w_out, wo_pieces
    )[None]


def rotate_pairs(values, positions, columns_from, head_size):
    rows, cols = values.shape
    column = columns_from + jnp.arange(cols // 2, dtype=jnp.int32) * 2
    within = (column % head_size).astype(jnp.float32)
    inv_freq = jnp.exp(within * (-math.log(10000.0) / head_size))
    angle = positions[:, None] * inv_freq[None, :]
    cosine = jnp.cos(angle)
    sine = jnp.sin(angle)
    pairs = values.reshape(rows, cols // 2, 2)
    first = pairs[:, :, 0]
    second = pairs[:, :, 1]
    turned = jnp.stack([first * cosine - second * sine, first * sine + second * cosine], axis=-1)
    return turned.reshape(rows, cols)


def attend(query, keys, values, first_row, heads, head_size, window):
    rows = query.shape[0]
    count = keys.shape[0]
    q_heads = query.reshape(rows, heads, head_size)
    scores = jnp.einsum("rhd,kd->hrk", q_heads, keys, preferred_element_type=jnp.float32) * (
        1.0 / math.sqrt(head_size)
    )
    row_ids = first_row + jnp.arange(rows, dtype=jnp.int32)
    key_ids = jnp.arange(count, dtype=jnp.int32)
    seen = (key_ids[None, :] >= row_ids[:, None] + 1) & (
        key_ids[None, :] <= row_ids[:, None] + window
    )
    scores = jnp.where(seen[None, :, :], scores, -1e30)
    top = jnp.max(scores, axis=-1, keepdims=True)
    expd = jnp.exp(scores - top)
    total = jnp.sum(expd, axis=-1, keepdims=True)
    probs = (expd / total).astype(jnp.bfloat16)
    mixed = jnp.einsum("hrk,kd->rhd", probs, values, preferred_element_type=jnp.float32)
    return mixed.reshape(rows, heads * head_size).astype(jnp.bfloat16)


def shards(tokens, norm_gain, w_query, w_keyval, w_out, kv_pages, page_table, lengths, starts):
    width = tokens.shape[2]
    head_size = w_keyval.shape[1] // 2
    heads = width // head_size
    part = lax.axis_index("tensor")
    local_rows = tokens.shape[1]
    q_cols = w_query.shape[1]
    start = starts[0]
    length = lengths[0]
    xf = tokens[0].astype(jnp.float32)
    scale = lax.rsqrt(jnp.mean(xf * xf, axis=-1, keepdims=True) + 1e-06)
    normed = (xf * scale * norm_gain).astype(jnp.bfloat16)
    piece = lax.all_gather(normed, "tensor", axis=0, tiled=True)
    positions = (start + jnp.arange(piece.shape[0], dtype=jnp.int32)).astype(jnp.float32)
    query = rotate_pairs(
        jnp.dot(piece, w_query, preferred_element_type=jnp.float32),
        positions,
        part * q_cols,
        head_size,
    )
    keyval = jnp.dot(piece, w_keyval, preferred_element_type=jnp.float32)
    new_keys = rotate_pairs(keyval[:, :head_size], positions, 0, head_size)
    projected = jnp.concatenate([query, new_keys, keyval[:, head_size:]], axis=1).astype(
        jnp.bfloat16
    )
    query_cols = projected[:, :q_cols]
    keys_new = projected[:, q_cols : q_cols + head_size]
    values_new = projected[:, q_cols + head_size :]
    query = lax.all_to_all(query_cols, "tensor", split_axis=0, concat_axis=1, tiled=True)
    table = page_table[0]
    piece = lax.all_gather(kv_pages, ("rep", "dp"), axis=0, tiled=True)
    ident = jnp.arange(piece.shape[0], dtype=jnp.int32)
    onehot = (table[:, None] == ident[None, :]).astype(jnp.bfloat16)
    picked = jnp.einsum("cn,nrk->crk", onehot, piece, preferred_element_type=jnp.float32)
    window_pages = lax.all_gather(picked.astype(jnp.bfloat16), "tensor", axis=1, tiled=True)
    cached = window_pages.reshape(-1, 2 * head_size)
    window = cached.shape[0]
    keys = jnp.concatenate([cached[:, :head_size], keys_new], axis=0)
    values = jnp.concatenate([cached[:, head_size:], values_new], axis=0)
    mixed = attend(query, keys, values, part * local_rows, heads, head_size, window)
    mixed_cols = lax.all_to_all(mixed, "tensor", split_axis=1, concat_axis=0, tiled=True)
    summed = lax.psum_scatter(
        jnp.dot(mixed_cols, w_out, preferred_element_type=jnp.float32).astype(jnp.bfloat16),
        "tensor",
        scatter_dimension=0,
        tiled=True,
    ).astype(jnp.float32)
    live = part * local_rows + jnp.arange(local_rows, dtype=jnp.int32) < length
    return jnp.where(live[:, None], summed, 0.0).astype(jnp.bfloat16)[None]


def solution(mesh):
    placed = (
        P(("rep", "dp"), "tensor", None),
        P(),
        P(None, "tensor"),
        P(),
        P("tensor", None),
        P(("rep", "dp"), "tensor", None),
        P(("rep", "dp"), None),
        P(("rep", "dp")),
        P(("rep", "dp")),
    )
    pair = mesh.shape["tensor"] == 2 and mesh.shape["rep"] == 2 and mesh.shape["dp"] % 2 == 0
    body = pair_shards if pair else shards
    return jax.shard_map(
        body,
        mesh=mesh,
        in_specs=placed,
        out_specs=P(("rep", "dp"), "tensor", None),
        check_vma=False,
    )
```

```python
import functools
import math

import jax
import jax.numpy as jnp
from jax import lax
from jax.experimental import pallas as pl
from jax.experimental.pallas import tpu as pltpu
from jax.sharding import PartitionSpec as P

BF16 = jnp.bfloat16
F32 = jnp.float32
MASKED = -1e30
ANY = pl.ANY


def spec(space):
    return pl.BlockSpec(memory_space=space)


def rotation_tables(first, rows, step, head_size):
    column = jnp.arange(head_size, dtype=jnp.int32)
    within = (column // 2 * 2).astype(F32)
    inv_freq = jnp.exp(within * (-math.log(10000.0) / head_size))
    sign = jnp.where(column % 2 == 0, -1.0, 1.0).astype(F32)
    coarse = (first + step * jnp.arange(rows // step, dtype=jnp.int32)).astype(F32)
    fine = jnp.arange(step, dtype=jnp.int32).astype(F32)
    at = jnp.concatenate([coarse, fine])
    angle = at[:, None] * inv_freq[None, :]
    return jnp.cos(angle), jnp.sin(angle) * sign[None, :]


def fill_rotation(cos_t, sin_t, cos_s, sin_s, step):
    blocks = cos_s.shape[0] // step
    cf = cos_t[blocks:, :]
    sf = sin_t[blocks:, :]
    for u in range(blocks):
        cu = cos_t[u : u + 1, :]
        su = sin_t[u : u + 1, :]
        cos_s[u * step : (u + 1) * step, :] = cu * cf - su * sf
        sin_s[u * step : (u + 1) * step, :] = su * cf + cu * sf


def rotate(v, cos, sin, even):
    width = v.shape[1]
    swapped = jnp.where(even, pltpu.roll(v, width - 1, 1), pltpu.roll(v, 1, 1))
    return v * cos + swapped * sin


def score_factor(head_size):
    return math.log2(math.e) / math.sqrt(head_size)


def project_kernel(head_size, step, factor, tok, gain, wq, wkv, cos_t, sin_t, normed, q, kv, cos, sin):
    rows = tok.shape[0]
    tile = min(256, rows)
    fill_rotation(cos_t, sin_t, cos, sin, step)
    even = lax.broadcasted_iota(jnp.int32, (tile, head_size), 1) % 2 == 0
    for i in range(rows // tile):
        at = pl.ds(i * tile, tile)
        xf = tok[at, :].astype(F32)
        scale = lax.rsqrt(jnp.mean(xf * xf, axis=-1, keepdims=True) + 1e-06)
        nb = (xf * scale * gain[...]).astype(BF16)
        normed[at, :] = nb
        c = cos[at, :]
        s = sin[at, :]
        both = jnp.dot(nb, wkv[...], preferred_element_type=F32)
        kv[at, :head_size] = rotate(both[:, :head_size], c, s, even).astype(BF16)
        kv[at, head_size:] = both[:, head_size:].astype(BF16)
        for h in range(wq.shape[1] // head_size):
            cols = slice(h * head_size, (h + 1) * head_size)
            part = jnp.dot(nb, wq[:, cols], preferred_element_type=F32)
            q[at, cols] = (rotate(part, c, s, even) * factor).astype(BF16)


def project(tok, gain, wq, wkv, cos_t, sin_t, head_size, step):
    rows, width = tok.shape
    qc, kc = wq.shape[1], wkv.shape[1]
    return pl.pallas_call(
        functools.partial(project_kernel, head_size, step, score_factor(head_size)),
        out_shape=(
            jax.ShapeDtypeStruct((rows, width), BF16),
            jax.ShapeDtypeStruct((rows, qc), BF16),
            jax.ShapeDtypeStruct((rows, kc), BF16),
            jax.ShapeDtypeStruct((rows, head_size), F32),
            jax.ShapeDtypeStruct((rows, head_size), F32),
        ),
        in_specs=[spec(pltpu.VMEM)] * 6,
        out_specs=[spec(pltpu.VMEM)] * 5,
        compiler_params=pltpu.CompilerParams(vmem_limit_bytes=20 * 2**20),
        cost_estimate=pl.CostEstimate(
            flops=2 * rows * width * (qc + kc), bytes_accessed=10 * 2**20, transcendentals=0
        ),
        name="project_own",
    )(tok, gain.reshape(1, width), wq, wkv, cos_t, sin_t)


def other_kernel(head_size, factor, order, normed, w0, w1, w2, w3, cos, sin, q):
    rows = normed.shape[0]
    tile = min(256, rows)
    deep = w0.shape[0]
    even = lax.broadcasted_iota(jnp.int32, (tile, head_size), 1) % 2 == 0
    for i in range(rows // tile):
        at = pl.ds(i * tile, tile)
        c = cos[at, :]
        s = sin[at, :]
        for h in range(q.shape[1] // head_size):
            cols = slice(h * head_size, (h + 1) * head_size)
            total = None
            for n, w in enumerate((w0, w1, w2, w3)):
                x = normed[at, pl.ds(pl.multiple_of(order[n] * deep, 128), deep)]
                part = jnp.dot(x, w[:, cols], preferred_element_type=F32)
                total = part if total is None else total + part
            q[at, cols] = (rotate(total, c, s, even) * factor).astype(BF16)


def project_other(normed, pieces, order, cos, sin, head_size):
    rows, width = normed.shape
    qc = pieces[0].shape[1]
    return pl.pallas_call(
        functools.partial(other_kernel, head_size, score_factor(head_size)),
        out_shape=jax.ShapeDtypeStruct((rows, qc), BF16),
        in_specs=[spec(pltpu.SMEM)] + [spec(pltpu.VMEM)] * 7,
        out_specs=spec(pltpu.VMEM),
        compiler_params=pltpu.CompilerParams(vmem_limit_bytes=20 * 2**20),
        cost_estimate=pl.CostEstimate(
            flops=2 * rows * width * qc, bytes_accessed=6 * 2**20, transcendentals=0
        ),
        name="project_other",
    )(order, normed, *pieces, cos, sin)


def pick_kernel(idx, pool, keys, vals, sem):
    count, _, head_size = keys.shape
    copies = []
    for n, out in enumerate((keys, vals)):
        cols = pl.ds(n * head_size, head_size)
        for j in range(count):
            page = pool.at[idx[j], :, cols]
            copies.append(pltpu.make_async_copy(page, out.at[j], sem.at[n * count + j]))
    for c in copies:
        c.start()
    for c in copies:
        c.wait()


def pick(pool, idx):
    count = idx.shape[0]
    half = jax.ShapeDtypeStruct((count, pool.shape[1], pool.shape[2] // 2), pool.dtype)
    return pl.pallas_call(
        pick_kernel,
        out_shape=(half, half),
        in_specs=[spec(pltpu.SMEM), spec(ANY)],
        out_specs=[spec(pltpu.VMEM)] * 2,
        scratch_shapes=[pltpu.SemaphoreType.DMA((2 * count,))],
        compiler_params=pltpu.CompilerParams(vmem_limit_bytes=60 * 2**20),
        cost_estimate=pl.CostEstimate(flops=0, bytes_accessed=2**20, transcendentals=0),
        name="pick_pages",
    )(idx, pool)


def attend_kernel(
    head_size,
    info,
    qa_hbm,
    qb_hbm,
    k_mine,
    k_peer,
    v_mine,
    v_peer,
    kv_own,
    kv_peer,
    woa,
    wob0,
    wob1,
    out_hbm,
    qa,
    qb,
    keys,
    vals,
    wa,
    wb,
    mix,
    out,
    ksem,
    vsem,
    wsem,
    osem,
):
    part = info[0]
    length = info[1]
    rows, half = qa.shape
    pages, prow, _ = k_mine.shape
    page = 2 * prow
    width = out.shape[1]
    core = info[2]
    deep = wob0.shape[0]
    nheads = half // head_size
    window = pages * page

    def start(mine, peer, lo, dst, sem):
        cols = pl.ds(lo, head_size)
        for case in (0, 1):

            @pl.when(part == case)
            def _():
                skip = case * rows // page
                for u in range(skip, pages):
                    for src, side in ((mine, case), (peer, 1 - case)):
                        to = pl.ds((u - skip) * page + side * prow, prow)
                        pltpu.make_async_copy(src.at[u], dst.at[to, :], sem).start()
                if case == 1:
                    to = pl.ds(window - rows, rows)
                    pltpu.make_async_copy(kv_peer.at[:, cols], dst.at[to, :], sem).start()
                to = pl.ds(window, rows)
                pltpu.make_async_copy(kv_own.at[:, cols], dst.at[to, :], sem).start()

    def finish(dst, sem):
        pltpu.make_async_copy(dst, dst, sem).wait()

    queries = [
        pltpu.make_async_copy(qa_hbm, qa, wsem.at[3]),
        pltpu.make_async_copy(qb_hbm, qb, wsem.at[4]),
    ]
    queries[0].start()
    start(k_mine, k_peer, 0, keys, ksem)
    queries[1].start()
    start(v_mine, v_peer, head_size, vals, vsem)
    weights = [
        pltpu.make_async_copy(woa, wa, wsem.at[0]),
        pltpu.make_async_copy(wob0, wb.at[pl.ds(core * deep, deep), :], wsem.at[1]),
        pltpu.make_async_copy(wob1, wb.at[pl.ds((1 - core) * deep, deep), :], wsem.at[2]),
    ]
    for c in weights:
        c.start()

    tile = min(256, rows)
    span = window + tile
    row_id = lax.broadcasted_iota(jnp.int32, (tile, tile), 0)
    col_id = lax.broadcasted_iota(jnp.int32, (tile, tile), 1)
    first_seen = col_id >= row_id + 1
    last_seen = col_id <= row_id
    queries[0].wait()
    finish(keys, ksem)
    stores = []
    for i in range(rows // tile):
        at = pl.ds(i * tile, tile)
        for n, q in enumerate((qa, qb)):
            for h in range(nheads):
                cols = slice(h * head_size, (h + 1) * head_size)
                kk = keys[pl.ds(i * tile, span), :]
                s = lax.dot_general(
                    q[at, cols], kk, (((1,), (1,)), ((), ())), preferred_element_type=F32
                )
                s = jnp.concatenate(
                    [
                        jnp.where(first_seen, s[:, :tile], MASKED),
                        s[:, tile : span - tile],
                        jnp.where(last_seen, s[:, span - tile :], MASKED),
                    ],
                    axis=1,
                )
                top = jnp.max(s, axis=-1, keepdims=True)
                e = jnp.exp2(s - top)
                total = jnp.sum(e, axis=-1, keepdims=True)
                if i == 0 and n == 0 and h == 0:
                    finish(vals, vsem)
                    queries[1].wait()
                vv = vals[pl.ds(i * tile, span), :]
                m = jnp.dot(e.astype(BF16), vv, preferred_element_type=F32)
                mix[n, at, cols] = (m / total).astype(BF16)
        if i == 0:
            for c in weights:
                c.wait()
        row = part * rows + i * tile + lax.broadcasted_iota(jnp.int32, (tile, 1), 0)
        live = row < length
        for j in range(width // 512):
            cols = slice(j * 512, (j + 1) * 512)
            a = jnp.dot(mix[0, at, :], wa[:, cols], preferred_element_type=F32)
            b = jnp.dot(mix[1, at, :], wb[:, cols], preferred_element_type=F32)
            both = a.astype(BF16).astype(F32) + b.astype(BF16).astype(F32)
            out[at, cols] = jnp.where(live, both, 0.0).astype(BF16)
        stores.append(pltpu.make_async_copy(out.at[at, :], out_hbm.at[at, :], osem.at[i]))
        stores[i].start()
    for c in stores:
        c.wait()


def attend_pages(info, qa, qb, k_mine, k_peer, v_mine, v_peer, kv_own, kv_peer, woa, wobs):
    rows, half = qa.shape
    width = woa.shape[1]
    head_size = k_mine.shape[2]
    window = k_mine.shape[0] * k_mine.shape[1] * 2
    return pl.pallas_call(
        functools.partial(attend_kernel, head_size),
        out_shape=jax.ShapeDtypeStruct((rows, width), BF16),
        in_specs=[spec(pltpu.SMEM)]
        + [spec(ANY)] * 2
        + [spec(pltpu.VMEM)] * 4
        + [spec(ANY)] * 5,
        out_specs=spec(ANY),
        scratch_shapes=[
            pltpu.VMEM((rows, half), BF16),
            pltpu.VMEM((rows, half), BF16),
            pltpu.VMEM((window + rows, head_size), BF16),
            pltpu.VMEM((window + rows, head_size), BF16),
            pltpu.VMEM(woa.shape, BF16),
            pltpu.VMEM(woa.shape, BF16),
            pltpu.VMEM((2, rows, half), BF16),
            pltpu.VMEM((rows, width), BF16),
            pltpu.SemaphoreType.DMA,
            pltpu.SemaphoreType.DMA,
            pltpu.SemaphoreType.DMA((5,)),
            pltpu.SemaphoreType.DMA((rows // min(256, rows),)),
        ],
        compiler_params=pltpu.CompilerParams(vmem_limit_bytes=56 * 2**20),
        cost_estimate=pl.CostEstimate(
            flops=4 * rows * 2 * half * (window + 256) + 4 * rows * half * width,
            bytes_accessed=12 * 2**20,
            transcendentals=rows * 6 * (window + 256),
        ),
        name="attend_and_out",
    )(info, qa, qb, k_mine, k_peer, v_mine, v_peer, kv_own, kv_peer, woa, *wobs)


def pair_shards(tokens, norm_gain, w_query, w_keyval, w_out, kv_pages, page_table, lengths, starts):
    head_size = w_keyval.shape[1] // 2
    part = lax.axis_index("tensor")
    rep = lax.axis_index("rep")
    dp = lax.axis_index("dp")
    ndp = lax.axis_size("dp")
    core = dp % 2
    rows = tokens.shape[1]
    swap = [(0, 1), (1, 0)]
    cores = [(i, i ^ 1) for i in range(ndp)]

    pool = lax.all_gather(kv_pages, "dp", axis=0, tiled=True)

    def peer_rows(w, at, parts):
        deep = w.shape[0] // parts
        return lax.ppermute(lax.dynamic_slice_in_dim(w, at * deep, deep, 0), "tensor", swap)

    step = 32
    cos_t, sin_t = rotation_tables(starts[0] + part * rows, rows, step, head_size)
    normed, qa, kv_own, cos, sin = project(
        tokens[0], norm_gain, w_query, w_keyval, cos_t, sin_t, head_size, step
    )

    a = peer_rows(w_query, rep * 2 + core, 4)
    a, kv_own, w_out_late, page_table = lax.optimization_barrier((a, kv_own, w_out, page_table))
    b = lax.ppermute(a, "rep", swap)
    c = peer_rows(w_out_late, core, 2)
    table = page_table[0]
    peer_table = lax.ppermute(table, "rep", swap)
    wq_pieces = (a, b, lax.ppermute(a, "dp", cores), lax.ppermute(b, "dp", cores))
    order = jnp.stack(
        [rep * 2 + core, (1 - rep) * 2 + core, rep * 2 + 1 - core, (1 - rep) * 2 + 1 - core]
    ).astype(jnp.int32)
    qb = project_other(normed, wq_pieces, order, cos, sin, head_size)
    c, qb, kv_own = lax.optimization_barrier((c, qb, kv_own))
    wo_pieces = (c, lax.ppermute(c, "dp", cores))
    kv_peer = lax.ppermute(kv_own, "tensor", swap)

    per_rep = kv_pages.shape[0] * ndp
    home = table[0] // per_rep == rep
    own_at, peer_at = table % per_rep, peer_table % per_rep
    wo_pieces, pool, own_at, peer_at = lax.optimization_barrier(
        (wo_pieces, pool, own_at, peer_at)
    )
    k_sent, v_sent = pick(pool, peer_at)
    k_came = lax.ppermute(k_sent, "rep", swap)
    v_came = lax.ppermute(v_sent, "rep", swap)
    k_held, v_held = pick(pool, own_at)
    k_came, kv_peer, k_held = lax.optimization_barrier((k_came, kv_peer, k_held))
    k_mine = jnp.where(home, k_held, k_came)
    k_peer = lax.ppermute(k_mine, "tensor", swap)
    v_mine = jnp.where(home, v_held, v_came)
    v_peer = lax.ppermute(v_mine, "tensor", swap)

    info = jnp.stack([part, lengths[0], core]).astype(jnp.int32)
    return attend_pages(
        info, qa, qb, k_mine, k_peer, v_mine, v_peer, kv_own, kv_peer, w_out, wo_pieces
    )[None]


def rotate_pairs(values, positions, columns_from, head_size):
    rows, cols = values.shape
    column = columns_from + jnp.arange(cols // 2, dtype=jnp.int32) * 2
    within = (column % head_size).astype(jnp.float32)
    inv_freq = jnp.exp(within * (-math.log(10000.0) / head_size))
    angle = positions[:, None] * inv_freq[None, :]
    cosine = jnp.cos(angle)
    sine = jnp.sin(angle)
    pairs = values.reshape(rows, cols // 2, 2)
    first = pairs[:, :, 0]
    second = pairs[:, :, 1]
    turned = jnp.stack([first * cosine - second * sine, first * sine + second * cosine], axis=-1)
    return turned.reshape(rows, cols)


def attend(query, keys, values, first_row, heads, head_size, window):
    rows = query.shape[0]
    count = keys.shape[0]
    q_heads = query.reshape(rows, heads, head_size)
    scores = jnp.einsum("rhd,kd->hrk", q_heads, keys, preferred_element_type=jnp.float32) * (
        1.0 / math.sqrt(head_size)
    )
    row_ids = first_row + jnp.arange(rows, dtype=jnp.int32)
    key_ids = jnp.arange(count, dtype=jnp.int32)
    seen = (key_ids[None, :] >= row_ids[:, None] + 1) & (
        key_ids[None, :] <= row_ids[:, None] + window
    )
    scores = jnp.where(seen[None, :, :], scores, -1e30)
    top = jnp.max(scores, axis=-1, keepdims=True)
    expd = jnp.exp(scores - top)
    total = jnp.sum(expd, axis=-1, keepdims=True)
    probs = (expd / total).astype(jnp.bfloat16)
    mixed = jnp.einsum("hrk,kd->rhd", probs, values, preferred_element_type=jnp.float32)
    return mixed.reshape(rows, heads * head_size).astype(jnp.bfloat16)


def shards(tokens, norm_gain, w_query, w_keyval, w_out, kv_pages, page_table, lengths, starts):
    width = tokens.shape[2]
    head_size = w_keyval.shape[1] // 2
    heads = width // head_size
    part = lax.axis_index("tensor")
    local_rows = tokens.shape[1]
    q_cols = w_query.shape[1]
    start = starts[0]
    length = lengths[0]
    xf = tokens[0].astype(jnp.float32)
    scale = lax.rsqrt(jnp.mean(xf * xf, axis=-1, keepdims=True) + 1e-06)
    normed = (xf * scale * norm_gain).astype(jnp.bfloat16)
    piece = lax.all_gather(normed, "tensor", axis=0, tiled=True)
    positions = (start + jnp.arange(piece.shape[0], dtype=jnp.int32)).astype(jnp.float32)
    query = rotate_pairs(
        jnp.dot(piece, w_query, preferred_element_type=jnp.float32),
        positions,
        part * q_cols,
        head_size,
    )
    keyval = jnp.dot(piece, w_keyval, preferred_element_type=jnp.float32)
    new_keys = rotate_pairs(keyval[:, :head_size], positions, 0, head_size)
    projected = jnp.concatenate([query, new_keys, keyval[:, head_size:]], axis=1).astype(
        jnp.bfloat16
    )
    query_cols = projected[:, :q_cols]
    keys_new = projected[:, q_cols : q_cols + head_size]
    values_new = projected[:, q_cols + head_size :]
    query = lax.all_to_all(query_cols, "tensor", split_axis=0, concat_axis=1, tiled=True)
    table = page_table[0]
    piece = lax.all_gather(kv_pages, ("rep", "dp"), axis=0, tiled=True)
    ident = jnp.arange(piece.shape[0], dtype=jnp.int32)
    onehot = (table[:, None] == ident[None, :]).astype(jnp.bfloat16)
    picked = jnp.einsum("cn,nrk->crk", onehot, piece, preferred_element_type=jnp.float32)
    window_pages = lax.all_gather(picked.astype(jnp.bfloat16), "tensor", axis=1, tiled=True)
    cached = window_pages.reshape(-1, 2 * head_size)
    window = cached.shape[0]
    keys = jnp.concatenate([cached[:, :head_size], keys_new], axis=0)
    values = jnp.concatenate([cached[:, head_size:], values_new], axis=0)
    mixed = attend(query, keys, values, part * local_rows, heads, head_size, window)
    mixed_cols = lax.all_to_all(mixed, "tensor", split_axis=1, concat_axis=0, tiled=True)
    summed = lax.psum_scatter(
        jnp.dot(mixed_cols, w_out, preferred_element_type=jnp.float32).astype(jnp.bfloat16),
        "tensor",
        scatter_dimension=0,
        tiled=True,
    ).astype(jnp.float32)
    live = part * local_rows + jnp.arange(local_rows, dtype=jnp.int32) < length
    return jnp.where(live[:, None], summed, 0.0).astype(jnp.bfloat16)[None]


def solution(mesh):
    placed = (
        P(("rep", "dp"), "tensor", None),
        P(),
        P(None, "tensor"),
        P(),
        P("tensor", None),
        P(("rep", "dp"), "tensor", None),
        P(("rep", "dp"), None),
        P(("rep", "dp")),
        P(("rep", "dp")),
    )
    pair = mesh.shape["tensor"] == 2 and mesh.shape["rep"] == 2 and mesh.shape["dp"] % 2 == 0
    body = pair_shards if pair else shards
    return jax.shard_map(
        body,
        mesh=mesh,
        in_specs=placed,
        out_specs=P(("rep", "dp"), "tensor", None),
        check_vma=False,
    )
```

```python
import functools
import math

import jax
import jax.numpy as jnp
from jax import lax
from jax.experimental import pallas as pl
from jax.experimental.pallas import tpu as pltpu
from jax.sharding import PartitionSpec as P

BF16 = jnp.bfloat16
F32 = jnp.float32
MASKED = -1e30
ANY = pl.ANY


def spec(space):
    return pl.BlockSpec(memory_space=space)


def rotation_tables(first, rows, step, head_size):
    column = jnp.arange(head_size, dtype=jnp.int32)
    within = (column // 2 * 2).astype(F32)
    inv_freq = jnp.exp(within * (-math.log(10000.0) / head_size))
    sign = jnp.where(column % 2 == 0, -1.0, 1.0).astype(F32)
    coarse = (first + step * jnp.arange(rows // step, dtype=jnp.int32)).astype(F32)
    fine = jnp.arange(step, dtype=jnp.int32).astype(F32)
    at = jnp.concatenate([coarse, fine])
    angle = at[:, None] * inv_freq[None, :]
    return jnp.cos(angle), jnp.sin(angle) * sign[None, :]


def fill_rotation(cos_t, sin_t, cos_s, sin_s, step):
    blocks = cos_s.shape[0] // step
    cf = cos_t[blocks:, :]
    sf = sin_t[blocks:, :]
    for u in range(blocks):
        cu = cos_t[u : u + 1, :]
        su = sin_t[u : u + 1, :]
        cos_s[u * step : (u + 1) * step, :] = cu * cf - su * sf
        sin_s[u * step : (u + 1) * step, :] = su * cf + cu * sf


def rotate(v, cos, sin, even):
    width = v.shape[1]
    swapped = jnp.where(even, pltpu.roll(v, width - 1, 1), pltpu.roll(v, 1, 1))
    return v * cos + swapped * sin


def score_factor(head_size):
    return math.log2(math.e) / math.sqrt(head_size)


def project_kernel(head_size, step, factor, tok, gain, wq, wkv, cos_t, sin_t, normed, q, kv, cos, sin):
    rows = tok.shape[0]
    tile = min(256, rows)
    fill_rotation(cos_t, sin_t, cos, sin, step)
    even = lax.broadcasted_iota(jnp.int32, (tile, head_size), 1) % 2 == 0
    for i in range(rows // tile):
        at = pl.ds(i * tile, tile)
        xf = tok[at, :].astype(F32)
        scale = lax.rsqrt(jnp.mean(xf * xf, axis=-1, keepdims=True) + 1e-06)
        nb = (xf * scale * gain[...]).astype(BF16)
        normed[at, :] = nb
        c = cos[at, :]
        s = sin[at, :]
        both = jnp.dot(nb, wkv[...], preferred_element_type=F32)
        kv[at, :head_size] = rotate(both[:, :head_size], c, s, even).astype(BF16)
        kv[at, head_size:] = both[:, head_size:].astype(BF16)
        for h in range(wq.shape[1] // head_size):
            cols = slice(h * head_size, (h + 1) * head_size)
            part = jnp.dot(nb, wq[:, cols], preferred_element_type=F32)
            q[at, cols] = (rotate(part, c, s, even) * factor).astype(BF16)


def project(tok, gain, wq, wkv, cos_t, sin_t, head_size, step):
    rows, width = tok.shape
    qc, kc = wq.shape[1], wkv.shape[1]
    return pl.pallas_call(
        functools.partial(project_kernel, head_size, step, score_factor(head_size)),
        out_shape=(
            jax.ShapeDtypeStruct((rows, width), BF16),
            jax.ShapeDtypeStruct((rows, qc), BF16),
            jax.ShapeDtypeStruct((rows, kc), BF16),
            jax.ShapeDtypeStruct((rows, head_size), F32),
            jax.ShapeDtypeStruct((rows, head_size), F32),
        ),
        in_specs=[spec(pltpu.VMEM)] * 6,
        out_specs=[spec(pltpu.VMEM)] * 5,
        compiler_params=pltpu.CompilerParams(vmem_limit_bytes=20 * 2**20),
        cost_estimate=pl.CostEstimate(
            flops=2 * rows * width * (qc + kc), bytes_accessed=10 * 2**20, transcendentals=0
        ),
        name="project_own",
    )(tok, gain.reshape(1, width), wq, wkv, cos_t, sin_t)


def other_kernel(head_size, factor, order, normed, w0, w1, w2, w3, cos, sin, q):
    rows = normed.shape[0]
    tile = min(256, rows)
    deep = w0.shape[0]
    even = lax.broadcasted_iota(jnp.int32, (tile, head_size), 1) % 2 == 0
    for i in range(rows // tile):
        at = pl.ds(i * tile, tile)
        c = cos[at, :]
        s = sin[at, :]
        for h in range(q.shape[1] // head_size):
            cols = slice(h * head_size, (h + 1) * head_size)
            total = None
            for n, w in enumerate((w0, w1, w2, w3)):
                x = normed[at, pl.ds(pl.multiple_of(order[n] * deep, 128), deep)]
                part = jnp.dot(x, w[:, cols], preferred_element_type=F32)
                total = part if total is None else total + part
            q[at, cols] = (rotate(total, c, s, even) * factor).astype(BF16)


def project_other(normed, pieces, order, cos, sin, head_size):
    rows, width = normed.shape
    qc = pieces[0].shape[1]
    return pl.pallas_call(
        functools.partial(other_kernel, head_size, score_factor(head_size)),
        out_shape=jax.ShapeDtypeStruct((rows, qc), BF16),
        in_specs=[spec(pltpu.SMEM)] + [spec(pltpu.VMEM)] * 7,
        out_specs=spec(pltpu.VMEM),
        compiler_params=pltpu.CompilerParams(vmem_limit_bytes=20 * 2**20),
        cost_estimate=pl.CostEstimate(
            flops=2 * rows * width * qc, bytes_accessed=6 * 2**20, transcendentals=0
        ),
        name="project_other",
    )(order, normed, *pieces, cos, sin)


def pick_kernel(idx, pool, keys, vals, sem):
    count, _, head_size = keys.shape
    copies = []
    for n, out in enumerate((keys, vals)):
        cols = pl.ds(n * head_size, head_size)
        for j in range(count):
            page = pool.at[idx[j], :, cols]
            copies.append(pltpu.make_async_copy(page, out.at[j], sem.at[n * count + j]))
    for c in copies:
        c.start()
    for c in copies:
        c.wait()


def pick(pool, idx):
    count = idx.shape[0]
    half = jax.ShapeDtypeStruct((count, pool.shape[1], pool.shape[2] // 2), pool.dtype)
    return pl.pallas_call(
        pick_kernel,
        out_shape=(half, half),
        in_specs=[spec(pltpu.SMEM), spec(ANY)],
        out_specs=[spec(pltpu.VMEM)] * 2,
        scratch_shapes=[pltpu.SemaphoreType.DMA((2 * count,))],
        compiler_params=pltpu.CompilerParams(vmem_limit_bytes=60 * 2**20),
        cost_estimate=pl.CostEstimate(flops=0, bytes_accessed=2**20, transcendentals=0),
        name="pick_pages",
    )(idx, pool)


def attend_kernel(
    head_size,
    info,
    qa_hbm,
    qb_hbm,
    k_mine,
    k_peer,
    v_mine,
    v_peer,
    kv_own,
    kv_peer,
    woa,
    wob0,
    wob1,
    out_hbm,
    qa,
    qb,
    keys,
    vals,
    wa,
    wb,
    mix,
    out,
    sbuf,
    pbuf,
    sums,
    ksem,
    vsem,
    wsem,
    osem,
):
    part = info[0]
    length = info[1]
    rows, half = qa.shape
    pages, prow, _ = k_mine.shape
    page = 2 * prow
    width = out.shape[1]
    core = info[2]
    deep = wob0.shape[0]
    nheads = half // head_size
    window = pages * page

    def start(mine, peer, lo, dst, sem):
        cols = pl.ds(lo, head_size)
        for case in (0, 1):

            @pl.when(part == case)
            def _():
                skip = case * rows // page
                for u in range(skip, pages):
                    for src, side in ((mine, case), (peer, 1 - case)):
                        to = pl.ds((u - skip) * page + side * prow, prow)
                        pltpu.make_async_copy(src.at[u], dst.at[to, :], sem).start()
                if case == 1:
                    to = pl.ds(window - rows, rows)
                    pltpu.make_async_copy(kv_peer.at[:, cols], dst.at[to, :], sem).start()
                to = pl.ds(window, rows)
                pltpu.make_async_copy(kv_own.at[:, cols], dst.at[to, :], sem).start()

    def finish(dst, sem):
        pltpu.make_async_copy(dst, dst, sem).wait()

    queries = [
        pltpu.make_async_copy(qa_hbm, qa, wsem.at[3]),
        pltpu.make_async_copy(qb_hbm, qb, wsem.at[4]),
    ]
    queries[0].start()
    start(k_mine, k_peer, 0, keys, ksem)
    queries[1].start()
    start(v_mine, v_peer, head_size, vals, vsem)
    weights = [
        pltpu.make_async_copy(woa, wa, wsem.at[0]),
        pltpu.make_async_copy(wob0, wb.at[pl.ds(core * deep, deep), :], wsem.at[1]),
        pltpu.make_async_copy(wob1, wb.at[pl.ds((1 - core) * deep, deep), :], wsem.at[2]),
    ]
    for c in weights:
        c.start()

    tile = min(256, rows)
    span = window + tile
    band = min(32, tile)
    gap = lax.broadcasted_iota(jnp.int32, (band, tile), 1) - lax.broadcasted_iota(
        jnp.int32, (band, tile), 0
    )
    order = [(i, n, h) for i in range(rows // tile) for n in range(2) for h in range(nheads)]

    def score(m):
        i, n, h = order[m]
        q = (qa, qb)[n][pl.ds(i * tile, tile), h * head_size : (h + 1) * head_size]
        for lo in range(0, span, tile):
            sbuf[m % 2, :, lo : lo + tile] = lax.dot_general(
                q,
                keys[pl.ds(i * tile + lo, tile), :],
                (((1,), (1,)), ((), ())),
                preferred_element_type=F32,
            )

    def soften(m):
        for lo in range(0, tile, band):
            at = pl.ds(lo, band)
            s = jnp.concatenate(
                [
                    jnp.where(gap >= lo + 1, sbuf[m % 2, at, :tile], MASKED),
                    sbuf[m % 2, at, tile : span - tile],
                    jnp.where(gap <= lo, sbuf[m % 2, at, span - tile :], MASKED),
                ],
                axis=1,
            )
            e = jnp.exp2(s - jnp.max(s, axis=-1, keepdims=True))
            total = jnp.sum(e, axis=-1, keepdims=True)
            pbuf[m % 2, at, :] = e.astype(BF16)
            sums[m % 2, at, :] = jnp.broadcast_to(1.0 / total, (band, 128))

    def combine(m):
        i, n, h = order[m]
        mixed = jnp.dot(
            pbuf[m % 2], vals[pl.ds(i * tile, span), :], preferred_element_type=F32
        )
        mixed = mixed * sums[m % 2, :, :1]
        at = pl.ds(i * tile, tile)
        mix[n, at, h * head_size : (h + 1) * head_size] = mixed.astype(BF16)

    block = 512

    def project_out(i, lo):
        at = pl.ds(i * tile, tile)
        row = part * rows + i * tile + lax.broadcasted_iota(jnp.int32, (tile, 1), 0)
        cols = slice(lo, lo + block)
        a = jnp.dot(mix[0, at, :], wa[:, cols], preferred_element_type=F32)
        b = jnp.dot(mix[1, at, :], wb[:, cols], preferred_element_type=F32)
        both = a.astype(BF16).astype(F32) + b.astype(BF16).astype(F32)
        out[at, cols] = jnp.where(row < length, both, 0.0).astype(BF16)

    stores = []

    def send_out(i):
        at = pl.ds(i * tile, tile)
        stores.append(pltpu.make_async_copy(out.at[at, :], out_hbm.at[at, :], osem.at[i]))
        stores[i].start()

    queries[0].wait()
    finish(keys, ksem)
    queries[1].wait()
    score(0)
    ready = []
    for m in range(len(order)):
        if m + 1 < len(order):
            score(m + 1)
        if m == 1:
            finish(vals, vsem)
        if m >= 1:
            combine(m - 1)
            i, n, h = order[m - 1]
            if (n, h) == (1, nheads - 1):
                if i == 0:
                    for c in weights:
                        c.wait()
                ready += [(i, lo) for lo in range(0, width, block)]
        if m >= 1 and ready and order[m - 1][1:] != (1, nheads - 1):
            i, lo = ready.pop(0)
            project_out(i, lo)
            if lo + block == width:
                send_out(i)
        soften(m)
    combine(len(order) - 1)
    if rows == tile:
        for c in weights:
            c.wait()
    ready += [(rows // tile - 1, lo) for lo in range(0, width, block)]
    for i, lo in ready:
        project_out(i, lo)
        if lo + block == width:
            send_out(i)
    for c in stores:
        c.wait()


def attend_pages(info, qa, qb, k_mine, k_peer, v_mine, v_peer, kv_own, kv_peer, woa, wobs):
    rows, half = qa.shape
    tile = min(256, rows)
    width = woa.shape[1]
    head_size = k_mine.shape[2]
    window = k_mine.shape[0] * k_mine.shape[1] * 2
    return pl.pallas_call(
        functools.partial(attend_kernel, head_size),
        out_shape=jax.ShapeDtypeStruct((rows, width), BF16),
        in_specs=[spec(pltpu.SMEM)]
        + [spec(ANY)] * 2
        + [spec(pltpu.VMEM)] * 4
        + [spec(ANY)] * 5,
        out_specs=spec(ANY),
        scratch_shapes=[
            pltpu.VMEM((rows, half), BF16),
            pltpu.VMEM((rows, half), BF16),
            pltpu.VMEM((window + rows, head_size), BF16),
            pltpu.VMEM((window + rows, head_size), BF16),
            pltpu.VMEM(woa.shape, BF16),
            pltpu.VMEM(woa.shape, BF16),
            pltpu.VMEM((2, rows, half), BF16),
            pltpu.VMEM((rows, width), BF16),
            pltpu.VMEM((2, tile, window + tile), F32),
            pltpu.VMEM((2, tile, window + tile), BF16),
            pltpu.VMEM((2, tile, 128), F32),
            pltpu.SemaphoreType.DMA,
            pltpu.SemaphoreType.DMA,
            pltpu.SemaphoreType.DMA((5,)),
            pltpu.SemaphoreType.DMA((rows // tile,)),
        ],
        compiler_params=pltpu.CompilerParams(vmem_limit_bytes=56 * 2**20),
        cost_estimate=pl.CostEstimate(
            flops=4 * rows * 2 * half * (window + 256) + 4 * rows * half * width,
            bytes_accessed=12 * 2**20,
            transcendentals=rows * 6 * (window + 256),
        ),
        name="attend_and_out",
    )(info, qa, qb, k_mine, k_peer, v_mine, v_peer, kv_own, kv_peer, woa, *wobs)


def pair_shards(tokens, norm_gain, w_query, w_keyval, w_out, kv_pages, page_table, lengths, starts):
    head_size = w_keyval.shape[1] // 2
    part = lax.axis_index("tensor")
    rep = lax.axis_index("rep")
    dp = lax.axis_index("dp")
    ndp = lax.axis_size("dp")
    core = dp % 2
    rows = tokens.shape[1]
    swap = [(0, 1), (1, 0)]
    cores = [(i, i ^ 1) for i in range(ndp)]

    pool = lax.all_gather(kv_pages, "dp", axis=0, tiled=True)

    def peer_rows(w, at, parts):
        deep = w.shape[0] // parts
        return lax.ppermute(lax.dynamic_slice_in_dim(w, at * deep, deep, 0), "tensor", swap)

    step = 32
    cos_t, sin_t = rotation_tables(starts[0] + part * rows, rows, step, head_size)
    normed, qa, kv_own, cos, sin = project(
        tokens[0], norm_gain, w_query, w_keyval, cos_t, sin_t, head_size, step
    )

    a = peer_rows(w_query, rep * 2 + core, 4)
    a, kv_own, w_out_late, page_table = lax.optimization_barrier((a, kv_own, w_out, page_table))
    b = lax.ppermute(a, "rep", swap)
    c = peer_rows(w_out_late, core, 2)
    table = page_table[0]
    peer_table = lax.ppermute(table, "rep", swap)
    wq_pieces = (a, b, lax.ppermute(a, "dp", cores), lax.ppermute(b, "dp", cores))
    order = jnp.stack(
        [rep * 2 + core, (1 - rep) * 2 + core, rep * 2 + 1 - core, (1 - rep) * 2 + 1 - core]
    ).astype(jnp.int32)
    qb = project_other(normed, wq_pieces, order, cos, sin, head_size)
    c, qb, kv_own = lax.optimization_barrier((c, qb, kv_own))
    wo_pieces = (c, lax.ppermute(c, "dp", cores))
    kv_peer = lax.ppermute(kv_own, "tensor", swap)

    per_rep = kv_pages.shape[0] * ndp
    home = table[0] // per_rep == rep
    own_at, peer_at = table % per_rep, peer_table % per_rep
    wo_pieces, pool, own_at, peer_at = lax.optimization_barrier(
        (wo_pieces, pool, own_at, peer_at)
    )
    k_sent, v_sent = pick(pool, peer_at)
    k_came = lax.ppermute(k_sent, "rep", swap)
    v_came = lax.ppermute(v_sent, "rep", swap)
    k_held, v_held = pick(pool, own_at)
    k_came, kv_peer, k_held = lax.optimization_barrier((k_came, kv_peer, k_held))
    k_mine = jnp.where(home, k_held, k_came)
    k_peer = lax.ppermute(k_mine, "tensor", swap)
    v_mine = jnp.where(home, v_held, v_came)
    v_peer = lax.ppermute(v_mine, "tensor", swap)

    info = jnp.stack([part, lengths[0], core]).astype(jnp.int32)
    return attend_pages(
        info, qa, qb, k_mine, k_peer, v_mine, v_peer, kv_own, kv_peer, w_out, wo_pieces
    )[None]


def rotate_pairs(values, positions, columns_from, head_size):
    rows, cols = values.shape
    column = columns_from + jnp.arange(cols // 2, dtype=jnp.int32) * 2
    within = (column % head_size).astype(jnp.float32)
    inv_freq = jnp.exp(within * (-math.log(10000.0) / head_size))
    angle = positions[:, None] * inv_freq[None, :]
    cosine = jnp.cos(angle)
    sine = jnp.sin(angle)
    pairs = values.reshape(rows, cols // 2, 2)
    first = pairs[:, :, 0]
    second = pairs[:, :, 1]
    turned = jnp.stack([first * cosine - second * sine, first * sine + second * cosine], axis=-1)
    return turned.reshape(rows, cols)


def attend(query, keys, values, first_row, heads, head_size, window):
    rows = query.shape[0]
    count = keys.shape[0]
    q_heads = query.reshape(rows, heads, head_size)
    scores = jnp.einsum("rhd,kd->hrk", q_heads, keys, preferred_element_type=jnp.float32) * (
        1.0 / math.sqrt(head_size)
    )
    row_ids = first_row + jnp.arange(rows, dtype=jnp.int32)
    key_ids = jnp.arange(count, dtype=jnp.int32)
    seen = (key_ids[None, :] >= row_ids[:, None] + 1) & (
        key_ids[None, :] <= row_ids[:, None] + window
    )
    scores = jnp.where(seen[None, :, :], scores, -1e30)
    top = jnp.max(scores, axis=-1, keepdims=True)
    expd = jnp.exp(scores - top)
    total = jnp.sum(expd, axis=-1, keepdims=True)
    probs = (expd / total).astype(jnp.bfloat16)
    mixed = jnp.einsum("hrk,kd->rhd", probs, values, preferred_element_type=jnp.float32)
    return mixed.reshape(rows, heads * head_size).astype(jnp.bfloat16)


def shards(tokens, norm_gain, w_query, w_keyval, w_out, kv_pages, page_table, lengths, starts):
    width = tokens.shape[2]
    head_size = w_keyval.shape[1] // 2
    heads = width // head_size
    part = lax.axis_index("tensor")
    local_rows = tokens.shape[1]
    q_cols = w_query.shape[1]
    start = starts[0]
    length = lengths[0]
    xf = tokens[0].astype(jnp.float32)
    scale = lax.rsqrt(jnp.mean(xf * xf, axis=-1, keepdims=True) + 1e-06)
    normed = (xf * scale * norm_gain).astype(jnp.bfloat16)
    piece = lax.all_gather(normed, "tensor", axis=0, tiled=True)
    positions = (start + jnp.arange(piece.shape[0], dtype=jnp.int32)).astype(jnp.float32)
    query = rotate_pairs(
        jnp.dot(piece, w_query, preferred_element_type=jnp.float32),
        positions,
        part * q_cols,
        head_size,
    )
    keyval = jnp.dot(piece, w_keyval, preferred_element_type=jnp.float32)
    new_keys = rotate_pairs(keyval[:, :head_size], positions, 0, head_size)
    projected = jnp.concatenate([query, new_keys, keyval[:, head_size:]], axis=1).astype(
        jnp.bfloat16
    )
    query_cols = projected[:, :q_cols]
    keys_new = projected[:, q_cols : q_cols + head_size]
    values_new = projected[:, q_cols + head_size :]
    query = lax.all_to_all(query_cols, "tensor", split_axis=0, concat_axis=1, tiled=True)
    table = page_table[0]
    piece = lax.all_gather(kv_pages, ("rep", "dp"), axis=0, tiled=True)
    ident = jnp.arange(piece.shape[0], dtype=jnp.int32)
    onehot = (table[:, None] == ident[None, :]).astype(jnp.bfloat16)
    picked = jnp.einsum("cn,nrk->crk", onehot, piece, preferred_element_type=jnp.float32)
    window_pages = lax.all_gather(picked.astype(jnp.bfloat16), "tensor", axis=1, tiled=True)
    cached = window_pages.reshape(-1, 2 * head_size)
    window = cached.shape[0]
    keys = jnp.concatenate([cached[:, :head_size], keys_new], axis=0)
    values = jnp.concatenate([cached[:, head_size:], values_new], axis=0)
    mixed = attend(query, keys, values, part * local_rows, heads, head_size, window)
    mixed_cols = lax.all_to_all(mixed, "tensor", split_axis=1, concat_axis=0, tiled=True)
    summed = lax.psum_scatter(
        jnp.dot(mixed_cols, w_out, preferred_element_type=jnp.float32).astype(jnp.bfloat16),
        "tensor",
        scatter_dimension=0,
        tiled=True,
    ).astype(jnp.float32)
    live = part * local_rows + jnp.arange(local_rows, dtype=jnp.int32) < length
    return jnp.where(live[:, None], summed, 0.0).astype(jnp.bfloat16)[None]


def solution(mesh):
    placed = (
        P(("rep", "dp"), "tensor", None),
        P(),
        P(None, "tensor"),
        P(),
        P("tensor", None),
        P(("rep", "dp"), "tensor", None),
        P(("rep", "dp"), None),
        P(("rep", "dp")),
        P(("rep", "dp")),
    )
    pair = mesh.shape["tensor"] == 2 and mesh.shape["rep"] == 2 and mesh.shape["dp"] % 2 == 0
    body = pair_shards if pair else shards
    return jax.shard_map(
        body,
        mesh=mesh,
        in_specs=placed,
        out_specs=P(("rep", "dp"), "tensor", None),
        check_vma=False,
    )
```

```python
import functools
import math

import jax
import jax.numpy as jnp
from jax import lax
from jax.experimental import pallas as pl
from jax.experimental.pallas import tpu as pltpu
from jax.sharding import PartitionSpec as P

BF16 = jnp.bfloat16
F32 = jnp.float32
MASKED = -1e30
ANY = pl.ANY


def spec(space):
    return pl.BlockSpec(memory_space=space)


def rotation_tables(first, rows, step, head_size):
    column = jnp.arange(head_size, dtype=jnp.int32)
    within = (column // 2 * 2).astype(F32)
    inv_freq = jnp.exp(within * (-math.log(10000.0) / head_size))
    sign = jnp.where(column % 2 == 0, -1.0, 1.0).astype(F32)
    coarse = (first + step * jnp.arange(rows // step, dtype=jnp.int32)).astype(F32)
    fine = jnp.arange(step, dtype=jnp.int32).astype(F32)
    at = jnp.concatenate([coarse, fine])
    angle = at[:, None] * inv_freq[None, :]
    return jnp.cos(angle), jnp.sin(angle) * sign[None, :]


def fill_rotation(cos_t, sin_t, cos_s, sin_s, step):
    blocks = cos_s.shape[0] // step
    cf = cos_t[blocks:, :]
    sf = sin_t[blocks:, :]
    for u in range(blocks):
        cu = cos_t[u : u + 1, :]
        su = sin_t[u : u + 1, :]
        cos_s[u * step : (u + 1) * step, :] = cu * cf - su * sf
        sin_s[u * step : (u + 1) * step, :] = su * cf + cu * sf


def rotate(v, cos, sin, even):
    width = v.shape[1]
    swapped = jnp.where(even, pltpu.roll(v, width - 1, 1), pltpu.roll(v, 1, 1))
    return v * cos + swapped * sin


def score_factor(head_size):
    return math.log2(math.e) / math.sqrt(head_size)


def project_kernel(head_size, step, factor, tok, gain, wq, wkv, cos_t, sin_t, normed, q, kv, cos, sin):
    rows = tok.shape[0]
    tile = min(256, rows)
    fill_rotation(cos_t, sin_t, cos, sin, step)
    even = lax.broadcasted_iota(jnp.int32, (tile, head_size), 1) % 2 == 0
    for i in range(rows // tile):
        at = pl.ds(i * tile, tile)
        xf = tok[at, :].astype(F32)
        scale = lax.rsqrt(jnp.mean(xf * xf, axis=-1, keepdims=True) + 1e-06)
        nb = (xf * scale * gain[...]).astype(BF16)
        normed[at, :] = nb
        c = cos[at, :]
        s = sin[at, :]
        both = jnp.dot(nb, wkv[...], preferred_element_type=F32)
        kv[at, :head_size] = rotate(both[:, :head_size], c, s, even).astype(BF16)
        kv[at, head_size:] = both[:, head_size:].astype(BF16)
        for h in range(wq.shape[1] // head_size):
            cols = slice(h * head_size, (h + 1) * head_size)
            part = jnp.dot(nb, wq[:, cols], preferred_element_type=F32)
            q[h, at, :] = (rotate(part, c, s, even) * factor).astype(BF16)


def project(tok, gain, wq, wkv, cos_t, sin_t, head_size, step):
    rows, width = tok.shape
    qc, kc = wq.shape[1], wkv.shape[1]
    return pl.pallas_call(
        functools.partial(project_kernel, head_size, step, score_factor(head_size)),
        out_shape=(
            jax.ShapeDtypeStruct((rows, width), BF16),
            jax.ShapeDtypeStruct((qc // head_size, rows, head_size), BF16),
            jax.ShapeDtypeStruct((rows, kc), BF16),
            jax.ShapeDtypeStruct((rows, head_size), F32),
            jax.ShapeDtypeStruct((rows, head_size), F32),
        ),
        in_specs=[spec(pltpu.VMEM)] * 6,
        out_specs=[spec(pltpu.VMEM)] * 5,
        compiler_params=pltpu.CompilerParams(vmem_limit_bytes=20 * 2**20),
        cost_estimate=pl.CostEstimate(
            flops=2 * rows * width * (qc + kc), bytes_accessed=10 * 2**20, transcendentals=0
        ),
        name="project_own",
    )(tok, gain.reshape(1, width), wq, wkv, cos_t, sin_t)


def other_kernel(head_size, factor, order, normed, w0, w1, w2, w3, cos, sin, q):
    rows = normed.shape[0]
    deep = w0.shape[0]
    even = lax.broadcasted_iota(jnp.int32, (rows, head_size), 1) % 2 == 0
    for h in range(q.shape[0]):
        cols = slice(h * head_size, (h + 1) * head_size)
        total = None
        for n, w in enumerate((w0, w1, w2, w3)):
            x = normed[:, pl.ds(pl.multiple_of(order[n] * deep, 128), deep)]
            part = jnp.dot(x, w[:, cols], preferred_element_type=F32)
            total = part if total is None else total + part
        q[h] = (rotate(total, cos[...], sin[...], even) * factor).astype(BF16)


def project_other(normed, pieces, order, cos, sin, head_size):
    rows, width = normed.shape
    qc = pieces[0].shape[1]
    return pl.pallas_call(
        functools.partial(other_kernel, head_size, score_factor(head_size)),
        out_shape=jax.ShapeDtypeStruct((qc // head_size, rows, head_size), BF16),
        in_specs=[spec(pltpu.SMEM)] + [spec(pltpu.VMEM)] * 7,
        out_specs=spec(pltpu.VMEM),
        compiler_params=pltpu.CompilerParams(vmem_limit_bytes=20 * 2**20),
        cost_estimate=pl.CostEstimate(
            flops=2 * rows * width * qc, bytes_accessed=6 * 2**20, transcendentals=0
        ),
        name="project_other",
    )(order, normed, *pieces, cos, sin)


def pick_kernel(idx, pool, keys, vals, sem):
    count, _, head_size = keys.shape
    copies = []
    for n, out in enumerate((keys, vals)):
        cols = pl.ds(n * head_size, head_size)
        for j in range(count):
            page = pool.at[idx[j], :, cols]
            copies.append(pltpu.make_async_copy(page, out.at[j], sem.at[n * count + j]))
    for c in copies:
        c.start()
    for c in copies:
        c.wait()


def pick(pool, idx):
    count = idx.shape[0]
    half = jax.ShapeDtypeStruct((count, pool.shape[1], pool.shape[2] // 2), pool.dtype)
    return pl.pallas_call(
        pick_kernel,
        out_shape=(half, half),
        in_specs=[spec(pltpu.SMEM), spec(ANY)],
        out_specs=[spec(pltpu.VMEM)] * 2,
        scratch_shapes=[pltpu.SemaphoreType.DMA((2 * count,))],
        compiler_params=pltpu.CompilerParams(vmem_limit_bytes=60 * 2**20),
        cost_estimate=pl.CostEstimate(flops=0, bytes_accessed=2**20, transcendentals=0),
        name="pick_pages",
    )(idx, pool)


def attend_kernel(
    head_size,
    info,
    qa_hbm,
    qb_hbm,
    k_mine,
    k_peer,
    v_mine,
    v_peer,
    kv_own,
    kv_peer,
    woa,
    wob0,
    wob1,
    out_hbm,
    qa,
    qb,
    keys,
    vals,
    wa,
    wb,
    mix,
    out,
    sbuf,
    pbuf,
    sums,
    ksem,
    vsem,
    wsem,
    osem,
):
    part = info[0]
    length = info[1]
    nheads, rows, _ = qa.shape
    pages, prow, _ = k_mine.shape
    page = 2 * prow
    width = out.shape[1]
    core = info[2]
    deep = wob0.shape[0]
    window = pages * page

    def start(mine, peer, lo, dst, sem):
        cols = pl.ds(lo, head_size)
        for case in (0, 1):

            @pl.when(part == case)
            def _():
                skip = case * rows // page
                for u in range(skip, pages):
                    for src, side in ((mine, case), (peer, 1 - case)):
                        to = pl.ds((u - skip) * page + side * prow, prow)
                        pltpu.make_async_copy(src.at[u], dst.at[to, :], sem).start()
                if case == 1:
                    to = pl.ds(window - rows, rows)
                    pltpu.make_async_copy(kv_peer.at[:, cols], dst.at[to, :], sem).start()
                to = pl.ds(window, rows)
                pltpu.make_async_copy(kv_own.at[:, cols], dst.at[to, :], sem).start()

    def finish(dst, sem):
        pltpu.make_async_copy(dst, dst, sem).wait()

    queries = [
        pltpu.make_async_copy(qa_hbm, qa, wsem.at[3]),
        pltpu.make_async_copy(qb_hbm, qb, wsem.at[4]),
    ]
    queries[0].start()
    start(k_mine, k_peer, 0, keys, ksem)
    queries[1].start()
    start(v_mine, v_peer, head_size, vals, vsem)
    weights = [
        pltpu.make_async_copy(woa, wa, wsem.at[0]),
        pltpu.make_async_copy(wob0, wb.at[pl.ds(core * deep, deep), :], wsem.at[1]),
        pltpu.make_async_copy(wob1, wb.at[pl.ds((1 - core) * deep, deep), :], wsem.at[2]),
    ]
    for c in weights:
        c.start()

    tile = min(256, rows)
    span = window + tile
    band = min(32, tile)
    gap = lax.broadcasted_iota(jnp.int32, (band, tile), 1) - lax.broadcasted_iota(
        jnp.int32, (band, tile), 0
    )
    groups = [(i, n) for i in range(rows // tile) for n in range(2)]
    tall = nheads * tile

    def score(g):
        i, n = groups[g]
        q = (qa, qb)[n][:, pl.ds(i * tile, tile), :].reshape(tall, head_size)
        for lo in range(0, span, tile):
            sbuf[g % 2, :, lo : lo + tile] = lax.dot_general(
                q,
                keys[pl.ds(i * tile + lo, tile), :],
                (((1,), (1,)), ((), ())),
                preferred_element_type=F32,
            )

    def soften(g):
        for top in range(0, tall, band):
            at = pl.ds(top, band)
            lo = top % tile
            s = jnp.concatenate(
                [
                    jnp.where(gap >= lo + 1, sbuf[g % 2, at, :tile], MASKED),
                    sbuf[g % 2, at, tile : span - tile],
                    jnp.where(gap <= lo, sbuf[g % 2, at, span - tile :], MASKED),
                ],
                axis=1,
            )
            e = jnp.exp2(s - jnp.max(s, axis=-1, keepdims=True))
            total = jnp.sum(e, axis=-1, keepdims=True)
            pbuf[g % 2, at, :] = e.astype(BF16)
            sums[g % 2, at, :] = jnp.broadcast_to(1.0 / total, (band, 128))

    def combine(g):
        i, n = groups[g]
        mixed = jnp.dot(
            pbuf[g % 2], vals[pl.ds(i * tile, span), :], preferred_element_type=F32
        )
        mixed = (mixed * sums[g % 2, :, :1]).astype(BF16)
        for h in range(nheads):
            part_h = mixed[h * tile : (h + 1) * tile, :]
            mix[n, pl.ds(i * tile, tile), h * head_size : (h + 1) * head_size] = part_h

    queries[0].wait()
    finish(keys, ksem)
    score(0)
    queries[1].wait()
    for g in range(len(groups)):
        if g + 1 < len(groups):
            score(g + 1)
        if g == 1:
            finish(vals, vsem)
        if g >= 1:
            combine(g - 1)
        soften(g)
    if len(groups) == 1:
        finish(vals, vsem)
    combine(len(groups) - 1)
    for c in weights:
        c.wait()
    row = part * rows + lax.broadcasted_iota(jnp.int32, (rows, 1), 0)
    live = row < length
    block = 256
    stores = []
    for lo in range(0, width, block):
        cols = slice(lo, lo + block)
        a = jnp.dot(mix[0], wa[:, cols], preferred_element_type=F32)
        b = jnp.dot(mix[1], wb[:, cols], preferred_element_type=F32)
        both = a.astype(BF16).astype(F32) + b.astype(BF16).astype(F32)
        out[:, cols] = jnp.where(live, both, 0.0).astype(BF16)
        m = len(stores)
        stores.append(pltpu.make_async_copy(out.at[:, cols], out_hbm.at[:, cols], osem.at[m]))
        stores[m].start()
    for c in stores:
        c.wait()


def attend_pages(info, qa, qb, k_mine, k_peer, v_mine, v_peer, kv_own, kv_peer, woa, wobs):
    nheads, rows, _ = qa.shape
    half = woa.shape[0]
    tile = min(256, rows)
    tall = nheads * tile
    width = woa.shape[1]
    head_size = k_mine.shape[2]
    window = k_mine.shape[0] * k_mine.shape[1] * 2
    return pl.pallas_call(
        functools.partial(attend_kernel, head_size),
        out_shape=jax.ShapeDtypeStruct((rows, width), BF16),
        in_specs=[spec(pltpu.SMEM)]
        + [spec(ANY)] * 2
        + [spec(pltpu.VMEM)] * 4
        + [spec(ANY)] * 5,
        out_specs=spec(ANY),
        scratch_shapes=[
            pltpu.VMEM(qa.shape, BF16),
            pltpu.VMEM(qa.shape, BF16),
            pltpu.VMEM((window + rows, head_size), BF16),
            pltpu.VMEM((window + rows, head_size), BF16),
            pltpu.VMEM(woa.shape, BF16),
            pltpu.VMEM(woa.shape, BF16),
            pltpu.VMEM((2, rows, half), BF16),
            pltpu.VMEM((rows, width), BF16),
            pltpu.VMEM((2, tall, window + tile), F32),
            pltpu.VMEM((2, tall, window + tile), BF16),
            pltpu.VMEM((2, tall, 128), F32),
            pltpu.SemaphoreType.DMA,
            pltpu.SemaphoreType.DMA,
            pltpu.SemaphoreType.DMA((5,)),
            pltpu.SemaphoreType.DMA((width // 256,)),
        ],
        compiler_params=pltpu.CompilerParams(vmem_limit_bytes=56 * 2**20),
        cost_estimate=pl.CostEstimate(
            flops=4 * rows * 2 * half * (window + 256) + 4 * rows * half * width,
            bytes_accessed=12 * 2**20,
            transcendentals=rows * 6 * (window + 256),
        ),
        name="attend_and_out",
    )(info, qa, qb, k_mine, k_peer, v_mine, v_peer, kv_own, kv_peer, woa, *wobs)


def pair_shards(tokens, norm_gain, w_query, w_keyval, w_out, kv_pages, page_table, lengths, starts):
    head_size = w_keyval.shape[1] // 2
    part = lax.axis_index("tensor")
    rep = lax.axis_index("rep")
    dp = lax.axis_index("dp")
    ndp = lax.axis_size("dp")
    core = dp % 2
    rows = tokens.shape[1]
    swap = [(0, 1), (1, 0)]
    cores = [(i, i ^ 1) for i in range(ndp)]

    pool = lax.all_gather(kv_pages, "dp", axis=0, tiled=True)

    def peer_rows(w, at, parts):
        deep = w.shape[0] // parts
        return lax.ppermute(lax.dynamic_slice_in_dim(w, at * deep, deep, 0), "tensor", swap)

    step = 32
    cos_t, sin_t = rotation_tables(starts[0] + part * rows, rows, step, head_size)
    normed, qa, kv_own, cos, sin = project(
        tokens[0], norm_gain, w_query, w_keyval, cos_t, sin_t, head_size, step
    )

    a = peer_rows(w_query, rep * 2 + core, 4)
    a, kv_own, w_out_late, page_table = lax.optimization_barrier((a, kv_own, w_out, page_table))
    b = lax.ppermute(a, "rep", swap)
    c = peer_rows(w_out_late, core, 2)
    table = page_table[0]
    peer_table = lax.ppermute(table, "rep", swap)
    wq_pieces = (a, b, lax.ppermute(a, "dp", cores), lax.ppermute(b, "dp", cores))
    order = jnp.stack(
        [rep * 2 + core, (1 - rep) * 2 + core, rep * 2 + 1 - core, (1 - rep) * 2 + 1 - core]
    ).astype(jnp.int32)
    qb = project_other(normed, wq_pieces, order, cos, sin, head_size)
    c, qb, kv_own = lax.optimization_barrier((c, qb, kv_own))
    wo_pieces = (c, lax.ppermute(c, "dp", cores))
    kv_peer = lax.ppermute(kv_own, "tensor", swap)

    per_rep = kv_pages.shape[0] * ndp
    home = table[0] // per_rep == rep
    own_at, peer_at = table % per_rep, peer_table % per_rep
    wo_pieces, pool, own_at, peer_at = lax.optimization_barrier(
        (wo_pieces, pool, own_at, peer_at)
    )
    k_sent, v_sent = pick(pool, peer_at)
    k_came = lax.ppermute(k_sent, "rep", swap)
    v_came = lax.ppermute(v_sent, "rep", swap)
    k_held, v_held = pick(pool, own_at)
    k_came, kv_peer, k_held = lax.optimization_barrier((k_came, kv_peer, k_held))
    k_mine = jnp.where(home, k_held, k_came)
    k_peer = lax.ppermute(k_mine, "tensor", swap)
    v_mine = jnp.where(home, v_held, v_came)
    v_peer = lax.ppermute(v_mine, "tensor", swap)

    info = jnp.stack([part, lengths[0], core]).astype(jnp.int32)
    return attend_pages(
        info, qa, qb, k_mine, k_peer, v_mine, v_peer, kv_own, kv_peer, w_out, wo_pieces
    )[None]


def rotate_pairs(values, positions, columns_from, head_size):
    rows, cols = values.shape
    column = columns_from + jnp.arange(cols // 2, dtype=jnp.int32) * 2
    within = (column % head_size).astype(jnp.float32)
    inv_freq = jnp.exp(within * (-math.log(10000.0) / head_size))
    angle = positions[:, None] * inv_freq[None, :]
    cosine = jnp.cos(angle)
    sine = jnp.sin(angle)
    pairs = values.reshape(rows, cols // 2, 2)
    first = pairs[:, :, 0]
    second = pairs[:, :, 1]
    turned = jnp.stack([first * cosine - second * sine, first * sine + second * cosine], axis=-1)
    return turned.reshape(rows, cols)


def attend(query, keys, values, first_row, heads, head_size, window):
    rows = query.shape[0]
    count = keys.shape[0]
    q_heads = query.reshape(rows, heads, head_size)
    scores = jnp.einsum("rhd,kd->hrk", q_heads, keys, preferred_element_type=jnp.float32) * (
        1.0 / math.sqrt(head_size)
    )
    row_ids = first_row + jnp.arange(rows, dtype=jnp.int32)
    key_ids = jnp.arange(count, dtype=jnp.int32)
    seen = (key_ids[None, :] >= row_ids[:, None] + 1) & (
        key_ids[None, :] <= row_ids[:, None] + window
    )
    scores = jnp.where(seen[None, :, :], scores, -1e30)
    top = jnp.max(scores, axis=-1, keepdims=True)
    expd = jnp.exp(scores - top)
    total = jnp.sum(expd, axis=-1, keepdims=True)
    probs = (expd / total).astype(jnp.bfloat16)
    mixed = jnp.einsum("hrk,kd->rhd", probs, values, preferred_element_type=jnp.float32)
    return mixed.reshape(rows, heads * head_size).astype(jnp.bfloat16)


def shards(tokens, norm_gain, w_query, w_keyval, w_out, kv_pages, page_table, lengths, starts):
    width = tokens.shape[2]
    head_size = w_keyval.shape[1] // 2
    heads = width // head_size
    part = lax.axis_index("tensor")
    local_rows = tokens.shape[1]
    q_cols = w_query.shape[1]
    start = starts[0]
    length = lengths[0]
    xf = tokens[0].astype(jnp.float32)
    scale = lax.rsqrt(jnp.mean(xf * xf, axis=-1, keepdims=True) + 1e-06)
    normed = (xf * scale * norm_gain).astype(jnp.bfloat16)
    piece = lax.all_gather(normed, "tensor", axis=0, tiled=True)
    positions = (start + jnp.arange(piece.shape[0], dtype=jnp.int32)).astype(jnp.float32)
    query = rotate_pairs(
        jnp.dot(piece, w_query, preferred_element_type=jnp.float32),
        positions,
        part * q_cols,
        head_size,
    )
    keyval = jnp.dot(piece, w_keyval, preferred_element_type=jnp.float32)
    new_keys = rotate_pairs(keyval[:, :head_size], positions, 0, head_size)
    projected = jnp.concatenate([query, new_keys, keyval[:, head_size:]], axis=1).astype(
        jnp.bfloat16
    )
    query_cols = projected[:, :q_cols]
    keys_new = projected[:, q_cols : q_cols + head_size]
    values_new = projected[:, q_cols + head_size :]
    query = lax.all_to_all(query_cols, "tensor", split_axis=0, concat_axis=1, tiled=True)
    table = page_table[0]
    piece = lax.all_gather(kv_pages, ("rep", "dp"), axis=0, tiled=True)
    ident = jnp.arange(piece.shape[0], dtype=jnp.int32)
    onehot = (table[:, None] == ident[None, :]).astype(jnp.bfloat16)
    picked = jnp.einsum("cn,nrk->crk", onehot, piece, preferred_element_type=jnp.float32)
    window_pages = lax.all_gather(picked.astype(jnp.bfloat16), "tensor", axis=1, tiled=True)
    cached = window_pages.reshape(-1, 2 * head_size)
    window = cached.shape[0]
    keys = jnp.concatenate([cached[:, :head_size], keys_new], axis=0)
    values = jnp.concatenate([cached[:, head_size:], values_new], axis=0)
    mixed = attend(query, keys, values, part * local_rows, heads, head_size, window)
    mixed_cols = lax.all_to_all(mixed, "tensor", split_axis=1, concat_axis=0, tiled=True)
    summed = lax.psum_scatter(
        jnp.dot(mixed_cols, w_out, preferred_element_type=jnp.float32).astype(jnp.bfloat16),
        "tensor",
        scatter_dimension=0,
        tiled=True,
    ).astype(jnp.float32)
    live = part * local_rows + jnp.arange(local_rows, dtype=jnp.int32) < length
    return jnp.where(live[:, None], summed, 0.0).astype(jnp.bfloat16)[None]


def solution(mesh):
    placed = (
        P(("rep", "dp"), "tensor", None),
        P(),
        P(None, "tensor"),
        P(),
        P("tensor", None),
        P(("rep", "dp"), "tensor", None),
        P(("rep", "dp"), None),
        P(("rep", "dp")),
        P(("rep", "dp")),
    )
    pair = mesh.shape["tensor"] == 2 and mesh.shape["rep"] == 2 and mesh.shape["dp"] % 2 == 0
    body = pair_shards if pair else shards
    return jax.shard_map(
        body,
        mesh=mesh,
        in_specs=placed,
        out_specs=P(("rep", "dp"), "tensor", None),
        check_vma=False,
    )
```

```python
import functools
import math

import jax
import jax.numpy as jnp
from jax import lax
from jax.experimental import pallas as pl
from jax.experimental.pallas import tpu as pltpu
from jax.sharding import PartitionSpec as P

BF16 = jnp.bfloat16
F32 = jnp.float32
MASKED = -1e30
ANY = pl.ANY


def spec(space):
    return pl.BlockSpec(memory_space=space)


def rotation_tables(first, rows, step, head_size):
    column = jnp.arange(head_size, dtype=jnp.int32)
    within = (column // 2 * 2).astype(F32)
    inv_freq = jnp.exp(within * (-math.log(10000.0) / head_size))
    sign = jnp.where(column % 2 == 0, -1.0, 1.0).astype(F32)
    coarse = (first + step * jnp.arange(rows // step, dtype=jnp.int32)).astype(F32)
    fine = jnp.arange(step, dtype=jnp.int32).astype(F32)
    at = jnp.concatenate([coarse, fine])
    angle = at[:, None] * inv_freq[None, :]
    return jnp.cos(angle), jnp.sin(angle) * sign[None, :]


def fill_rotation(cos_t, sin_t, cos_s, sin_s, step):
    blocks = cos_s.shape[0] // step
    cf = cos_t[blocks:, :]
    sf = sin_t[blocks:, :]
    for u in range(blocks):
        cu = cos_t[u : u + 1, :]
        su = sin_t[u : u + 1, :]
        cos_s[u * step : (u + 1) * step, :] = cu * cf - su * sf
        sin_s[u * step : (u + 1) * step, :] = su * cf + cu * sf


def rotate(v, cos, sin, even):
    width = v.shape[1]
    swapped = jnp.where(even, pltpu.roll(v, width - 1, 1), pltpu.roll(v, 1, 1))
    return v * cos + swapped * sin


def score_factor(head_size):
    return math.log2(math.e) / math.sqrt(head_size)


def project_kernel(head_size, step, factor, tok, gain, wq, wkv, cos_t, sin_t, normed, q, kv, cos, sin):
    rows = tok.shape[0]
    tile = min(256, rows)
    fill_rotation(cos_t, sin_t, cos, sin, step)
    even = lax.broadcasted_iota(jnp.int32, (tile, head_size), 1) % 2 == 0
    for i in range(rows // tile):
        at = pl.ds(i * tile, tile)
        xf = tok[at, :].astype(F32)
        scale = lax.rsqrt(jnp.mean(xf * xf, axis=-1, keepdims=True) + 1e-06)
        nb = (xf * scale * gain[...]).astype(BF16)
        normed[at, :] = nb
        c = cos[at, :]
        s = sin[at, :]
        both = jnp.dot(nb, wkv[...], preferred_element_type=F32)
        kv[at, :head_size] = rotate(both[:, :head_size], c, s, even).astype(BF16)
        kv[at, head_size:] = both[:, head_size:].astype(BF16)
        for h in range(wq.shape[1] // head_size):
            cols = slice(h * head_size, (h + 1) * head_size)
            part = jnp.dot(nb, wq[:, cols], preferred_element_type=F32)
            q[at, cols] = (rotate(part, c, s, even) * factor).astype(BF16)


def project(tok, gain, wq, wkv, cos_t, sin_t, head_size, step):
    rows, width = tok.shape
    qc, kc = wq.shape[1], wkv.shape[1]
    return pl.pallas_call(
        functools.partial(project_kernel, head_size, step, score_factor(head_size)),
        out_shape=(
            jax.ShapeDtypeStruct((rows, width), BF16),
            jax.ShapeDtypeStruct((rows, qc), BF16),
            jax.ShapeDtypeStruct((rows, kc), BF16),
            jax.ShapeDtypeStruct((rows, head_size), F32),
            jax.ShapeDtypeStruct((rows, head_size), F32),
        ),
        in_specs=[spec(pltpu.VMEM)] * 6,
        out_specs=[spec(pltpu.VMEM)] * 5,
        compiler_params=pltpu.CompilerParams(vmem_limit_bytes=20 * 2**20),
        cost_estimate=pl.CostEstimate(
            flops=2 * rows * width * (qc + kc), bytes_accessed=10 * 2**20, transcendentals=0
        ),
        name="project_own",
    )(tok, gain.reshape(1, width), wq, wkv, cos_t, sin_t)


def other_kernel(head_size, factor, order, normed, w0, w1, w2, w3, cos, sin, q):
    rows = normed.shape[0]
    tile = min(256, rows)
    deep = w0.shape[0]
    even = lax.broadcasted_iota(jnp.int32, (tile, head_size), 1) % 2 == 0
    for i in range(rows // tile):
        at = pl.ds(i * tile, tile)
        c = cos[at, :]
        s = sin[at, :]
        for h in range(q.shape[1] // head_size):
            cols = slice(h * head_size, (h + 1) * head_size)
            total = None
            for n, w in enumerate((w0, w1, w2, w3)):
                x = normed[at, pl.ds(pl.multiple_of(order[n] * deep, 128), deep)]
                part = jnp.dot(x, w[:, cols], preferred_element_type=F32)
                total = part if total is None else total + part
            q[at, cols] = (rotate(total, c, s, even) * factor).astype(BF16)


def project_other(normed, pieces, order, cos, sin, head_size):
    rows, width = normed.shape
    qc = pieces[0].shape[1]
    return pl.pallas_call(
        functools.partial(other_kernel, head_size, score_factor(head_size)),
        out_shape=jax.ShapeDtypeStruct((rows, qc), BF16),
        in_specs=[spec(pltpu.SMEM)] + [spec(pltpu.VMEM)] * 7,
        out_specs=spec(pltpu.VMEM),
        compiler_params=pltpu.CompilerParams(vmem_limit_bytes=20 * 2**20),
        cost_estimate=pl.CostEstimate(
            flops=2 * rows * width * qc, bytes_accessed=6 * 2**20, transcendentals=0
        ),
        name="project_other",
    )(order, normed, *pieces, cos, sin)


def pick_kernel(idx, pool, keys, vals, sem):
    count, _, head_size = keys.shape
    copies = []
    for n, out in enumerate((keys, vals)):
        cols = pl.ds(n * head_size, head_size)
        for j in range(count):
            page = pool.at[idx[j], :, cols]
            copies.append(pltpu.make_async_copy(page, out.at[j], sem.at[n * count + j]))
    for c in copies:
        c.start()
    for c in copies:
        c.wait()


def pick(pool, idx):
    count = idx.shape[0]
    half = jax.ShapeDtypeStruct((count, pool.shape[1], pool.shape[2] // 2), pool.dtype)
    return pl.pallas_call(
        pick_kernel,
        out_shape=(half, half),
        in_specs=[spec(pltpu.SMEM), spec(ANY)],
        out_specs=[spec(pltpu.VMEM)] * 2,
        scratch_shapes=[pltpu.SemaphoreType.DMA((2 * count,))],
        compiler_params=pltpu.CompilerParams(vmem_limit_bytes=60 * 2**20),
        cost_estimate=pl.CostEstimate(flops=0, bytes_accessed=2**20, transcendentals=0),
        name="pick_pages",
    )(idx, pool)


def attend_kernel(
    head_size,
    info,
    qa_hbm,
    qb_hbm,
    k_mine,
    k_peer,
    v_mine,
    v_peer,
    kv_own,
    kv_peer,
    woa,
    wob0,
    wob1,
    out_hbm,
    qa,
    qb,
    keys,
    vals,
    wa,
    wb,
    mix,
    out,
    sbuf,
    pbuf,
    sums,
    tops,
    ksem,
    vsem,
    wsem,
    osem,
):
    part = info[0]
    length = info[1]
    rows, half = qa.shape
    pages, prow, _ = k_mine.shape
    page = 2 * prow
    width = out.shape[1]
    core = info[2]
    deep = wob0.shape[0]
    nheads = half // head_size
    window = pages * page

    def start(mine, peer, lo, dst, sem):
        cols = pl.ds(lo, head_size)
        for case in (0, 1):

            @pl.when(part == case)
            def _():
                skip = case * rows // page
                for u in range(skip, pages):
                    for src, side in ((mine, case), (peer, 1 - case)):
                        to = pl.ds((u - skip) * page + side * prow, prow)
                        pltpu.make_async_copy(src.at[u], dst.at[to, :], sem).start()
                if case == 1:
                    to = pl.ds(window - rows, rows)
                    pltpu.make_async_copy(kv_peer.at[:, cols], dst.at[to, :], sem).start()
                to = pl.ds(window, rows)
                pltpu.make_async_copy(kv_own.at[:, cols], dst.at[to, :], sem).start()

    def finish(dst, sem):
        pltpu.make_async_copy(dst, dst, sem).wait()

    queries = [
        pltpu.make_async_copy(qa_hbm, qa, wsem.at[3]),
        pltpu.make_async_copy(qb_hbm, qb, wsem.at[4]),
    ]
    queries[0].start()
    start(k_mine, k_peer, 0, keys, ksem)
    queries[1].start()
    start(v_mine, v_peer, head_size, vals, vsem)
    weights = [
        pltpu.make_async_copy(woa, wa, wsem.at[0]),
        pltpu.make_async_copy(wob0, wb.at[pl.ds(core * deep, deep), :], wsem.at[1]),
        pltpu.make_async_copy(wob1, wb.at[pl.ds((1 - core) * deep, deep), :], wsem.at[2]),
    ]
    tile = min(256, rows)
    span = window + tile
    lanes = 128
    gap = lax.broadcasted_iota(jnp.int32, (tile, tile), 1) - lax.broadcasted_iota(
        jnp.int32, (tile, tile), 0
    )
    order = [(i, n, h) for i in range(rows // tile) for n in range(2) for h in range(nheads)]

    def score(m):
        i, n, h = order[m]
        q = (qa, qb)[n][pl.ds(i * tile, tile), h * head_size : (h + 1) * head_size]
        top = None
        for lo in range(0, span, tile):
            s = lax.dot_general(
                q,
                keys[pl.ds(i * tile + lo, tile), :],
                (((1,), (1,)), ((), ())),
                preferred_element_type=F32,
            )
            if lo == 0:
                s = jnp.where(gap >= 1, s, MASKED)
            if lo + tile == span:
                s = jnp.where(gap <= 0, s, MASKED)
            sbuf[m % 2, :, lo : lo + tile] = s
            for at in range(0, tile, lanes):
                piece = s[:, at : at + lanes]
                top = piece if top is None else jnp.maximum(top, piece)
        top = jnp.max(top, axis=-1, keepdims=True)
        tops[m % 2] = jnp.broadcast_to(top, (tile, lanes))

    def soften(m):
        total = None
        for lo in range(0, span, lanes):
            e = jnp.exp2(sbuf[m % 2, :, lo : lo + lanes] - tops[m % 2])
            pbuf[m % 2, :, lo : lo + lanes] = e.astype(BF16)
            total = e if total is None else total + e
        total = jnp.sum(total, axis=-1, keepdims=True)
        sums[m % 2] = jnp.broadcast_to(1.0 / total, (tile, lanes))

    def combine(m):
        i, n, h = order[m]
        mixed = jnp.dot(
            pbuf[m % 2], vals[pl.ds(i * tile, span), :], preferred_element_type=F32
        )
        mixed = mixed * sums[m % 2, :, :1]
        at = pl.ds(i * tile, tile)
        mix[n, at, h * head_size : (h + 1) * head_size] = mixed.astype(BF16)

    block = 512

    def project_out(i, lo):
        at = pl.ds(i * tile, tile)
        row = part * rows + i * tile + lax.broadcasted_iota(jnp.int32, (tile, 1), 0)
        cols = slice(lo, lo + block)
        a = jnp.dot(mix[0, at, :], wa[:, cols], preferred_element_type=F32)
        b = jnp.dot(mix[1, at, :], wb[:, cols], preferred_element_type=F32)
        both = a.astype(BF16).astype(F32) + b.astype(BF16).astype(F32)
        out[at, cols] = jnp.where(row < length, both, 0.0).astype(BF16)

    stores = []

    def send_out(i):
        at = pl.ds(i * tile, tile)
        stores.append(pltpu.make_async_copy(out.at[at, :], out_hbm.at[at, :], osem.at[i]))
        stores[i].start()

    queries[0].wait()
    finish(keys, ksem)
    queries[1].wait()
    for c in weights:
        c.start()
    score(0)
    ready = []
    for m in range(len(order)):
        if m + 1 < len(order):
            score(m + 1)
        if m == 1:
            finish(vals, vsem)
        if m >= 1:
            combine(m - 1)
            i, n, h = order[m - 1]
            if (n, h) == (1, nheads - 1):
                if i == 0:
                    for c in weights:
                        c.wait()
                ready += [(i, lo) for lo in range(0, width, block)]
        if m >= 1 and ready and order[m - 1][1:] != (1, nheads - 1):
            i, lo = ready.pop(0)
            project_out(i, lo)
            if lo + block == width:
                send_out(i)
        soften(m)
    combine(len(order) - 1)
    if rows == tile:
        for c in weights:
            c.wait()
    ready += [(rows // tile - 1, lo) for lo in range(0, width, block)]
    for i, lo in ready:
        project_out(i, lo)
        if lo + block == width:
            send_out(i)
    for c in stores:
        c.wait()


def attend_pages(info, qa, qb, k_mine, k_peer, v_mine, v_peer, kv_own, kv_peer, woa, wobs):
    rows, half = qa.shape
    tile = min(256, rows)
    width = woa.shape[1]
    head_size = k_mine.shape[2]
    window = k_mine.shape[0] * k_mine.shape[1] * 2
    return pl.pallas_call(
        functools.partial(attend_kernel, head_size),
        out_shape=jax.ShapeDtypeStruct((rows, width), BF16),
        in_specs=[spec(pltpu.SMEM)]
        + [spec(ANY)] * 2
        + [spec(pltpu.VMEM)] * 4
        + [spec(ANY)] * 5,
        out_specs=spec(ANY),
        scratch_shapes=[
            pltpu.VMEM((rows, half), BF16),
            pltpu.VMEM((rows, half), BF16),
            pltpu.VMEM((window + rows, head_size), BF16),
            pltpu.VMEM((window + rows, head_size), BF16),
            pltpu.VMEM(woa.shape, BF16),
            pltpu.VMEM(woa.shape, BF16),
            pltpu.VMEM((2, rows, half), BF16),
            pltpu.VMEM((rows, width), BF16),
            pltpu.VMEM((2, tile, window + tile), F32),
            pltpu.VMEM((2, tile, window + tile), BF16),
            pltpu.VMEM((2, tile, 128), F32),
            pltpu.VMEM((2, tile, 128), F32),
            pltpu.SemaphoreType.DMA,
            pltpu.SemaphoreType.DMA,
            pltpu.SemaphoreType.DMA((5,)),
            pltpu.SemaphoreType.DMA((rows // tile,)),
        ],
        compiler_params=pltpu.CompilerParams(vmem_limit_bytes=56 * 2**20),
        cost_estimate=pl.CostEstimate(
            flops=4 * rows * 2 * half * (window + 256) + 4 * rows * half * width,
            bytes_accessed=12 * 2**20,
            transcendentals=rows * 6 * (window + 256),
        ),
        name="attend_and_out",
    )(info, qa, qb, k_mine, k_peer, v_mine, v_peer, kv_own, kv_peer, woa, *wobs)


def pair_shards(tokens, norm_gain, w_query, w_keyval, w_out, kv_pages, page_table, lengths, starts):
    head_size = w_keyval.shape[1] // 2
    part = lax.axis_index("tensor")
    rep = lax.axis_index("rep")
    dp = lax.axis_index("dp")
    ndp = lax.axis_size("dp")
    core = dp % 2
    rows = tokens.shape[1]
    swap = [(0, 1), (1, 0)]
    cores = [(i, i ^ 1) for i in range(ndp)]

    pool = lax.all_gather(kv_pages, "dp", axis=0, tiled=True)

    def peer_rows(w, at, parts):
        deep = w.shape[0] // parts
        return lax.ppermute(lax.dynamic_slice_in_dim(w, at * deep, deep, 0), "tensor", swap)

    step = 32
    cos_t, sin_t = rotation_tables(starts[0] + part * rows, rows, step, head_size)
    normed, qa, kv_own, cos, sin = project(
        tokens[0], norm_gain, w_query, w_keyval, cos_t, sin_t, head_size, step
    )

    a = peer_rows(w_query, rep * 2 + core, 4)
    a, kv_own, w_out_late, page_table = lax.optimization_barrier((a, kv_own, w_out, page_table))
    b = lax.ppermute(a, "rep", swap)
    c = peer_rows(w_out_late, core, 2)
    table = page_table[0]
    peer_table = lax.ppermute(table, "rep", swap)
    wq_pieces = (a, b, lax.ppermute(a, "dp", cores), lax.ppermute(b, "dp", cores))
    order = jnp.stack(
        [rep * 2 + core, (1 - rep) * 2 + core, rep * 2 + 1 - core, (1 - rep) * 2 + 1 - core]
    ).astype(jnp.int32)
    qb = project_other(normed, wq_pieces, order, cos, sin, head_size)
    c, qb, kv_own = lax.optimization_barrier((c, qb, kv_own))
    wo_pieces = (c, lax.ppermute(c, "dp", cores))
    kv_peer = lax.ppermute(kv_own, "tensor", swap)

    per_rep = kv_pages.shape[0] * ndp
    home = table[0] // per_rep == rep
    own_at, peer_at = table % per_rep, peer_table % per_rep
    wo_pieces, pool, own_at, peer_at = lax.optimization_barrier(
        (wo_pieces, pool, own_at, peer_at)
    )
    k_sent, v_sent = pick(pool, peer_at)
    k_came = lax.ppermute(k_sent, "rep", swap)
    v_came = lax.ppermute(v_sent, "rep", swap)
    k_held, v_held = pick(pool, own_at)
    k_came, kv_peer, k_held = lax.optimization_barrier((k_came, kv_peer, k_held))
    k_mine = jnp.where(home, k_held, k_came)
    k_peer = lax.ppermute(k_mine, "tensor", swap)
    v_mine = jnp.where(home, v_held, v_came)
    v_peer = lax.ppermute(v_mine, "tensor", swap)

    info = jnp.stack([part, lengths[0], core]).astype(jnp.int32)
    return attend_pages(
        info, qa, qb, k_mine, k_peer, v_mine, v_peer, kv_own, kv_peer, w_out, wo_pieces
    )[None]


def rotate_pairs(values, positions, columns_from, head_size):
    rows, cols = values.shape
    column = columns_from + jnp.arange(cols // 2, dtype=jnp.int32) * 2
    within = (column % head_size).astype(jnp.float32)
    inv_freq = jnp.exp(within * (-math.log(10000.0) / head_size))
    angle = positions[:, None] * inv_freq[None, :]
    cosine = jnp.cos(angle)
    sine = jnp.sin(angle)
    pairs = values.reshape(rows, cols // 2, 2)
    first = pairs[:, :, 0]
    second = pairs[:, :, 1]
    turned = jnp.stack([first * cosine - second * sine, first * sine + second * cosine], axis=-1)
    return turned.reshape(rows, cols)


def attend(query, keys, values, first_row, heads, head_size, window):
    rows = query.shape[0]
    count = keys.shape[0]
    q_heads = query.reshape(rows, heads, head_size)
    scores = jnp.einsum("rhd,kd->hrk", q_heads, keys, preferred_element_type=jnp.float32) * (
        1.0 / math.sqrt(head_size)
    )
    row_ids = first_row + jnp.arange(rows, dtype=jnp.int32)
    key_ids = jnp.arange(count, dtype=jnp.int32)
    seen = (key_ids[None, :] >= row_ids[:, None] + 1) & (
        key_ids[None, :] <= row_ids[:, None] + window
    )
    scores = jnp.where(seen[None, :, :], scores, -1e30)
    top = jnp.max(scores, axis=-1, keepdims=True)
    expd = jnp.exp(scores - top)
    total = jnp.sum(expd, axis=-1, keepdims=True)
    probs = (expd / total).astype(jnp.bfloat16)
    mixed = jnp.einsum("hrk,kd->rhd", probs, values, preferred_element_type=jnp.float32)
    return mixed.reshape(rows, heads * head_size).astype(jnp.bfloat16)


def shards(tokens, norm_gain, w_query, w_keyval, w_out, kv_pages, page_table, lengths, starts):
    width = tokens.shape[2]
    head_size = w_keyval.shape[1] // 2
    heads = width // head_size
    part = lax.axis_index("tensor")
    local_rows = tokens.shape[1]
    q_cols = w_query.shape[1]
    start = starts[0]
    length = lengths[0]
    xf = tokens[0].astype(jnp.float32)
    scale = lax.rsqrt(jnp.mean(xf * xf, axis=-1, keepdims=True) + 1e-06)
    normed = (xf * scale * norm_gain).astype(jnp.bfloat16)
    piece = lax.all_gather(normed, "tensor", axis=0, tiled=True)
    positions = (start + jnp.arange(piece.shape[0], dtype=jnp.int32)).astype(jnp.float32)
    query = rotate_pairs(
        jnp.dot(piece, w_query, preferred_element_type=jnp.float32),
        positions,
        part * q_cols,
        head_size,
    )
    keyval = jnp.dot(piece, w_keyval, preferred_element_type=jnp.float32)
    new_keys = rotate_pairs(keyval[:, :head_size], positions, 0, head_size)
    projected = jnp.concatenate([query, new_keys, keyval[:, head_size:]], axis=1).astype(
        jnp.bfloat16
    )
    query_cols = projected[:, :q_cols]
    keys_new = projected[:, q_cols : q_cols + head_size]
    values_new = projected[:, q_cols + head_size :]
    query = lax.all_to_all(query_cols, "tensor", split_axis=0, concat_axis=1, tiled=True)
    table = page_table[0]
    piece = lax.all_gather(kv_pages, ("rep", "dp"), axis=0, tiled=True)
    ident = jnp.arange(piece.shape[0], dtype=jnp.int32)
    onehot = (table[:, None] == ident[None, :]).astype(jnp.bfloat16)
    picked = jnp.einsum("cn,nrk->crk", onehot, piece, preferred_element_type=jnp.float32)
    window_pages = lax.all_gather(picked.astype(jnp.bfloat16), "tensor", axis=1, tiled=True)
    cached = window_pages.reshape(-1, 2 * head_size)
    window = cached.shape[0]
    keys = jnp.concatenate([cached[:, :head_size], keys_new], axis=0)
    values = jnp.concatenate([cached[:, head_size:], values_new], axis=0)
    mixed = attend(query, keys, values, part * local_rows, heads, head_size, window)
    mixed_cols = lax.all_to_all(mixed, "tensor", split_axis=1, concat_axis=0, tiled=True)
    summed = lax.psum_scatter(
        jnp.dot(mixed_cols, w_out, preferred_element_type=jnp.float32).astype(jnp.bfloat16),
        "tensor",
        scatter_dimension=0,
        tiled=True,
    ).astype(jnp.float32)
    live = part * local_rows + jnp.arange(local_rows, dtype=jnp.int32) < length
    return jnp.where(live[:, None], summed, 0.0).astype(jnp.bfloat16)[None]


def solution(mesh):
    placed = (
        P(("rep", "dp"), "tensor", None),
        P(),
        P(None, "tensor"),
        P(),
        P("tensor", None),
        P(("rep", "dp"), "tensor", None),
        P(("rep", "dp"), None),
        P(("rep", "dp")),
        P(("rep", "dp")),
    )
    pair = mesh.shape["tensor"] == 2 and mesh.shape["rep"] == 2 and mesh.shape["dp"] % 2 == 0
    body = pair_shards if pair else shards
    return jax.shard_map(
        body,
        mesh=mesh,
        in_specs=placed,
        out_specs=P(("rep", "dp"), "tensor", None),
        check_vma=False,
    )
```

```python
import functools
import math

import jax
import jax.numpy as jnp
from jax import lax
from jax.experimental import pallas as pl
from jax.experimental.pallas import tpu as pltpu
from jax.sharding import PartitionSpec as P

BF16 = jnp.bfloat16
F32 = jnp.float32
MASKED = -1e30
ANY = pl.ANY


def spec(space):
    return pl.BlockSpec(memory_space=space)


def rotation_tables(first, rows, step, head_size):
    column = jnp.arange(head_size, dtype=jnp.int32)
    within = (column // 2 * 2).astype(F32)
    inv_freq = jnp.exp(within * (-math.log(10000.0) / head_size))
    sign = jnp.where(column % 2 == 0, -1.0, 1.0).astype(F32)
    coarse = (first + step * jnp.arange(rows // step, dtype=jnp.int32)).astype(F32)
    fine = jnp.arange(step, dtype=jnp.int32).astype(F32)
    at = jnp.concatenate([coarse, fine])
    angle = at[:, None] * inv_freq[None, :]
    return jnp.cos(angle), jnp.sin(angle) * sign[None, :]


def fill_rotation(cos_t, sin_t, cos_s, sin_s, step):
    blocks = cos_s.shape[0] // step
    cf = cos_t[blocks:, :]
    sf = sin_t[blocks:, :]
    for u in range(blocks):
        cu = cos_t[u : u + 1, :]
        su = sin_t[u : u + 1, :]
        cos_s[u * step : (u + 1) * step, :] = cu * cf - su * sf
        sin_s[u * step : (u + 1) * step, :] = su * cf + cu * sf


def rotate(v, cos, sin, even):
    width = v.shape[1]
    swapped = jnp.where(even, pltpu.roll(v, width - 1, 1), pltpu.roll(v, 1, 1))
    return v * cos + swapped * sin


def score_factor(head_size):
    return math.log2(math.e) / math.sqrt(head_size)


def project_kernel(head_size, step, factor, tok, gain, wq, wkv, cos_t, sin_t, normed, q, kv, cos, sin):
    rows = tok.shape[0]
    tile = min(256, rows)
    fill_rotation(cos_t, sin_t, cos, sin, step)
    even = lax.broadcasted_iota(jnp.int32, (tile, head_size), 1) % 2 == 0
    for i in range(rows // tile):
        at = pl.ds(i * tile, tile)
        xf = tok[at, :].astype(F32)
        scale = lax.rsqrt(jnp.mean(xf * xf, axis=-1, keepdims=True) + 1e-06)
        nb = (xf * scale * gain[...]).astype(BF16)
        normed[at, :] = nb
        c = cos[at, :]
        s = sin[at, :]
        both = jnp.dot(nb, wkv[...], preferred_element_type=F32)
        kv[at, :head_size] = rotate(both[:, :head_size], c, s, even).astype(BF16)
        kv[at, head_size:] = both[:, head_size:].astype(BF16)
        for h in range(wq.shape[1] // head_size):
            cols = slice(h * head_size, (h + 1) * head_size)
            part = jnp.dot(nb, wq[:, cols], preferred_element_type=F32)
            q[at, cols] = (rotate(part, c, s, even) * factor).astype(BF16)


def project(tok, gain, wq, wkv, cos_t, sin_t, head_size, step):
    rows, width = tok.shape
    qc, kc = wq.shape[1], wkv.shape[1]
    return pl.pallas_call(
        functools.partial(project_kernel, head_size, step, score_factor(head_size)),
        out_shape=(
            jax.ShapeDtypeStruct((rows, width), BF16),
            jax.ShapeDtypeStruct((rows, qc), BF16),
            jax.ShapeDtypeStruct((rows, kc), BF16),
            jax.ShapeDtypeStruct((rows, head_size), F32),
            jax.ShapeDtypeStruct((rows, head_size), F32),
        ),
        in_specs=[spec(pltpu.VMEM)] * 6,
        out_specs=[spec(pltpu.VMEM)] * 5,
        compiler_params=pltpu.CompilerParams(vmem_limit_bytes=20 * 2**20),
        cost_estimate=pl.CostEstimate(
            flops=2 * rows * width * (qc + kc), bytes_accessed=10 * 2**20, transcendentals=0
        ),
        name="project_own",
    )(tok, gain.reshape(1, width), wq, wkv, cos_t, sin_t)


def other_kernel(head_size, factor, order, normed, w0, w1, w2, w3, cos, sin, q):
    rows = normed.shape[0]
    tile = min(256, rows)
    deep = w0.shape[0]
    even = lax.broadcasted_iota(jnp.int32, (tile, head_size), 1) % 2 == 0
    for i in range(rows // tile):
        at = pl.ds(i * tile, tile)
        c = cos[at, :]
        s = sin[at, :]
        for h in range(q.shape[1] // head_size):
            cols = slice(h * head_size, (h + 1) * head_size)
            total = None
            for n, w in enumerate((w0, w1, w2, w3)):
                x = normed[at, pl.ds(pl.multiple_of(order[n] * deep, 128), deep)]
                part = jnp.dot(x, w[:, cols], preferred_element_type=F32)
                total = part if total is None else total + part
            q[at, cols] = (rotate(total, c, s, even) * factor).astype(BF16)


def project_other(normed, pieces, order, cos, sin, head_size):
    rows, width = normed.shape
    qc = pieces[0].shape[1]
    return pl.pallas_call(
        functools.partial(other_kernel, head_size, score_factor(head_size)),
        out_shape=jax.ShapeDtypeStruct((rows, qc), BF16),
        in_specs=[spec(pltpu.SMEM)] + [spec(pltpu.VMEM)] * 7,
        out_specs=spec(pltpu.VMEM),
        compiler_params=pltpu.CompilerParams(vmem_limit_bytes=20 * 2**20),
        cost_estimate=pl.CostEstimate(
            flops=2 * rows * width * qc, bytes_accessed=6 * 2**20, transcendentals=0
        ),
        name="project_other",
    )(order, normed, *pieces, cos, sin)


def pick_kernel(idx, pool, keys, vals, sem):
    count, _, head_size = keys.shape
    copies = []
    for n, out in enumerate((keys, vals)):
        cols = pl.ds(n * head_size, head_size)
        for j in range(count):
            page = pool.at[idx[j], :, cols]
            copies.append(pltpu.make_async_copy(page, out.at[j], sem.at[n * count + j]))
    for c in copies:
        c.start()
    for c in copies:
        c.wait()


def pick(pool, idx):
    count = idx.shape[0]
    half = jax.ShapeDtypeStruct((count, pool.shape[1], pool.shape[2] // 2), pool.dtype)
    return pl.pallas_call(
        pick_kernel,
        out_shape=(half, half),
        in_specs=[spec(pltpu.SMEM), spec(ANY)],
        out_specs=[spec(pltpu.VMEM)] * 2,
        scratch_shapes=[pltpu.SemaphoreType.DMA((2 * count,))],
        compiler_params=pltpu.CompilerParams(vmem_limit_bytes=60 * 2**20),
        cost_estimate=pl.CostEstimate(flops=0, bytes_accessed=2**20, transcendentals=0),
        name="pick_pages",
    )(idx, pool)


def hold_kernel(info, qa, qb, own, peer, woa, wob0, wob1, qa_v, qb_v, own_v, peer_v, wa, wb, sem):
    core = info[2]
    deep = wob0.shape[0]
    moves = [
        (woa, wa),
        (wob0, wb.at[pl.ds(core * deep, deep), :]),
        (wob1, wb.at[pl.ds((1 - core) * deep, deep), :]),
        (qa, qa_v),
        (qb, qb_v),
        (own, own_v),
        (peer, peer_v),
    ]
    copies = [pltpu.make_async_copy(a, b, sem.at[n]) for n, (a, b) in enumerate(moves)]
    for c in copies:
        c.start()
    for c in copies:
        c.wait()


def hold(info, qa, qb, kv_own, kv_peer, woa, wobs):
    kept = (qa, qb, kv_own, kv_peer, woa, woa)
    return pl.pallas_call(
        hold_kernel,
        out_shape=[jax.ShapeDtypeStruct(x.shape, x.dtype) for x in kept],
        in_specs=[spec(pltpu.SMEM)] + [spec(ANY)] * 7,
        out_specs=[spec(pltpu.VMEM)] * 6,
        scratch_shapes=[pltpu.SemaphoreType.DMA((7,))],
        compiler_params=pltpu.CompilerParams(vmem_limit_bytes=16 * 2**20),
        cost_estimate=pl.CostEstimate(flops=0, bytes_accessed=8 * 2**20, transcendentals=0),
        name="hold",
    )(info, qa, qb, kv_own, kv_peer, woa, *wobs)


def attend_kernel(
    head_size,
    info,
    qa,
    qb,
    k_mine,
    k_peer,
    v_mine,
    v_peer,
    kv_own,
    kv_peer,
    wa,
    wb,
    out_hbm,
    keys,
    vals,
    mix,
    out,
    sbuf,
    pbuf,
    sums,
    tops,
    ksem,
    vsem,
    osem,
):
    part = info[0]
    length = info[1]
    rows, half = qa.shape
    pages, prow, _ = k_mine.shape
    page = 2 * prow
    width = out.shape[1]
    nheads = half // head_size
    window = pages * page

    def start(mine, peer, lo, dst, sem):
        cols = pl.ds(lo, head_size)
        for case in (0, 1):

            @pl.when(part == case)
            def _():
                skip = case * rows // page
                for u in range(skip, pages):
                    for src, side in ((mine, case), (peer, 1 - case)):
                        to = pl.ds((u - skip) * page + side * prow, prow)
                        pltpu.make_async_copy(src.at[u], dst.at[to, :], sem).start()
                if case == 1:
                    to = pl.ds(window - rows, rows)
                    pltpu.make_async_copy(kv_peer.at[:, cols], dst.at[to, :], sem).start()
                to = pl.ds(window, rows)
                pltpu.make_async_copy(kv_own.at[:, cols], dst.at[to, :], sem).start()

    def finish(dst, sem):
        pltpu.make_async_copy(dst, dst, sem).wait()

    start(k_mine, k_peer, 0, keys, ksem)
    start(v_mine, v_peer, head_size, vals, vsem)
    tile = min(256, rows)
    span = window + tile
    lanes = 128
    gap = lax.broadcasted_iota(jnp.int32, (tile, tile), 1) - lax.broadcasted_iota(
        jnp.int32, (tile, tile), 0
    )
    order = [(i, n, h) for i in range(rows // tile) for n in range(2) for h in range(nheads)]

    def score(m):
        i, n, h = order[m]
        q = (qa, qb)[n][pl.ds(i * tile, tile), h * head_size : (h + 1) * head_size]
        top = None
        for lo in range(0, span, tile):
            s = lax.dot_general(
                q,
                keys[pl.ds(i * tile + lo, tile), :],
                (((1,), (1,)), ((), ())),
                preferred_element_type=F32,
            )
            if lo == 0:
                s = jnp.where(gap >= 1, s, MASKED)
            if lo + tile == span:
                s = jnp.where(gap <= 0, s, MASKED)
            sbuf[m % 2, :, lo : lo + tile] = s
            for at in range(0, tile, lanes):
                piece = s[:, at : at + lanes]
                top = piece if top is None else jnp.maximum(top, piece)
        top = jnp.max(top, axis=-1, keepdims=True)
        tops[m % 2] = jnp.broadcast_to(top, (tile, lanes))

    def soften(m):
        total = None
        for lo in range(0, span, lanes):
            e = jnp.exp2(sbuf[m % 2, :, lo : lo + lanes] - tops[m % 2])
            pbuf[m % 2, :, lo : lo + lanes] = e.astype(BF16)
            total = e if total is None else total + e
        total = jnp.sum(total, axis=-1, keepdims=True)
        sums[m % 2] = jnp.broadcast_to(1.0 / total, (tile, lanes))

    def combine(m):
        i, n, h = order[m]
        mixed = jnp.dot(
            pbuf[m % 2], vals[pl.ds(i * tile, span), :], preferred_element_type=F32
        )
        mixed = mixed * sums[m % 2, :, :1]
        at = pl.ds(i * tile, tile)
        mix[n, at, h * head_size : (h + 1) * head_size] = mixed.astype(BF16)

    block = 512

    def project_out(i, lo):
        at = pl.ds(i * tile, tile)
        row = part * rows + i * tile + lax.broadcasted_iota(jnp.int32, (tile, 1), 0)
        cols = slice(lo, lo + block)
        a = jnp.dot(mix[0, at, :], wa[:, cols], preferred_element_type=F32)
        b = jnp.dot(mix[1, at, :], wb[:, cols], preferred_element_type=F32)
        both = a.astype(BF16).astype(F32) + b.astype(BF16).astype(F32)
        out[at, cols] = jnp.where(row < length, both, 0.0).astype(BF16)

    stores = []

    def send_out(i):
        at = pl.ds(i * tile, tile)
        stores.append(pltpu.make_async_copy(out.at[at, :], out_hbm.at[at, :], osem.at[i]))
        stores[i].start()

    finish(keys, ksem)
    score(0)
    ready = []
    for m in range(len(order)):
        if m + 1 < len(order):
            score(m + 1)
        if m == 1:
            finish(vals, vsem)
        if m >= 1:
            combine(m - 1)
            i, n, h = order[m - 1]
            if (n, h) == (1, nheads - 1):
                ready += [(i, lo) for lo in range(0, width, block)]
        if m >= 1 and ready and order[m - 1][1:] != (1, nheads - 1):
            i, lo = ready.pop(0)
            project_out(i, lo)
            if lo + block == width:
                send_out(i)
        soften(m)
    combine(len(order) - 1)
    ready += [(rows // tile - 1, lo) for lo in range(0, width, block)]
    for i, lo in ready:
        project_out(i, lo)
        if lo + block == width:
            send_out(i)
    for c in stores:
        c.wait()


def attend_pages(info, qa, qb, k_mine, k_peer, v_mine, v_peer, kv_own, kv_peer, wa, wb):
    rows, half = qa.shape
    tile = min(256, rows)
    width = wa.shape[1]
    head_size = k_mine.shape[2]
    window = k_mine.shape[0] * k_mine.shape[1] * 2
    return pl.pallas_call(
        functools.partial(attend_kernel, head_size),
        out_shape=jax.ShapeDtypeStruct((rows, width), BF16),
        in_specs=[spec(pltpu.SMEM)] + [spec(pltpu.VMEM)] * 10,
        out_specs=spec(ANY),
        scratch_shapes=[
            pltpu.VMEM((window + rows, head_size), BF16),
            pltpu.VMEM((window + rows, head_size), BF16),
            pltpu.VMEM((2, rows, half), BF16),
            pltpu.VMEM((rows, width), BF16),
            pltpu.VMEM((2, tile, window + tile), F32),
            pltpu.VMEM((2, tile, window + tile), BF16),
            pltpu.VMEM((2, tile, 128), F32),
            pltpu.VMEM((2, tile, 128), F32),
            pltpu.SemaphoreType.DMA,
            pltpu.SemaphoreType.DMA,
            pltpu.SemaphoreType.DMA((rows // tile,)),
        ],
        compiler_params=pltpu.CompilerParams(vmem_limit_bytes=30 * 2**20),
        cost_estimate=pl.CostEstimate(
            flops=4 * rows * 2 * half * (window + 256) + 4 * rows * half * width,
            bytes_accessed=12 * 2**20,
            transcendentals=rows * 6 * (window + 256),
        ),
        name="attend_and_out",
    )(info, qa, qb, k_mine, k_peer, v_mine, v_peer, kv_own, kv_peer, wa, wb)


def pair_shards(tokens, norm_gain, w_query, w_keyval, w_out, kv_pages, page_table, lengths, starts):
    head_size = w_keyval.shape[1] // 2
    part = lax.axis_index("tensor")
    rep = lax.axis_index("rep")
    dp = lax.axis_index("dp")
    ndp = lax.axis_size("dp")
    core = dp % 2
    rows = tokens.shape[1]
    swap = [(0, 1), (1, 0)]
    cores = [(i, i ^ 1) for i in range(ndp)]

    pool = lax.all_gather(kv_pages, "dp", axis=0, tiled=True)

    def peer_rows(w, at, parts):
        deep = w.shape[0] // parts
        return lax.ppermute(lax.dynamic_slice_in_dim(w, at * deep, deep, 0), "tensor", swap)

    step = 32
    cos_t, sin_t = rotation_tables(starts[0] + part * rows, rows, step, head_size)
    normed, qa, kv_own, cos, sin = project(
        tokens[0], norm_gain, w_query, w_keyval, cos_t, sin_t, head_size, step
    )

    a = peer_rows(w_query, rep * 2 + core, 4)
    a, kv_own, w_out_late, page_table = lax.optimization_barrier((a, kv_own, w_out, page_table))
    b = lax.ppermute(a, "rep", swap)
    c = peer_rows(w_out_late, core, 2)
    table = page_table[0]
    peer_table = lax.ppermute(table, "rep", swap)
    wq_pieces = (a, b, lax.ppermute(a, "dp", cores), lax.ppermute(b, "dp", cores))
    order = jnp.stack(
        [rep * 2 + core, (1 - rep) * 2 + core, rep * 2 + 1 - core, (1 - rep) * 2 + 1 - core]
    ).astype(jnp.int32)
    qb = project_other(normed, wq_pieces, order, cos, sin, head_size)
    c, qb, kv_own = lax.optimization_barrier((c, qb, kv_own))
    wo_pieces = (c, lax.ppermute(c, "dp", cores))
    kv_peer = lax.ppermute(kv_own, "tensor", swap)

    per_rep = kv_pages.shape[0] * ndp
    home = table[0] // per_rep == rep
    own_at, peer_at = table % per_rep, peer_table % per_rep
    wo_pieces, pool, own_at, peer_at = lax.optimization_barrier(
        (wo_pieces, pool, own_at, peer_at)
    )
    k_sent, v_sent = pick(pool, peer_at)
    k_came = lax.ppermute(k_sent, "rep", swap)
    v_came = lax.ppermute(v_sent, "rep", swap)
    k_held, v_held = pick(pool, own_at)
    k_came, kv_peer, k_held = lax.optimization_barrier((k_came, kv_peer, k_held))
    k_mine = jnp.where(home, k_held, k_came)
    k_peer = lax.ppermute(k_mine, "tensor", swap)
    v_mine = jnp.where(home, v_held, v_came)
    v_peer = lax.ppermute(v_mine, "tensor", swap)

    info = jnp.stack([part, lengths[0], core]).astype(jnp.int32)
    info, k_mine = lax.optimization_barrier((info, k_mine))
    qa, qb, kv_own, kv_peer, wa, wb = hold(info, qa, qb, kv_own, kv_peer, w_out, wo_pieces)
    return attend_pages(
        info, qa, qb, k_mine, k_peer, v_mine, v_peer, kv_own, kv_peer, wa, wb
    )[None]


def rotate_pairs(values, positions, columns_from, head_size):
    rows, cols = values.shape
    column = columns_from + jnp.arange(cols // 2, dtype=jnp.int32) * 2
    within = (column % head_size).astype(jnp.float32)
    inv_freq = jnp.exp(within * (-math.log(10000.0) / head_size))
    angle = positions[:, None] * inv_freq[None, :]
    cosine = jnp.cos(angle)
    sine = jnp.sin(angle)
    pairs = values.reshape(rows, cols // 2, 2)
    first = pairs[:, :, 0]
    second = pairs[:, :, 1]
    turned = jnp.stack([first * cosine - second * sine, first * sine + second * cosine], axis=-1)
    return turned.reshape(rows, cols)


def attend(query, keys, values, first_row, heads, head_size, window):
    rows = query.shape[0]
    count = keys.shape[0]
    q_heads = query.reshape(rows, heads, head_size)
    scores = jnp.einsum("rhd,kd->hrk", q_heads, keys, preferred_element_type=jnp.float32) * (
        1.0 / math.sqrt(head_size)
    )
    row_ids = first_row + jnp.arange(rows, dtype=jnp.int32)
    key_ids = jnp.arange(count, dtype=jnp.int32)
    seen = (key_ids[None, :] >= row_ids[:, None] + 1) & (
        key_ids[None, :] <= row_ids[:, None] + window
    )
    scores = jnp.where(seen[None, :, :], scores, -1e30)
    top = jnp.max(scores, axis=-1, keepdims=True)
    expd = jnp.exp(scores - top)
    total = jnp.sum(expd, axis=-1, keepdims=True)
    probs = (expd / total).astype(jnp.bfloat16)
    mixed = jnp.einsum("hrk,kd->rhd", probs, values, preferred_element_type=jnp.float32)
    return mixed.reshape(rows, heads * head_size).astype(jnp.bfloat16)


def shards(tokens, norm_gain, w_query, w_keyval, w_out, kv_pages, page_table, lengths, starts):
    width = tokens.shape[2]
    head_size = w_keyval.shape[1] // 2
    heads = width // head_size
    part = lax.axis_index("tensor")
    local_rows = tokens.shape[1]
    q_cols = w_query.shape[1]
    start = starts[0]
    length = lengths[0]
    xf = tokens[0].astype(jnp.float32)
    scale = lax.rsqrt(jnp.mean(xf * xf, axis=-1, keepdims=True) + 1e-06)
    normed = (xf * scale * norm_gain).astype(jnp.bfloat16)
    piece = lax.all_gather(normed, "tensor", axis=0, tiled=True)
    positions = (start + jnp.arange(piece.shape[0], dtype=jnp.int32)).astype(jnp.float32)
    query = rotate_pairs(
        jnp.dot(piece, w_query, preferred_element_type=jnp.float32),
        positions,
        part * q_cols,
        head_size,
    )
    keyval = jnp.dot(piece, w_keyval, preferred_element_type=jnp.float32)
    new_keys = rotate_pairs(keyval[:, :head_size], positions, 0, head_size)
    projected = jnp.concatenate([query, new_keys, keyval[:, head_size:]], axis=1).astype(
        jnp.bfloat16
    )
    query_cols = projected[:, :q_cols]
    keys_new = projected[:, q_cols : q_cols + head_size]
    values_new = projected[:, q_cols + head_size :]
    query = lax.all_to_all(query_cols, "tensor", split_axis=0, concat_axis=1, tiled=True)
    table = page_table[0]
    piece = lax.all_gather(kv_pages, ("rep", "dp"), axis=0, tiled=True)
    ident = jnp.arange(piece.shape[0], dtype=jnp.int32)
    onehot = (table[:, None] == ident[None, :]).astype(jnp.bfloat16)
    picked = jnp.einsum("cn,nrk->crk", onehot, piece, preferred_element_type=jnp.float32)
    window_pages = lax.all_gather(picked.astype(jnp.bfloat16), "tensor", axis=1, tiled=True)
    cached = window_pages.reshape(-1, 2 * head_size)
    window = cached.shape[0]
    keys = jnp.concatenate([cached[:, :head_size], keys_new], axis=0)
    values = jnp.concatenate([cached[:, head_size:], values_new], axis=0)
    mixed = attend(query, keys, values, part * local_rows, heads, head_size, window)
    mixed_cols = lax.all_to_all(mixed, "tensor", split_axis=1, concat_axis=0, tiled=True)
    summed = lax.psum_scatter(
        jnp.dot(mixed_cols, w_out, preferred_element_type=jnp.float32).astype(jnp.bfloat16),
        "tensor",
        scatter_dimension=0,
        tiled=True,
    ).astype(jnp.float32)
    live = part * local_rows + jnp.arange(local_rows, dtype=jnp.int32) < length
    return jnp.where(live[:, None], summed, 0.0).astype(jnp.bfloat16)[None]


def solution(mesh):
    placed = (
        P(("rep", "dp"), "tensor", None),
        P(),
        P(None, "tensor"),
        P(),
        P("tensor", None),
        P(("rep", "dp"), "tensor", None),
        P(("rep", "dp"), None),
        P(("rep", "dp")),
        P(("rep", "dp")),
    )
    pair = mesh.shape["tensor"] == 2 and mesh.shape["rep"] == 2 and mesh.shape["dp"] % 2 == 0
    body = pair_shards if pair else shards
    return jax.shard_map(
        body,
        mesh=mesh,
        in_specs=placed,
        out_specs=P(("rep", "dp"), "tensor", None),
        check_vma=False,
    )
```

```python
import functools
import math

import jax
import jax.numpy as jnp
from jax import lax
from jax.experimental import pallas as pl
from jax.experimental.pallas import tpu as pltpu
from jax.sharding import PartitionSpec as P

BF16 = jnp.bfloat16
F32 = jnp.float32
MASKED = -1e30
ANY = pl.ANY


def spec(space):
    return pl.BlockSpec(memory_space=space)


def rotation_tables(first, rows, step, head_size):
    column = jnp.arange(head_size, dtype=jnp.int32)
    within = (column // 2 * 2).astype(F32)
    inv_freq = jnp.exp(within * (-math.log(10000.0) / head_size))
    sign = jnp.where(column % 2 == 0, -1.0, 1.0).astype(F32)
    coarse = (first + step * jnp.arange(rows // step, dtype=jnp.int32)).astype(F32)
    fine = jnp.arange(step, dtype=jnp.int32).astype(F32)
    at = jnp.concatenate([coarse, fine])
    angle = at[:, None] * inv_freq[None, :]
    return jnp.cos(angle), jnp.sin(angle) * sign[None, :]


def fill_rotation(cos_t, sin_t, cos_s, sin_s, step):
    blocks = cos_s.shape[0] // step
    cf = cos_t[blocks:, :]
    sf = sin_t[blocks:, :]
    for u in range(blocks):
        cu = cos_t[u : u + 1, :]
        su = sin_t[u : u + 1, :]
        cos_s[u * step : (u + 1) * step, :] = cu * cf - su * sf
        sin_s[u * step : (u + 1) * step, :] = su * cf + cu * sf


def rotate(v, cos, sin, even):
    width = v.shape[1]
    swapped = jnp.where(even, pltpu.roll(v, width - 1, 1), pltpu.roll(v, 1, 1))
    return v * cos + swapped * sin


def score_factor(head_size):
    return math.log2(math.e) / math.sqrt(head_size)


def project_kernel(head_size, step, factor, tok, gain, wq, wkv, cos_t, sin_t, normed, q, kv, cos, sin):
    rows = tok.shape[0]
    tile = min(256, rows)
    fill_rotation(cos_t, sin_t, cos, sin, step)
    even = lax.broadcasted_iota(jnp.int32, (tile, head_size), 1) % 2 == 0
    for i in range(rows // tile):
        at = pl.ds(i * tile, tile)
        xf = tok[at, :].astype(F32)
        scale = lax.rsqrt(jnp.mean(xf * xf, axis=-1, keepdims=True) + 1e-06)
        nb = (xf * scale * gain[...]).astype(BF16)
        normed[at, :] = nb
        c = cos[at, :]
        s = sin[at, :]
        both = jnp.dot(nb, wkv[...], preferred_element_type=F32)
        kv[at, :head_size] = rotate(both[:, :head_size], c, s, even).astype(BF16)
        kv[at, head_size:] = both[:, head_size:].astype(BF16)
        for h in range(wq.shape[1] // head_size):
            cols = slice(h * head_size, (h + 1) * head_size)
            part = jnp.dot(nb, wq[:, cols], preferred_element_type=F32)
            q[at, cols] = (rotate(part, c, s, even) * factor).astype(BF16)


def project(tok, gain, wq, wkv, cos_t, sin_t, head_size, step):
    rows, width = tok.shape
    qc, kc = wq.shape[1], wkv.shape[1]
    return pl.pallas_call(
        functools.partial(project_kernel, head_size, step, score_factor(head_size)),
        out_shape=(
            jax.ShapeDtypeStruct((rows, width), BF16),
            jax.ShapeDtypeStruct((rows, qc), BF16),
            jax.ShapeDtypeStruct((rows, kc), BF16),
            jax.ShapeDtypeStruct((rows, head_size), F32),
            jax.ShapeDtypeStruct((rows, head_size), F32),
        ),
        in_specs=[spec(pltpu.VMEM)] * 6,
        out_specs=[spec(pltpu.VMEM)] * 5,
        compiler_params=pltpu.CompilerParams(vmem_limit_bytes=20 * 2**20),
        cost_estimate=pl.CostEstimate(
            flops=2 * rows * width * (qc + kc), bytes_accessed=10 * 2**20, transcendentals=0
        ),
        name="project_own",
    )(tok, gain.reshape(1, width), wq, wkv, cos_t, sin_t)


def other_kernel(head_size, factor, order, normed, w0, w1, w2, w3, cos, sin, q):
    rows = normed.shape[0]
    tile = min(256, rows)
    deep = w0.shape[0]
    even = lax.broadcasted_iota(jnp.int32, (tile, head_size), 1) % 2 == 0
    for i in range(rows // tile):
        at = pl.ds(i * tile, tile)
        c = cos[at, :]
        s = sin[at, :]
        for h in range(q.shape[1] // head_size):
            cols = slice(h * head_size, (h + 1) * head_size)
            total = None
            for n, w in enumerate((w0, w1, w2, w3)):
                x = normed[at, pl.ds(pl.multiple_of(order[n] * deep, 128), deep)]
                part = jnp.dot(x, w[:, cols], preferred_element_type=F32)
                total = part if total is None else total + part
            q[at, cols] = (rotate(total, c, s, even) * factor).astype(BF16)


def project_other(normed, pieces, order, cos, sin, head_size):
    rows, width = normed.shape
    qc = pieces[0].shape[1]
    return pl.pallas_call(
        functools.partial(other_kernel, head_size, score_factor(head_size)),
        out_shape=jax.ShapeDtypeStruct((rows, qc), BF16),
        in_specs=[spec(pltpu.SMEM)] + [spec(pltpu.VMEM)] * 7,
        out_specs=spec(pltpu.VMEM),
        compiler_params=pltpu.CompilerParams(vmem_limit_bytes=20 * 2**20),
        cost_estimate=pl.CostEstimate(
            flops=2 * rows * width * qc, bytes_accessed=6 * 2**20, transcendentals=0
        ),
        name="project_other",
    )(order, normed, *pieces, cos, sin)


def pick_kernel(idx, pool, keys, vals, sem):
    count, _, head_size = keys.shape
    copies = []
    for n, out in enumerate((keys, vals)):
        cols = pl.ds(n * head_size, head_size)
        for j in range(count):
            page = pool.at[idx[j], :, cols]
            copies.append(pltpu.make_async_copy(page, out.at[j], sem.at[n * count + j]))
    for c in copies:
        c.start()
    for c in copies:
        c.wait()


def pick(pool, idx):
    count = idx.shape[0]
    half = jax.ShapeDtypeStruct((count, pool.shape[1], pool.shape[2] // 2), pool.dtype)
    return pl.pallas_call(
        pick_kernel,
        out_shape=(half, half),
        in_specs=[spec(pltpu.SMEM), spec(ANY)],
        out_specs=[spec(pltpu.VMEM)] * 2,
        scratch_shapes=[pltpu.SemaphoreType.DMA((2 * count,))],
        compiler_params=pltpu.CompilerParams(vmem_limit_bytes=60 * 2**20),
        cost_estimate=pl.CostEstimate(flops=0, bytes_accessed=2**20, transcendentals=0),
        name="pick_pages",
    )(idx, pool)


def hold_kernel(info, qa, qb, own, peer, woa, wob0, wob1, qa_v, qb_v, own_v, peer_v, wa, wb, sem):
    core = info[2]
    deep = wob0.shape[0]
    moves = [
        (woa, wa),
        (wob0, wb.at[pl.ds(core * deep, deep), :]),
        (wob1, wb.at[pl.ds((1 - core) * deep, deep), :]),
        (qa, qa_v),
        (qb, qb_v),
        (own, own_v),
        (peer, peer_v),
    ]
    copies = [pltpu.make_async_copy(a, b, sem.at[n]) for n, (a, b) in enumerate(moves)]
    for c in copies:
        c.start()
    for c in copies:
        c.wait()


def hold(info, qa, qb, kv_own, kv_peer, woa, wobs):
    kept = (qa, qb, kv_own, kv_peer, woa, woa)
    return pl.pallas_call(
        hold_kernel,
        out_shape=[jax.ShapeDtypeStruct(x.shape, x.dtype) for x in kept],
        in_specs=[spec(pltpu.SMEM)] + [spec(ANY)] * 7,
        out_specs=[spec(pltpu.VMEM)] * 6,
        scratch_shapes=[pltpu.SemaphoreType.DMA((7,))],
        compiler_params=pltpu.CompilerParams(vmem_limit_bytes=16 * 2**20),
        cost_estimate=pl.CostEstimate(flops=0, bytes_accessed=8 * 2**20, transcendentals=0),
        name="hold",
    )(info, qa, qb, kv_own, kv_peer, woa, *wobs)


def attend_kernel(
    head_size,
    info,
    qa,
    qb,
    k_mine,
    k_peer,
    v_mine,
    v_peer,
    kv_own,
    kv_peer,
    wa,
    wb,
    out_hbm,
    keys,
    turned,
    vals,
    mix,
    out,
    sbuf,
    pbuf,
    sums,
    tops,
    ksem,
    vsem,
    osem,
):
    part = info[0]
    length = info[1]
    rows, half = qa.shape
    pages, prow, _ = k_mine.shape
    page = 2 * prow
    width = out.shape[1]
    nheads = half // head_size
    window = pages * page

    def start(mine, peer, lo, dst, sem):
        cols = pl.ds(lo, head_size)
        for case in (0, 1):

            @pl.when(part == case)
            def _():
                skip = case * rows // page
                for u in range(skip, pages):
                    for src, side in ((mine, case), (peer, 1 - case)):
                        to = pl.ds((u - skip) * page + side * prow, prow)
                        pltpu.make_async_copy(src.at[u], dst.at[to, :], sem).start()
                if case == 1:
                    to = pl.ds(window - rows, rows)
                    pltpu.make_async_copy(kv_peer.at[:, cols], dst.at[to, :], sem).start()
                to = pl.ds(window, rows)
                pltpu.make_async_copy(kv_own.at[:, cols], dst.at[to, :], sem).start()

    def finish(dst, sem):
        pltpu.make_async_copy(dst, dst, sem).wait()

    start(k_mine, k_peer, 0, keys, ksem)
    start(v_mine, v_peer, head_size, vals, vsem)
    tile = min(256, rows)
    span = window + tile
    lanes = 128
    gap = lax.broadcasted_iota(jnp.int32, (tile, tile), 1) - lax.broadcasted_iota(
        jnp.int32, (tile, tile), 0
    )
    order = [(i, n, h) for i in range(rows // tile) for n in range(2) for h in range(nheads)]

    def score(m):
        i, n, h = order[m]
        q = (qa, qb)[n][pl.ds(i * tile, tile), h * head_size : (h + 1) * head_size]
        top = None
        for lo in range(0, span, tile):
            at = i * tile + lo
            s = jnp.dot(q, turned[:, at : at + tile], preferred_element_type=F32)
            if lo == 0:
                s = jnp.where(gap >= 1, s, MASKED)
            if lo + tile == span:
                s = jnp.where(gap <= 0, s, MASKED)
            sbuf[m % 2, :, lo : lo + tile] = s
            for at in range(0, tile, lanes):
                piece = s[:, at : at + lanes]
                top = piece if top is None else jnp.maximum(top, piece)
        top = jnp.max(top, axis=-1, keepdims=True)
        tops[m % 2] = jnp.broadcast_to(top, (tile, lanes))

    def soften(m):
        total = None
        for lo in range(0, span, lanes):
            e = jnp.exp2(sbuf[m % 2, :, lo : lo + lanes] - tops[m % 2])
            pbuf[m % 2, :, lo : lo + lanes] = e.astype(BF16)
            total = e if total is None else total + e
        total = jnp.sum(total, axis=-1, keepdims=True)
        sums[m % 2] = jnp.broadcast_to(1.0 / total, (tile, lanes))

    def combine(m):
        i, n, h = order[m]
        mixed = jnp.dot(
            pbuf[m % 2], vals[pl.ds(i * tile, span), :], preferred_element_type=F32
        )
        mixed = mixed * sums[m % 2, :, :1]
        at = pl.ds(i * tile, tile)
        mix[n, at, h * head_size : (h + 1) * head_size] = mixed.astype(BF16)

    block = 512

    def project_out(i, lo):
        at = pl.ds(i * tile, tile)
        row = part * rows + i * tile + lax.broadcasted_iota(jnp.int32, (tile, 1), 0)
        cols = slice(lo, lo + block)
        a = jnp.dot(mix[0, at, :], wa[:, cols], preferred_element_type=F32)
        b = jnp.dot(mix[1, at, :], wb[:, cols], preferred_element_type=F32)
        both = a.astype(BF16).astype(F32) + b.astype(BF16).astype(F32)
        out[at, cols] = jnp.where(row < length, both, 0.0).astype(BF16)

    stores = []

    def send_out(i):
        at = pl.ds(i * tile, tile)
        stores.append(pltpu.make_async_copy(out.at[at, :], out_hbm.at[at, :], osem.at[i]))
        stores[i].start()

    finish(keys, ksem)
    for lo in range(0, window + rows, tile):
        turned[:, lo : lo + tile] = keys[lo : lo + tile, :].T
    score(0)
    ready = []
    for m in range(len(order)):
        if m + 1 < len(order):
            score(m + 1)
        if m == 1:
            finish(vals, vsem)
        if m >= 1:
            combine(m - 1)
            i, n, h = order[m - 1]
            if (n, h) == (1, nheads - 1):
                ready += [(i, lo) for lo in range(0, width, block)]
        if m >= 1 and ready and order[m - 1][1:] != (1, nheads - 1):
            i, lo = ready.pop(0)
            project_out(i, lo)
            if lo + block == width:
                send_out(i)
        soften(m)
    combine(len(order) - 1)
    ready += [(rows // tile - 1, lo) for lo in range(0, width, block)]
    for i, lo in ready:
        project_out(i, lo)
        if lo + block == width:
            send_out(i)
    for c in stores:
        c.wait()


def attend_pages(info, qa, qb, k_mine, k_peer, v_mine, v_peer, kv_own, kv_peer, wa, wb):
    rows, half = qa.shape
    tile = min(256, rows)
    width = wa.shape[1]
    head_size = k_mine.shape[2]
    window = k_mine.shape[0] * k_mine.shape[1] * 2
    return pl.pallas_call(
        functools.partial(attend_kernel, head_size),
        out_shape=jax.ShapeDtypeStruct((rows, width), BF16),
        in_specs=[spec(pltpu.SMEM)] + [spec(pltpu.VMEM)] * 10,
        out_specs=spec(ANY),
        scratch_shapes=[
            pltpu.VMEM((window + rows, head_size), BF16),
            pltpu.VMEM((head_size, window + rows), BF16),
            pltpu.VMEM((window + rows, head_size), BF16),
            pltpu.VMEM((2, rows, half), BF16),
            pltpu.VMEM((rows, width), BF16),
            pltpu.VMEM((2, tile, window + tile), F32),
            pltpu.VMEM((2, tile, window + tile), BF16),
            pltpu.VMEM((2, tile, 128), F32),
            pltpu.VMEM((2, tile, 128), F32),
            pltpu.SemaphoreType.DMA,
            pltpu.SemaphoreType.DMA,
            pltpu.SemaphoreType.DMA((rows // tile,)),
        ],
        compiler_params=pltpu.CompilerParams(vmem_limit_bytes=30 * 2**20),
        cost_estimate=pl.CostEstimate(
            flops=4 * rows * 2 * half * (window + 256) + 4 * rows * half * width,
            bytes_accessed=12 * 2**20,
            transcendentals=rows * 6 * (window + 256),
        ),
        name="attend_and_out",
    )(info, qa, qb, k_mine, k_peer, v_mine, v_peer, kv_own, kv_peer, wa, wb)


def pair_shards(tokens, norm_gain, w_query, w_keyval, w_out, kv_pages, page_table, lengths, starts):
    head_size = w_keyval.shape[1] // 2
    part = lax.axis_index("tensor")
    rep = lax.axis_index("rep")
    dp = lax.axis_index("dp")
    ndp = lax.axis_size("dp")
    core = dp % 2
    rows = tokens.shape[1]
    swap = [(0, 1), (1, 0)]
    cores = [(i, i ^ 1) for i in range(ndp)]

    pool = lax.all_gather(kv_pages, "dp", axis=0, tiled=True)

    def peer_rows(w, at, parts):
        deep = w.shape[0] // parts
        return lax.ppermute(lax.dynamic_slice_in_dim(w, at * deep, deep, 0), "tensor", swap)

    step = 32
    cos_t, sin_t = rotation_tables(starts[0] + part * rows, rows, step, head_size)
    normed, qa, kv_own, cos, sin = project(
        tokens[0], norm_gain, w_query, w_keyval, cos_t, sin_t, head_size, step
    )

    a = peer_rows(w_query, rep * 2 + core, 4)
    a, kv_own, w_out_late, page_table = lax.optimization_barrier((a, kv_own, w_out, page_table))
    b = lax.ppermute(a, "rep", swap)
    c = peer_rows(w_out_late, core, 2)
    table = page_table[0]
    peer_table = lax.ppermute(table, "rep", swap)
    wq_pieces = (a, b, lax.ppermute(a, "dp", cores), lax.ppermute(b, "dp", cores))
    order = jnp.stack(
        [rep * 2 + core, (1 - rep) * 2 + core, rep * 2 + 1 - core, (1 - rep) * 2 + 1 - core]
    ).astype(jnp.int32)
    qb = project_other(normed, wq_pieces, order, cos, sin, head_size)
    c, qb, kv_own = lax.optimization_barrier((c, qb, kv_own))
    wo_pieces = (c, lax.ppermute(c, "dp", cores))
    kv_peer = lax.ppermute(kv_own, "tensor", swap)

    per_rep = kv_pages.shape[0] * ndp
    home = table[0] // per_rep == rep
    own_at, peer_at = table % per_rep, peer_table % per_rep
    wo_pieces, pool, own_at, peer_at = lax.optimization_barrier(
        (wo_pieces, pool, own_at, peer_at)
    )
    k_sent, v_sent = pick(pool, peer_at)
    k_came = lax.ppermute(k_sent, "rep", swap)
    v_came = lax.ppermute(v_sent, "rep", swap)
    k_held, v_held = pick(pool, own_at)
    k_came, kv_peer, k_held = lax.optimization_barrier((k_came, kv_peer, k_held))
    k_mine = jnp.where(home, k_held, k_came)
    k_peer = lax.ppermute(k_mine, "tensor", swap)
    v_mine = jnp.where(home, v_held, v_came)
    v_peer = lax.ppermute(v_mine, "tensor", swap)

    info = jnp.stack([part, lengths[0], core]).astype(jnp.int32)
    info, k_mine = lax.optimization_barrier((info, k_mine))
    qa, qb, kv_own, kv_peer, wa, wb = hold(info, qa, qb, kv_own, kv_peer, w_out, wo_pieces)
    return attend_pages(
        info, qa, qb, k_mine, k_peer, v_mine, v_peer, kv_own, kv_peer, wa, wb
    )[None]


def rotate_pairs(values, positions, columns_from, head_size):
    rows, cols = values.shape
    column = columns_from + jnp.arange(cols // 2, dtype=jnp.int32) * 2
    within = (column % head_size).astype(jnp.float32)
    inv_freq = jnp.exp(within * (-math.log(10000.0) / head_size))
    angle = positions[:, None] * inv_freq[None, :]
    cosine = jnp.cos(angle)
    sine = jnp.sin(angle)
    pairs = values.reshape(rows, cols // 2, 2)
    first = pairs[:, :, 0]
    second = pairs[:, :, 1]
    turned = jnp.stack([first * cosine - second * sine, first * sine + second * cosine], axis=-1)
    return turned.reshape(rows, cols)


def attend(query, keys, values, first_row, heads, head_size, window):
    rows = query.shape[0]
    count = keys.shape[0]
    q_heads = query.reshape(rows, heads, head_size)
    scores = jnp.einsum("rhd,kd->hrk", q_heads, keys, preferred_element_type=jnp.float32) * (
        1.0 / math.sqrt(head_size)
    )
    row_ids = first_row + jnp.arange(rows, dtype=jnp.int32)
    key_ids = jnp.arange(count, dtype=jnp.int32)
    seen = (key_ids[None, :] >= row_ids[:, None] + 1) & (
        key_ids[None, :] <= row_ids[:, None] + window
    )
    scores = jnp.where(seen[None, :, :], scores, -1e30)
    top = jnp.max(scores, axis=-1, keepdims=True)
    expd = jnp.exp(scores - top)
    total = jnp.sum(expd, axis=-1, keepdims=True)
    probs = (expd / total).astype(jnp.bfloat16)
    mixed = jnp.einsum("hrk,kd->rhd", probs, values, preferred_element_type=jnp.float32)
    return mixed.reshape(rows, heads * head_size).astype(jnp.bfloat16)


def shards(tokens, norm_gain, w_query, w_keyval, w_out, kv_pages, page_table, lengths, starts):
    width = tokens.shape[2]
    head_size = w_keyval.shape[1] // 2
    heads = width // head_size
    part = lax.axis_index("tensor")
    local_rows = tokens.shape[1]
    q_cols = w_query.shape[1]
    start = starts[0]
    length = lengths[0]
    xf = tokens[0].astype(jnp.float32)
    scale = lax.rsqrt(jnp.mean(xf * xf, axis=-1, keepdims=True) + 1e-06)
    normed = (xf * scale * norm_gain).astype(jnp.bfloat16)
    piece = lax.all_gather(normed, "tensor", axis=0, tiled=True)
    positions = (start + jnp.arange(piece.shape[0], dtype=jnp.int32)).astype(jnp.float32)
    query = rotate_pairs(
        jnp.dot(piece, w_query, preferred_element_type=jnp.float32),
        positions,
        part * q_cols,
        head_size,
    )
    keyval = jnp.dot(piece, w_keyval, preferred_element_type=jnp.float32)
    new_keys = rotate_pairs(keyval[:, :head_size], positions, 0, head_size)
    projected = jnp.concatenate([query, new_keys, keyval[:, head_size:]], axis=1).astype(
        jnp.bfloat16
    )
    query_cols = projected[:, :q_cols]
    keys_new = projected[:, q_cols : q_cols + head_size]
    values_new = projected[:, q_cols + head_size :]
    query = lax.all_to_all(query_cols, "tensor", split_axis=0, concat_axis=1, tiled=True)
    table = page_table[0]
    piece = lax.all_gather(kv_pages, ("rep", "dp"), axis=0, tiled=True)
    ident = jnp.arange(piece.shape[0], dtype=jnp.int32)
    onehot = (table[:, None] == ident[None, :]).astype(jnp.bfloat16)
    picked = jnp.einsum("cn,nrk->crk", onehot, piece, preferred_element_type=jnp.float32)
    window_pages = lax.all_gather(picked.astype(jnp.bfloat16), "tensor", axis=1, tiled=True)
    cached = window_pages.reshape(-1, 2 * head_size)
    window = cached.shape[0]
    keys = jnp.concatenate([cached[:, :head_size], keys_new], axis=0)
    values = jnp.concatenate([cached[:, head_size:], values_new], axis=0)
    mixed = attend(query, keys, values, part * local_rows, heads, head_size, window)
    mixed_cols = lax.all_to_all(mixed, "tensor", split_axis=1, concat_axis=0, tiled=True)
    summed = lax.psum_scatter(
        jnp.dot(mixed_cols, w_out, preferred_element_type=jnp.float32).astype(jnp.bfloat16),
        "tensor",
        scatter_dimension=0,
        tiled=True,
    ).astype(jnp.float32)
    live = part * local_rows + jnp.arange(local_rows, dtype=jnp.int32) < length
    return jnp.where(live[:, None], summed, 0.0).astype(jnp.bfloat16)[None]


def solution(mesh):
    placed = (
        P(("rep", "dp"), "tensor", None),
        P(),
        P(None, "tensor"),
        P(),
        P("tensor", None),
        P(("rep", "dp"), "tensor", None),
        P(("rep", "dp"), None),
        P(("rep", "dp")),
        P(("rep", "dp")),
    )
    pair = mesh.shape["tensor"] == 2 and mesh.shape["rep"] == 2 and mesh.shape["dp"] % 2 == 0
    body = pair_shards if pair else shards
    return jax.shard_map(
        body,
        mesh=mesh,
        in_specs=placed,
        out_specs=P(("rep", "dp"), "tensor", None),
        check_vma=False,
    )
```
